32 devices in a mesh: row: 8 (over z, x), col: 4 (over y, core).
Axes of the slice: x: 2, y: 2, z: 4, core: 2. Of those that a mesh axis runs over, the one named last changes fastest.
Arguments:
- tokens: bfloat16 [8192, 2048], P('row', 'col'), may hold values from -6 to 6
- cotangent: bfloat16 [8192, 2048], P('row', 'col'), may hold values from -6 to 6
- segment_ids: int32 [8192], P('row'), may hold values from 0 to 128, as said below
- gain_attn: float32 [2048], replicated, may hold values from 0.1 to 1.9
- gain_ffn: float32 [2048], replicated, may hold values from 0.1 to 1.9
- gain_query: float32 [128], replicated, may hold values from 0.1 to 1.9
- gain_key: float32 [128], replicated, may hold values from 0.1 to 1.9
- w_query: bfloat16 [2048, 2048], P('row', 'col'), may hold values from -0.125 to 0.125
- w_gate: bfloat16 [2048, 2048], P('row', 'col'), may hold values from -0.125 to 0.125
- w_key: bfloat16 [2048, 1024], P('row', 'col'), may hold values from -0.125 to 0.125
- w_value: bfloat16 [2048, 1024], P('row', 'col'), may hold values from -0.125 to 0.125
- w_out: bfloat16 [2048, 2048], P('row', 'col'), may hold values from -0.75 to 0.75
- w_ffgate: bfloat16 [2048, 6144], P('row', 'col'), may hold values from -0.125 to 0.125
- w_up: bfloat16 [2048, 6144], P('row', 'col'), may hold values from -0.125 to 0.125
- w_down: bfloat16 [2048, 6144], P('row', 'col'), may hold values from -0.109375 to 0.109375
Outputs:
- output: bfloat16 [8192, 2048], P('row', 'col')
- grad_tokens: float32 [8192, 2048], P('row', 'col')
- grad_gain_attn: float32 [2048], replicated
- grad_gain_ffn: float32 [2048], replicated
- grad_gain_query: float32 [128], replicated
- grad_gain_key: float32 [128], replicated
- grad_w_query: float32 [2048, 2048], P('row', 'col')
- grad_w_gate: float32 [2048, 2048], P('row', 'col')
- grad_w_key: float32 [2048, 1024], P('row', 'col')
- grad_w_value: float32 [2048, 1024], P('row', 'col')
- grad_w_out: float32 [2048, 2048], P('row', 'col')
- grad_w_ffgate: float32 [2048, 6144], P('row', 'col')
- grad_w_up: float32 [2048, 6144], P('row', 'col')
- grad_w_down: float32 [2048, 6144], P('row', 'col')
The draws below stay inside these ranges and needn't reach their ends.
Inputs may be any that keep to these rules, and one draw needn't show every extreme that they name: `segment_ids`: each block of 1024 tokens is one packed sequence: its numbers start at 1, never fall and rise by at most one from token to token, up to a tail of padding (0) of one or more tokens; some sequence reaches 128 documents.
All inputs are finite; a program needn't handle non-finite values.
Results may differ from the reference program's by a relative error of at most 0.023.
Values may be sent and summed in bfloat16 or wider, within the bound.
No kernel may reach another device: no remote copies, remote signals or barrier semaphores. Data moves between devices by JAX's collectives and lax.ppermute only.
A program may use at most 256 MiB of HBM per device.

```python
from functools import partial
import jax
import jax.numpy as jnp
from jax import lax

D = 2048
HK = 8
HD = 128
FF = 6144
TOK_DEV = 1024
QD = 2048
KD = 1024
TOKENS = 8192


def draw_segment_ids(key, part):
    key = jax.random.fold_in(key, 11)
    sequences = TOKENS // TOK_DEV
    first_key, second_key, third_key, fourth_key = jax.random.split(key, 4)
    rates = jax.random.randint(first_key, (sequences, 1), 2, 8)
    coins = jax.random.randint(second_key, (sequences, TOK_DEV), 0, 65536)
    limits = jnp.right_shift(jnp.full((sequences, 1), 65536, jnp.int32), rates)
    index = jnp.arange(TOK_DEV, dtype=jnp.int32)[None, :]
    chosen = jax.random.randint(fourth_key, (), 0, sequences)
    rows = jnp.arange(sequences, dtype=jnp.int32)[:, None]
    forced = (rows == chosen) & (index % 4 == 0) & (index < TOK_DEV // 2)
    starts = jnp.where((coins < limits) | (index == 0) | forced, 1, 0).astype(jnp.int32)
    numbers = jnp.minimum(jnp.cumsum(starts, axis=1).astype(jnp.int32), TOK_DEV // 8)
    padding = jax.random.randint(third_key, (sequences, 1), 1, TOK_DEV // 4 + 1)
    numbers = jnp.where(index >= TOK_DEV - padding, 0, numbers)
    return numbers.reshape(TOKENS).astype(jnp.int32)


def level_of(own_key, dims, cuts, low, top_value):
    def one(dim, blocks):
        heights = jax.random.uniform(jax.random.fold_in(jax.random.fold_in(own_key, 6), dim), (blocks,), jnp.float32, low / len(cuts), top_value / len(cuts))
        return jnp.repeat(jnp.exp(heights), dims[dim] // blocks).reshape((-1,) + (1,) * (len(dims) - dim - 1))

    loudness = one(*cuts[0])
    for cut in cuts[1:]:
        loudness = loudness * one(*cut)
    return loudness


def centred(own_key, dims, deviation, most, shards=(), kind=jnp.bfloat16):
    level = level_of(own_key, dims, shards, -0.22, 0.18) if shards else 1.0
    entries = jax.random.normal(own_key, dims, jnp.float32) * deviation * level
    return jnp.minimum(jnp.maximum(entries, -most), most).astype(kind)


def setup_inputs(seed: int = 0) -> dict:
    streams_of = jax.random.split(jax.random.key(seed), 16)
    return {
        "tokens": centred(streams_of[0], (TOKENS, D), 1.0, 6.0, ((0, 8), (1, 4))),
        "cotangent": centred(streams_of[1], (TOKENS, D), 1.0, 6.0, ((0, 8), (1, 4))),
        "segment_ids": draw_segment_ids(jax.random.fold_in(streams_of[15], 71), 0),
        "gain_attn": jnp.clip(1.0 + 0.18 * jax.random.normal(streams_of[3], (D,), jnp.float32), 0.1, 1.9),
        "gain_ffn": jnp.clip(1.0 + 0.18 * jax.random.normal(streams_of[4], (D,), jnp.float32), 0.1, 1.9),
        "gain_query": jnp.clip(1.0 + 0.18 * jax.random.normal(streams_of[5], (HD,), jnp.float32), 0.1, 1.9),
        "gain_key": jnp.clip(1.0 + 0.18 * jax.random.normal(streams_of[6], (HD,), jnp.float32), 0.1, 1.9),
        "w_query": centred(streams_of[7], (D, QD), D ** -0.5, 0.125, ((0, 8), (1, 4))),
        "w_gate": centred(streams_of[8], (D, QD), D ** -0.5, 0.125, ((0, 8), (1, 4))),
        "w_key": centred(streams_of[9], (D, KD), D ** -0.5, 0.125, ((0, 8), (1, 4))),
        "w_value": centred(streams_of[10], (D, KD), D ** -0.5, 0.125, ((0, 8), (1, 4))),
        "w_out": centred(streams_of[11], (D, QD), (QD // 32) ** -0.5, 0.75, ((0, 8), (1, 4))),
        "w_ffgate": centred(streams_of[12], (D, FF), D ** -0.5, 0.125, ((0, 8), (1, 4))),
        "w_up": centred(streams_of[13], (D, FF), D ** -0.5, 0.125, ((0, 8), (1, 4))),
        "w_down": centred(streams_of[14], (D, FF), (FF // 2) ** -0.5, 0.109375, ((0, 8), (1, 4))),
    }


eps_norm = 1e-06
rope_base = 1000000.0

@jax.custom_vjp
def low(v):
    return lax.optimization_barrier(v.astype(jnp.bfloat16)).astype(jnp.float32)

@jax.custom_vjp
def low_back(v):
    return v

def low_keep(v):
    return (low(v), None)

def low_pass(kept, grad):
    return (grad,)

def back_keep(v):
    return (v, None)

def back_low(kept, grad):
    return (low(grad),)
low.defvjp(low_keep, low_pass)
low_back.defvjp(back_keep, back_low)

def product(first, second):
    return jnp.dot(first, second, precision=lax.Precision.HIGHEST, preferred_element_type=jnp.float32)

def norm_rows(values, gain):
    inverse = lax.rsqrt(lax.optimization_barrier(jnp.mean(values * values, axis=-1, keepdims=True)) + eps_norm)
    return values * inverse * gain

def rope_tables(segments, head_dim):
    count = segments.shape[0]
    index = jnp.arange(count, dtype=jnp.int32)
    previous = jnp.concatenate([jnp.full((1,), -1, jnp.int32), segments[:-1]])
    starts = lax.cummax(jnp.where(segments != previous, index, 0), axis=0)
    position = (index - starts).astype(jnp.float32)
    half = head_dim // 2
    freqs = jnp.power(rope_base, -(jnp.arange(half, dtype=jnp.float32) * 2.0 / head_dim))
    angle = position[:, None] * freqs[None, :]
    angle = jnp.concatenate([angle, angle], axis=1)
    return (jnp.cos(angle), jnp.sin(angle))

def attend_mask(segments):
    count = segments.shape[0]
    index = jnp.arange(count, dtype=jnp.int32)
    earlier = index[None, :] < index[:, None]
    same = (segments[None, :] == segments[:, None]) & (segments[None, :] > 0)
    return (index[None, :] == index[:, None]) | earlier & same

def head_prepare(raw, gain, cosine, sine):
    count = raw.shape[0]
    head_dim = gain.shape[0]
    heads = raw.reshape(count, -1, head_dim)
    inverse = lax.rsqrt(lax.optimization_barrier(jnp.mean(heads * heads, axis=-1, keepdims=True)) + eps_norm)
    normed = heads * inverse * gain
    half = head_dim // 2
    turned = jnp.concatenate([-normed[..., half:], normed[..., :half]], axis=-1)
    return (normed * cosine[:, None, :] + turned * sine[:, None, :]).reshape(count, -1)

def attend_sequence(head_dim, kv_heads, inputs):
    query, keys, values, segments = inputs
    count = query.shape[0]
    group = query.shape[1] // (kv_heads * head_dim)
    grouped = query.reshape(count, kv_heads, group, head_dim)
    keyed = keys.reshape(count, kv_heads, head_dim)
    valued = values.reshape(count, kv_heads, head_dim)
    scores = jnp.einsum('qgrd,kgd->grqk', grouped, keyed, precision=lax.Precision.HIGHEST) * head_dim ** (-0.5)
    scores = low_back(jnp.where(attend_mask(segments), scores, -1e+30))
    peak = lax.optimization_barrier(jnp.max(scores, axis=-1, keepdims=True))
    weights = jnp.exp(scores - peak)
    probs = low(weights / lax.optimization_barrier(jnp.sum(weights, axis=-1, keepdims=True)))
    attended = jnp.einsum('grqk,kgd->qgrd', probs, valued, precision=lax.Precision.HIGHEST)
    return low_back(attended.reshape(count, -1))

def reference(tokens, cotangent, segment_ids, gain_attn, gain_ffn, gain_query, gain_key, w_query, w_gate, w_key, w_value, w_out, w_ffgate, w_up, w_down):
    sequences = segment_ids.reshape(-1, TOK_DEV)
    cosine, sine = jax.vmap(partial(rope_tables, head_dim=HD))(sequences)
    cosine = cosine.reshape(-1, HD)
    sine = sine.reshape(-1, HD)
    live = (segment_ids > 0).astype(jnp.float32)[:, None]

    def layer(inputs, g_attn, g_ffn, g_query, g_key, wq, wg, wk, wv, wo, wf, wu, wd):
        hidden1 = low(norm_rows(inputs, g_attn))
        query_raw = low_back(product(hidden1, wq))
        gate_raw = low_back(product(hidden1, wg))
        key_raw = low_back(product(hidden1, wk))
        values = low_back(low(product(hidden1, wv)))
        query = low(head_prepare(query_raw, g_query, cosine, sine))
        keys = low(head_prepare(key_raw, g_key, cosine, sine))
        attended = lax.map(jax.checkpoint(partial(attend_sequence, HD, HK)), (query.reshape(-1, TOK_DEV, QD), keys.reshape(-1, TOK_DEV, KD), values.reshape(-1, TOK_DEV, KD), sequences))
        attended = attended.reshape(-1, QD)
        mixed = low(attended * jax.nn.sigmoid(gate_raw))
        branch = low_back(product(mixed, wo.T))
        resid = inputs + branch
        hidden2 = low(norm_rows(low(resid), g_ffn))
        ff_gate = low_back(product(hidden2, wf))
        ff_up = low_back(product(hidden2, wu))
        activated = low(jax.nn.silu(ff_gate) * ff_up)
        ffn_out = low_back(product(activated, wd.T))
        return live * (resid + ffn_out)
    result, backward = jax.vjp(layer, tokens.astype(jnp.float32), gain_attn.astype(jnp.float32), gain_ffn.astype(jnp.float32), gain_query.astype(jnp.float32), gain_key.astype(jnp.float32), w_query.astype(jnp.float32), w_gate.astype(jnp.float32), w_key.astype(jnp.float32), w_value.astype(jnp.float32), w_out.astype(jnp.float32), w_ffgate.astype(jnp.float32), w_up.astype(jnp.float32), w_down.astype(jnp.float32))
    grads = backward(cotangent.astype(jnp.float32))
    return (result.astype(jnp.bfloat16), grads[0], grads[1], grads[2], grads[3], grads[4], grads[5], grads[6], grads[7], grads[8], grads[9], grads[10], grads[11], grads[12])
```

```python
from functools import partial

import jax
import jax.numpy as jnp
from jax import lax
from jax.experimental import pallas as pl
from jax.experimental.pallas import tpu as pltpu
from jax.sharding import Mesh
from jax.sharding import PartitionSpec as P

eps_norm = 1e-06
rope_base = 1000000.0


def norm_rows(values, gain):
    inverse = lax.rsqrt(jnp.mean(values * values, axis=-1, keepdims=True) + eps_norm)
    return (values * inverse * gain, inverse)


def rope_tables(segments, head_dim):
    count = segments.shape[0]
    index = jnp.arange(count, dtype=jnp.int32)
    previous = jnp.concatenate([jnp.full((1,), -1, jnp.int32), segments[:-1]])
    starts = lax.cummax(jnp.where(segments != previous, index, 0), axis=0)
    position = (index - starts).astype(jnp.float32)
    half = head_dim // 2
    freqs = jnp.power(rope_base, -(jnp.arange(half, dtype=jnp.float32) * 2.0 / head_dim))
    angle = position[:, None] * freqs[None, :]
    angle = jnp.concatenate([angle, angle], axis=1)
    return (jnp.cos(angle), jnp.sin(angle))


def attend_mask(segments):
    count = segments.shape[0]
    index = jnp.arange(count, dtype=jnp.int32)
    earlier = index[None, :] < index[:, None]
    same = (segments[None, :] == segments[:, None]) & (segments[None, :] > 0)
    return (index[None, :] == index[:, None]) | earlier & same


def head_prepare(raw, gain, cosine, sine):
    count = raw.shape[0]
    head_dim = gain.shape[0]
    heads = raw.reshape(count, -1, head_dim)
    inverse = lax.rsqrt(jnp.mean(heads * heads, axis=-1, keepdims=True) + eps_norm)
    normed = heads * inverse * gain
    half = head_dim // 2
    turned = jnp.concatenate([-normed[..., half:], normed[..., :half]], axis=-1)
    return (normed * cosine[:, None, :] + turned * sine[:, None, :]).reshape(count, -1)


def feature_gather(values):
    return lax.all_gather(values, "col", axis=1, tiled=True)


def feature_sum(values):
    return lax.psum_scatter(
        values.astype(jnp.bfloat16), "col", scatter_dimension=1, tiled=True
    ).astype(jnp.float32)


def rows_in(operand, weight):
    return jnp.dot(
        operand,
        lax.all_gather(weight, "row", axis=0, tiled=True),
        preferred_element_type=jnp.float32,
    )


def rows_out(operand, weight):
    return lax.dot_general(
        operand,
        lax.all_gather(weight, "row", axis=0, tiled=True),
        (((1,), (1,)), ((), ())),
        preferred_element_type=jnp.float32,
    )


def weight_grads(firsts, seconds):
    blocks = []
    for first, second in zip(firsts, seconds):
        blocks.append(
            lax.dot_general(
                first, second, (((0,), (0,)), ((), ())), preferred_element_type=jnp.float32
            )
        )
    return lax.psum_scatter(
        jnp.concatenate(blocks, axis=1).astype(jnp.bfloat16), "row", scatter_dimension=0, tiled=True
    ).astype(jnp.float32)


def norm_back(partial_grad, unit, inverse, gain, local):
    offset = lax.axis_index("col") * local
    width = unit.shape[1]
    unit_own = lax.dynamic_slice_in_dim(unit, offset, local, 1)
    grad_own = feature_sum(partial_grad)
    gain_own = lax.dynamic_slice_in_dim(gain, offset, local, 0)
    scaled = grad_own * gain_own
    dots = lax.psum(jnp.sum(scaled * unit_own, axis=1), "col")[:, None] / width
    grad_input = inverse * (scaled - unit_own * dots)
    gain_grad = lax.dynamic_update_slice_in_dim(
        jnp.zeros((width,), jnp.float32), jnp.sum(grad_own * unit_own, axis=0), offset, 0
    )
    return (grad_input, gain_grad)


def attend_scores(query, keys, allowed, kv_heads, head_dim):
    count = query.shape[0]
    grouped = query.reshape(count, kv_heads, -1, head_dim)
    keyed = keys.reshape(count, kv_heads, head_dim)
    scores = jnp.einsum(
        "qgrd,kgd->grqk", grouped, keyed, preferred_element_type=jnp.float32
    ) * head_dim ** (-0.5)
    return (jnp.where(allowed, scores, -1e30), grouped, keyed)


def attend_forward(query, keys, values, allowed, kv_heads, head_dim):
    count = query.shape[0]
    scores, grouped, keyed = attend_scores(query, keys, allowed, kv_heads, head_dim)
    peak = jnp.max(scores, axis=-1, keepdims=True)
    weights = jnp.exp(scores - peak)
    total = jnp.sum(weights, axis=-1, keepdims=True)
    probs = (weights / total).astype(jnp.bfloat16)
    valued = values.reshape(count, kv_heads, head_dim)
    attended = jnp.einsum("grqk,kgd->qgrd", probs, valued, preferred_element_type=jnp.float32)
    return (attended.reshape(count, -1), peak + jnp.log(total))


def attend_backward(query, keys, values, allowed, logsum, grad_attended, kv_heads, head_dim):
    count = query.shape[0]
    scores, grouped, keyed = attend_scores(query, keys, allowed, kv_heads, head_dim)
    probs_exact = jnp.exp(scores - logsum)
    probs = probs_exact.astype(jnp.bfloat16)
    valued = values.reshape(count, kv_heads, head_dim)
    grad_grouped = grad_attended.reshape(count, kv_heads, -1, head_dim)
    grad_values = jnp.einsum(
        "grqk,qgrd->kgd", probs, grad_grouped, preferred_element_type=jnp.float32
    )
    grad_probs = jnp.einsum(
        "qgrd,kgd->grqk", grad_grouped, valued, preferred_element_type=jnp.float32
    )
    delta = jnp.sum(probs_exact * grad_probs, axis=-1, keepdims=True)
    grad_scores = (probs_exact * (grad_probs - delta)).astype(jnp.bfloat16)
    grad_query = jnp.einsum(
        "grqk,kgd->qgrd", grad_scores, keyed, preferred_element_type=jnp.float32
    ) * head_dim ** (-0.5)
    grad_keys = jnp.einsum(
        "grqk,qgrd->kgd", grad_scores, grouped, preferred_element_type=jnp.float32
    ) * head_dim ** (-0.5)
    return (
        grad_query.reshape(count, -1),
        grad_keys.reshape(count, -1),
        grad_values.reshape(count, -1).astype(jnp.bfloat16),
    )


def body(
    tokens,
    cotangent,
    segment_ids,
    gain_attn,
    gain_ffn,
    gain_query,
    gain_key,
    w_query,
    w_gate,
    w_key,
    w_value,
    w_out,
    w_ffgate,
    w_up,
    w_down,
):
    local = tokens.shape[1]
    head_dim = gain_query.shape[0]
    query_width = w_query.shape[1]
    key_width = w_key.shape[1]
    kv_heads = key_width // head_dim
    hidden_width = w_ffgate.shape[1]
    live = (segment_ids > 0).astype(jnp.float32)[:, None]
    cosine, sine = rope_tables(segment_ids, head_dim)
    allowed = attend_mask(segment_ids)
    attn_weight = jnp.concatenate([w_query, w_gate, w_key, w_value], axis=1)
    ffn_weight = jnp.concatenate([w_ffgate, w_up], axis=1)
    blocks = (attn_weight, ffn_weight, w_out, w_down)

    def apply_in(operand, which_block):
        return rows_in(operand, blocks[which_block])

    def apply_out(operand, which_block):
        return rows_out(operand, blocks[which_block])

    inputs = feature_gather(tokens).astype(jnp.float32)
    normed1, inverse1 = norm_rows(inputs, gain_attn)
    hidden1 = normed1.astype(jnp.bfloat16)
    joint = apply_in(hidden1, 0)
    query_raw = joint[:, :query_width]
    gate_raw = joint[:, query_width : 2 * query_width]
    key_raw = joint[:, 2 * query_width : 2 * query_width + key_width]
    values = joint[:, 2 * query_width + key_width :].astype(jnp.bfloat16)
    prepare = partial(head_prepare, cosine=cosine, sine=sine)
    query = prepare(query_raw, gain_query).astype(jnp.bfloat16)
    keys = prepare(key_raw, gain_key).astype(jnp.bfloat16)
    attended, logsum = attend_forward(query, keys, values, allowed, kv_heads, head_dim)
    gate_sig = jax.nn.sigmoid(gate_raw)
    mixed = (attended * gate_sig).astype(jnp.bfloat16)
    resid = tokens.astype(jnp.float32) + feature_sum(apply_out(mixed, 2))
    resid_full = feature_gather(resid.astype(jnp.bfloat16)).astype(jnp.float32)
    normed2, inverse2 = norm_rows(resid_full, gain_ffn)
    hidden2 = normed2.astype(jnp.bfloat16)
    ffn_joint = apply_in(hidden2, 1)
    ff_gate = ffn_joint[:, :hidden_width]
    ff_up = ffn_joint[:, hidden_width:]
    sig_gate = jax.nn.sigmoid(ff_gate)
    activated = (jax.nn.silu(ff_gate) * ff_up).astype(jnp.bfloat16)
    ffn_out = feature_sum(apply_out(activated, 3))
    output = (live * (resid + ffn_out)).astype(jnp.bfloat16)
    grad_out = live * cotangent.astype(jnp.float32)
    grad_ffn_full = feature_gather(grad_out.astype(jnp.bfloat16))
    grad_act = apply_in(grad_ffn_full, 3)
    grad_ffup = (grad_act * (ff_gate * sig_gate)).astype(jnp.bfloat16)
    grad_ffgate = (grad_act * ff_up * sig_gate * (1.0 + ff_gate * (1.0 - sig_gate))).astype(
        jnp.bfloat16
    )
    grad_pair = jnp.concatenate([grad_ffgate, grad_ffup], axis=1)
    ffn_grads = weight_grads((hidden2, grad_ffn_full), (grad_pair, activated))
    grad_input2, gain_ffn_grad = norm_back(
        apply_out(grad_pair, 1), resid_full * inverse2, inverse2, gain_ffn, local
    )
    grad_resid = grad_out + grad_input2
    grad_branch_full = feature_gather(grad_resid.astype(jnp.bfloat16))
    grad_mixed = apply_in(grad_branch_full, 2)
    grad_attended = (grad_mixed * gate_sig).astype(jnp.bfloat16)
    grad_gate_raw = (grad_mixed * attended * gate_sig * (1.0 - gate_sig)).astype(jnp.bfloat16)
    grad_query, grad_keys, grad_values = attend_backward(
        query, keys, values, allowed, logsum, grad_attended, kv_heads, head_dim
    )
    unused_query, query_back = jax.vjp(prepare, query_raw, gain_query)
    grad_query_raw, grad_gain_query = query_back(grad_query)
    unused_key, key_back = jax.vjp(prepare, key_raw, gain_key)
    grad_key_raw, grad_gain_key = key_back(grad_keys)
    grad_joint = jnp.concatenate(
        [
            grad_query_raw.astype(jnp.bfloat16),
            grad_gate_raw,
            grad_key_raw.astype(jnp.bfloat16),
            grad_values,
        ],
        axis=1,
    )
    attn_grads = weight_grads((hidden1, grad_branch_full), (grad_joint, mixed))
    grad_input1, gain_attn_grad = norm_back(
        apply_out(grad_joint, 0), inputs * inverse1, inverse1, gain_attn, local
    )
    grad_tokens = grad_resid + grad_input1
    gains = lax.psum(
        (gain_attn_grad, gain_ffn_grad, grad_gain_query, grad_gain_key), ("row", "col")
    )
    second_cut = 2 * query_width
    third_cut = 2 * query_width + key_width
    fourth_cut = 2 * query_width + 2 * key_width
    return (
        output,
        grad_tokens,
        gains[0],
        gains[1],
        gains[2],
        gains[3],
        attn_grads[:, :query_width],
        attn_grads[:, query_width:second_cut],
        attn_grads[:, second_cut:third_cut],
        attn_grads[:, third_cut:fourth_cut],
        attn_grads[:, fourth_cut:],
        ffn_grads[:, :hidden_width],
        ffn_grads[:, hidden_width : 2 * hidden_width],
        ffn_grads[:, 2 * hidden_width :],
    )


def plain(mesh):
    in_specs = (
        P("row", "col"),
        P("row", "col"),
        P("row"),
        P(),
        P(),
        P(),
        P(),
        P("row", "col"),
        P("row", "col"),
        P("row", "col"),
        P("row", "col"),
        P("row", "col"),
        P("row", "col"),
        P("row", "col"),
        P("row", "col"),
    )
    out_specs = (
        P("row", "col"),
        P("row", "col"),
        P(),
        P(),
        P(),
        P(),
        P("row", "col"),
        P("row", "col"),
        P("row", "col"),
        P("row", "col"),
        P("row", "col"),
        P("row", "col"),
        P("row", "col"),
        P("row", "col"),
    )
    return jax.shard_map(body, mesh=mesh, in_specs=in_specs, out_specs=out_specs, check_vma=False)


def flip(values, axis):
    return lax.ppermute(values, axis, [(0, 1), (1, 0)])


def spread(own):
    half = own.shape[0] // 2
    via_y = flip(own, "y")
    via_x = flip(own, "x")
    first = flip(via_y[:half], "x")
    second = flip(via_x[half:], "y")
    held = ((own, via_y), (via_x, jnp.concatenate([first, second], axis=0)))
    return tuple(
        tuple(block for values in pair for block in (values, flip(values, "core")))
        for pair in held
    )


def pack_kernel(place_ref, gain_ref, *refs):
    blocks, out_ref = refs[:4], refs[4]
    width = blocks[0].shape[1]
    place = place_ref[0]
    if len(refs) == 6:
        values = [block[...].astype(jnp.float32) for block in blocks]
        squares = sum(jnp.sum(v * v, axis=1, keepdims=True) for v in values)
        inverse = lax.rsqrt(squares / (4 * width) + eps_norm)
        refs[5][...] = inverse
    for index in range(4):
        columns = pl.ds(pl.multiple_of((place ^ index) * width, width), width)
        if len(refs) == 6:
            result = values[index] * inverse * gain_ref[:, columns]
            out_ref[:, columns] = result.astype(out_ref.dtype)
        else:
            out_ref[:, columns] = blocks[index][...]


def pack(blocks, place, gain, normed):
    count, width = blocks[0].shape
    tile = 256
    out_shape = [jax.ShapeDtypeStruct((count, 4 * width), jnp.bfloat16)]
    out_specs = [pl.BlockSpec((tile, 4 * width), lambda i: (i, 0))]
    if normed:
        out_shape.append(jax.ShapeDtypeStruct((count, 1), jnp.float32))
        out_specs.append(pl.BlockSpec((tile, 1), lambda i: (i, 0)))
    return pl.pallas_call(
        pack_kernel,
        grid=(count // tile,),
        in_specs=[
            pl.BlockSpec(memory_space=pltpu.SMEM),
            pl.BlockSpec((1, 4 * width), lambda i: (0, 0)),
        ]
        + [pl.BlockSpec((tile, width), lambda i: (i, 0))] * 4,
        out_specs=out_specs,
        out_shape=out_shape,
        cost_estimate=pl.CostEstimate(
            flops=0, bytes_accessed=count * width * 16, transcendentals=0
        ),
    )(place.reshape(1), gain.reshape(1, -1), *blocks)


def gather_normed(own, place, gain):
    first, second = spread(own)
    normed_own, inverse = pack(first, place, gain, True)
    normed_other, unused = pack(second, place, gain, True)
    return (jnp.concatenate([normed_own, normed_other], axis=0), inverse)


def gather_plain(own, place, gain):
    first, second = spread(own)
    return jnp.concatenate(
        [pack(first, place, gain, False)[0], pack(second, place, gain, False)[0]], axis=0
    )


def halves(weights, across):
    keep, give = [], []
    for weight in weights:
        width = weight.shape[1] // 2
        keep.append(lax.dynamic_slice_in_dim(weight, across * width, width, 1))
        give.append(lax.dynamic_slice_in_dim(weight, (1 - across) * width, width, 1))
    return (keep, give)


def weight_gather(keep, give, across):
    keep = jnp.concatenate(keep, axis=1)
    got = flip(jnp.concatenate(give, axis=1), "x")
    top = jnp.where(across == 0, keep, got)
    bottom = jnp.where(across == 0, got, keep)
    return lax.all_gather(jnp.concatenate([top, bottom], axis=0), "z", axis=0, tiled=True)


def grad_scatter(grads, across):
    summed = lax.psum_scatter(grads, "z", scatter_dimension=0, tiled=True)
    rows = summed.shape[0] // 2
    keep = lax.dynamic_slice_in_dim(summed, across * rows, rows, 0)
    got = flip(lax.dynamic_slice_in_dim(summed, (1 - across) * rows, rows, 0), "x")
    return (jnp.where(across == 0, keep, got), jnp.where(across == 0, got, keep))


def feature_fold(pairs, place):
    def product(index):
        total = None
        for operand, weight in pairs:
            rows = weight.shape[0] // 4
            block = lax.dynamic_slice_in_dim(weight, (place ^ index) * rows, rows, 0)
            term = lax.dot_general(
                operand, block, (((1,), (1,)), ((), ())), preferred_element_type=jnp.float32
            )
            total = term if total is None else total + term
        return total

    low = jnp.bfloat16
    sent = [flip(product(index).astype(low), "core") for index in (1, 3)]
    held = [product(index) + got for index, got in zip((0, 2), sent)]
    count = held[0].shape[0] // 2
    half = count // 2
    near, far = [v.astype(low) for v in held]
    upper = flip(jnp.stack([near[count : count + half], far[count : count + half]]), "x")
    lower = flip(jnp.stack([far[half:count], far[count + half :]]), "y")
    upper_near = near[:half].astype(jnp.float32) + upper[0]
    upper_far = (far[:half].astype(jnp.float32) + upper[1]).astype(low)
    lower_own = near[half:count].astype(jnp.float32) + lower[0]
    lower_other = (near[count + half :].astype(jnp.float32) + lower[1]).astype(low)
    upper_final = upper_near + flip(upper_far, "y")
    lower_final = lower_own + flip(lower_other, "x")
    return jnp.concatenate([upper_final, lower_final], axis=0)


def norm_back_own(grad_own, values_own, inverse, gain_own, width):
    unit = values_own * inverse
    scaled = grad_own * gain_own
    dots = jnp.sum(scaled * unit, axis=1, keepdims=True)
    dots = dots + flip(dots, "core")
    dots = dots + flip(dots, "y")
    grad_input = inverse * (scaled - unit * (dots / width))
    return (grad_input, jnp.sum(grad_own * unit, axis=0))


def dot_in(operand, weight):
    return jnp.dot(operand, weight, preferred_element_type=jnp.float32)


def dot_grad(first, second):
    return lax.dot_general(
        first, second, (((0,), (0,)), ((), ())), preferred_element_type=jnp.float32
    ).astype(jnp.bfloat16)


def fast_body(
    tokens,
    cotangent,
    segment_ids,
    gain_attn,
    gain_ffn,
    gain_query,
    gain_key,
    w_query,
    w_gate,
    w_key,
    w_value,
    w_out,
    w_ffgate,
    w_up,
    w_down,
):
    across = lax.axis_index("x")
    place = lax.axis_index("y") * 2 + lax.axis_index("core")
    count, local = tokens.shape
    width = gain_attn.shape[0]
    head_dim = gain_query.shape[0]
    low = jnp.bfloat16
    query_width = w_query.shape[1] // 2
    key_width = w_key.shape[1] // 2
    kv_heads = key_width // head_dim
    hidden_width = w_ffgate.shape[1] // 2
    chunk = hidden_width // 2
    live = (segment_ids > 0).astype(jnp.float32)[:, None]
    offset = place * local
    gain_attn_own = lax.dynamic_slice_in_dim(gain_attn, offset, local, 0)
    gain_ffn_own = lax.dynamic_slice_in_dim(gain_ffn, offset, local, 0)

    keep, give = halves([w_query, w_gate, w_key, w_value], across)
    attn_weight = weight_gather(keep, give, across)
    hidden1, inverse1 = gather_normed(tokens, place, gain_attn)
    keep, give = halves([w_out], across)
    out_weight = weight_gather(keep, give, across)
    keep, give = halves([w_down], across)
    down_weight = weight_gather(keep, give, across)
    keep, give = halves([w_ffgate, w_up], across)
    pair_weights = []
    for part in range(2):
        cut = slice(part * chunk, (part + 1) * chunk)
        pair_weights.append(
            weight_gather([v[:, cut] for v in keep], [v[:, cut] for v in give], across)
        )

    segments = jnp.stack([segment_ids, flip(segment_ids, "x")])
    cosine, sine = jax.vmap(partial(rope_tables, head_dim=head_dim))(segments)
    cosine = cosine.reshape(2 * count, head_dim)
    sine = sine.reshape(2 * count, head_dim)
    allowed = jax.vmap(attend_mask)(segments)

    joint = dot_in(hidden1, attn_weight)
    query_raw = joint[:, :query_width]
    gate_raw = joint[:, query_width : 2 * query_width]
    key_raw = joint[:, 2 * query_width : 2 * query_width + key_width]
    values = joint[:, 2 * query_width + key_width :].astype(low)
    prepare = partial(head_prepare, cosine=cosine, sine=sine)
    query = prepare(query_raw, gain_query).astype(low)
    keys = prepare(key_raw, gain_key).astype(low)
    split = lambda v: v.reshape(2, count, -1)
    attended, logsum = jax.vmap(
        partial(attend_forward, kv_heads=kv_heads, head_dim=head_dim)
    )(split(query), split(keys), split(values), allowed)
    attended = attended.reshape(2 * count, -1)
    gate_sig = jax.nn.sigmoid(gate_raw)
    mixed = (attended * gate_sig).astype(low)
    resid = tokens.astype(jnp.float32) + feature_fold([(mixed, out_weight)], place)
    resid_low = resid.astype(low)
    hidden2, inverse2 = gather_normed(resid_low, place, gain_ffn)

    grad_out = live * cotangent.astype(jnp.float32)
    grad_out_full = gather_plain(grad_out.astype(low), place, gain_ffn)
    grad_act = dot_in(grad_out_full, down_weight)

    activated, grad_pairs = [], []
    for part in range(2):
        ffn_joint = dot_in(hidden2, pair_weights[part])
        ff_gate = ffn_joint[:, :chunk]
        ff_up = ffn_joint[:, chunk:]
        sig_gate = jax.nn.sigmoid(ff_gate)
        activated.append((ff_gate * sig_gate * ff_up).astype(low))
        grad_part = grad_act[:, part * chunk : (part + 1) * chunk]
        grad_ffup = (grad_part * (ff_gate * sig_gate)).astype(low)
        grad_ffgate = (grad_part * ff_up * sig_gate * (1.0 + ff_gate * (1.0 - sig_gate))).astype(
            low
        )
        grad_pairs.append(jnp.concatenate([grad_ffgate, grad_ffup], axis=1))
    activated = jnp.concatenate(activated, axis=1)
    pair_grads = [dot_grad(hidden2, grad_pair) for grad_pair in grad_pairs]
    down_grad = dot_grad(grad_out_full, activated)
    pair_sums = [grad_scatter(grads, across) for grads in pair_grads]
    down_sum = grad_scatter(down_grad, across)

    grad_hidden2 = feature_fold(list(zip(grad_pairs, pair_weights)), place)
    grad_input2, gain_ffn_grad = norm_back_own(
        grad_hidden2, resid_low.astype(jnp.float32), inverse2, gain_ffn_own, width
    )
    grad_resid = grad_out + grad_input2
    ffn_out = feature_fold([(activated, down_weight)], place)
    output = (live * (resid + ffn_out)).astype(low)
    grad_branch_full = gather_plain(grad_resid.astype(low), place, gain_ffn)
    grad_mixed = dot_in(grad_branch_full, out_weight)
    out_sum = grad_scatter(dot_grad(grad_branch_full, mixed), across)
    grad_attended = (grad_mixed * gate_sig).astype(low)
    grad_gate_raw = (grad_mixed * attended * gate_sig * (1.0 - gate_sig)).astype(low)
    grad_query, grad_keys, grad_values = jax.vmap(
        partial(attend_backward, kv_heads=kv_heads, head_dim=head_dim)
    )(split(query), split(keys), split(values), allowed, logsum, split(grad_attended))
    flat = lambda v: v.reshape(2 * count, -1)
    unused_query, query_back = jax.vjp(prepare, query_raw, gain_query)
    grad_query_raw, grad_gain_query = query_back(flat(grad_query))
    unused_key, key_back = jax.vjp(prepare, key_raw, gain_key)
    grad_key_raw, grad_gain_key = key_back(flat(grad_keys))
    grad_joint = jnp.concatenate(
        [grad_query_raw.astype(low), grad_gate_raw, grad_key_raw.astype(low), flat(grad_values)],
        axis=1,
    )
    attn_sum = grad_scatter(dot_grad(hidden1, grad_joint), across)
    grad_hidden1 = feature_fold([(grad_joint, attn_weight)], place)
    grad_input1, gain_attn_grad = norm_back_own(
        grad_hidden1, tokens.astype(jnp.float32), inverse1, gain_attn_own, width
    )
    grad_tokens = grad_resid + grad_input1

    spot = lambda v: lax.dynamic_update_slice_in_dim(jnp.zeros((width,), jnp.float32), v, offset, 0)
    gains = lax.psum(
        jnp.concatenate(
            [spot(gain_attn_grad), spot(gain_ffn_grad), grad_gain_query, grad_gain_key]
        ),
        ("z", "x", "y", "core"),
    )

    def join(sums, low_cut, high_cut):
        return jnp.concatenate(
            [s[:, low_cut:high_cut] for s in sums], axis=1
        ).astype(jnp.float32)

    def join_parts(low_cut, high_cut):
        return jnp.concatenate(
            [pair_sums[part][side][:, low_cut:high_cut] for side in range(2) for part in range(2)],
            axis=1,
        ).astype(jnp.float32)

    cuts = (
        0,
        query_width,
        2 * query_width,
        2 * query_width + key_width,
        2 * query_width + 2 * key_width,
    )
    return (
        output,
        grad_tokens,
        gains[:width],
        gains[width : 2 * width],
        gains[2 * width : 2 * width + head_dim],
        gains[2 * width + head_dim :],
        join(attn_sum, cuts[0], cuts[1]),
        join(attn_sum, cuts[1], cuts[2]),
        join(attn_sum, cuts[2], cuts[3]),
        join(attn_sum, cuts[3], cuts[4]),
        join(out_sum, 0, query_width),
        join_parts(0, chunk),
        join_parts(chunk, 2 * chunk),
        join(down_sum, 0, hidden_width),
    )


def solution(mesh):
    rows, columns = mesh.devices.shape
    split = rows % 2 == 0 and columns == 4

    def run(*args):
        if not split:
            return plain(mesh)(*args)
        names = ("z", "x", "y", "core")
        inner = Mesh(mesh.devices.reshape(rows // 2, 2, 2, 2), names)
        block = P(("z", "x"), ("y", "core"))
        whole = P()
        in_specs = (block, block, P(("z", "x"))) + (whole,) * 4 + (block,) * 8
        out_specs = (block, block) + (whole,) * 4 + (block,) * 8
        return jax.shard_map(
            fast_body, mesh=inner, in_specs=in_specs, out_specs=out_specs, check_vma=False
        )(*args)

    return run
```

```python
from functools import partial

import jax
import jax.numpy as jnp
from jax import lax
from jax.experimental import pallas as pl
from jax.experimental.pallas import tpu as pltpu
from jax.sharding import Mesh
from jax.sharding import PartitionSpec as P

eps_norm = 1e-06
rope_base = 1000000.0


def norm_rows(values, gain):
    inverse = lax.rsqrt(jnp.mean(values * values, axis=-1, keepdims=True) + eps_norm)
    return (values * inverse * gain, inverse)


def rope_tables(segments, head_dim):
    count = segments.shape[0]
    index = jnp.arange(count, dtype=jnp.int32)
    previous = jnp.concatenate([jnp.full((1,), -1, jnp.int32), segments[:-1]])
    starts = lax.cummax(jnp.where(segments != previous, index, 0), axis=0)
    position = (index - starts).astype(jnp.float32)
    half = head_dim // 2
    freqs = jnp.power(rope_base, -(jnp.arange(half, dtype=jnp.float32) * 2.0 / head_dim))
    angle = position[:, None] * freqs[None, :]
    angle = jnp.concatenate([angle, angle], axis=1)
    return (jnp.cos(angle), jnp.sin(angle))


def attend_mask(segments):
    count = segments.shape[0]
    index = jnp.arange(count, dtype=jnp.int32)
    earlier = index[None, :] < index[:, None]
    same = (segments[None, :] == segments[:, None]) & (segments[None, :] > 0)
    return (index[None, :] == index[:, None]) | earlier & same


def head_prepare(raw, gain, cosine, sine):
    count = raw.shape[0]
    head_dim = gain.shape[0]
    heads = raw.reshape(count, -1, head_dim)
    inverse = lax.rsqrt(jnp.mean(heads * heads, axis=-1, keepdims=True) + eps_norm)
    normed = heads * inverse * gain
    half = head_dim // 2
    turned = jnp.concatenate([-normed[..., half:], normed[..., :half]], axis=-1)
    return (normed * cosine[:, None, :] + turned * sine[:, None, :]).reshape(count, -1)


def feature_gather(values):
    return lax.all_gather(values, "col", axis=1, tiled=True)


def feature_sum(values):
    return lax.psum_scatter(
        values.astype(jnp.bfloat16), "col", scatter_dimension=1, tiled=True
    ).astype(jnp.float32)


def rows_in(operand, weight):
    return jnp.dot(
        operand,
        lax.all_gather(weight, "row", axis=0, tiled=True),
        preferred_element_type=jnp.float32,
    )


def rows_out(operand, weight):
    return lax.dot_general(
        operand,
        lax.all_gather(weight, "row", axis=0, tiled=True),
        (((1,), (1,)), ((), ())),
        preferred_element_type=jnp.float32,
    )


def weight_grads(firsts, seconds):
    blocks = []
    for first, second in zip(firsts, seconds):
        blocks.append(
            lax.dot_general(
                first, second, (((0,), (0,)), ((), ())), preferred_element_type=jnp.float32
            )
        )
    return lax.psum_scatter(
        jnp.concatenate(blocks, axis=1).astype(jnp.bfloat16), "row", scatter_dimension=0, tiled=True
    ).astype(jnp.float32)


def norm_back(partial_grad, unit, inverse, gain, local):
    offset = lax.axis_index("col") * local
    width = unit.shape[1]
    unit_own = lax.dynamic_slice_in_dim(unit, offset, local, 1)
    grad_own = feature_sum(partial_grad)
    gain_own = lax.dynamic_slice_in_dim(gain, offset, local, 0)
    scaled = grad_own * gain_own
    dots = lax.psum(jnp.sum(scaled * unit_own, axis=1), "col")[:, None] / width
    grad_input = inverse * (scaled - unit_own * dots)
    gain_grad = lax.dynamic_update_slice_in_dim(
        jnp.zeros((width,), jnp.float32), jnp.sum(grad_own * unit_own, axis=0), offset, 0
    )
    return (grad_input, gain_grad)


def attend_scores(query, keys, allowed, kv_heads, head_dim):
    count = query.shape[0]
    grouped = query.reshape(count, kv_heads, -1, head_dim)
    keyed = keys.reshape(count, kv_heads, head_dim)
    scores = jnp.einsum(
        "qgrd,kgd->grqk", grouped, keyed, preferred_element_type=jnp.float32
    ) * head_dim ** (-0.5)
    return (jnp.where(allowed, scores, -1e30), grouped, keyed)


def attend_forward(query, keys, values, allowed, kv_heads, head_dim):
    count = query.shape[0]
    scores, grouped, keyed = attend_scores(query, keys, allowed, kv_heads, head_dim)
    peak = jnp.max(scores, axis=-1, keepdims=True)
    weights = jnp.exp(scores - peak)
    total = jnp.sum(weights, axis=-1, keepdims=True)
    probs = (weights / total).astype(jnp.bfloat16)
    valued = values.reshape(count, kv_heads, head_dim)
    attended = jnp.einsum("grqk,kgd->qgrd", probs, valued, preferred_element_type=jnp.float32)
    return (attended.reshape(count, -1), peak + jnp.log(total))


def attend_backward(query, keys, values, allowed, logsum, grad_attended, kv_heads, head_dim):
    count = query.shape[0]
    scores, grouped, keyed = attend_scores(query, keys, allowed, kv_heads, head_dim)
    probs_exact = jnp.exp(scores - logsum)
    probs = probs_exact.astype(jnp.bfloat16)
    valued = values.reshape(count, kv_heads, head_dim)
    grad_grouped = grad_attended.reshape(count, kv_heads, -1, head_dim)
    grad_values = jnp.einsum(
        "grqk,qgrd->kgd", probs, grad_grouped, preferred_element_type=jnp.float32
    )
    grad_probs = jnp.einsum(
        "qgrd,kgd->grqk", grad_grouped, valued, preferred_element_type=jnp.float32
    )
    delta = jnp.sum(probs_exact * grad_probs, axis=-1, keepdims=True)
    grad_scores = (probs_exact * (grad_probs - delta)).astype(jnp.bfloat16)
    grad_query = jnp.einsum(
        "grqk,kgd->qgrd", grad_scores, keyed, preferred_element_type=jnp.float32
    ) * head_dim ** (-0.5)
    grad_keys = jnp.einsum(
        "grqk,qgrd->kgd", grad_scores, grouped, preferred_element_type=jnp.float32
    ) * head_dim ** (-0.5)
    return (
        grad_query.reshape(count, -1),
        grad_keys.reshape(count, -1),
        grad_values.reshape(count, -1).astype(jnp.bfloat16),
    )


def body(
    tokens,
    cotangent,
    segment_ids,
    gain_attn,
    gain_ffn,
    gain_query,
    gain_key,
    w_query,
    w_gate,
    w_key,
    w_value,
    w_out,
    w_ffgate,
    w_up,
    w_down,
):
    local = tokens.shape[1]
    head_dim = gain_query.shape[0]
    query_width = w_query.shape[1]
    key_width = w_key.shape[1]
    kv_heads = key_width // head_dim
    hidden_width = w_ffgate.shape[1]
    live = (segment_ids > 0).astype(jnp.float32)[:, None]
    cosine, sine = rope_tables(segment_ids, head_dim)
    allowed = attend_mask(segment_ids)
    attn_weight = jnp.concatenate([w_query, w_gate, w_key, w_value], axis=1)
    ffn_weight = jnp.concatenate([w_ffgate, w_up], axis=1)
    blocks = (attn_weight, ffn_weight, w_out, w_down)

    def apply_in(operand, which_block):
        return rows_in(operand, blocks[which_block])

    def apply_out(operand, which_block):
        return rows_out(operand, blocks[which_block])

    inputs = feature_gather(tokens).astype(jnp.float32)
    normed1, inverse1 = norm_rows(inputs, gain_attn)
    hidden1 = normed1.astype(jnp.bfloat16)
    joint = apply_in(hidden1, 0)
    query_raw = joint[:, :query_width]
    gate_raw = joint[:, query_width : 2 * query_width]
    key_raw = joint[:, 2 * query_width : 2 * query_width + key_width]
    values = joint[:, 2 * query_width + key_width :].astype(jnp.bfloat16)
    prepare = partial(head_prepare, cosine=cosine, sine=sine)
    query = prepare(query_raw, gain_query).astype(jnp.bfloat16)
    keys = prepare(key_raw, gain_key).astype(jnp.bfloat16)
    attended, logsum = attend_forward(query, keys, values, allowed, kv_heads, head_dim)
    gate_sig = jax.nn.sigmoid(gate_raw)
    mixed = (attended * gate_sig).astype(jnp.bfloat16)
    resid = tokens.astype(jnp.float32) + feature_sum(apply_out(mixed, 2))
    resid_full = feature_gather(resid.astype(jnp.bfloat16)).astype(jnp.float32)
    normed2, inverse2 = norm_rows(resid_full, gain_ffn)
    hidden2 = normed2.astype(jnp.bfloat16)
    ffn_joint = apply_in(hidden2, 1)
    ff_gate = ffn_joint[:, :hidden_width]
    ff_up = ffn_joint[:, hidden_width:]
    sig_gate = jax.nn.sigmoid(ff_gate)
    activated = (jax.nn.silu(ff_gate) * ff_up).astype(jnp.bfloat16)
    ffn_out = feature_sum(apply_out(activated, 3))
    output = (live * (resid + ffn_out)).astype(jnp.bfloat16)
    grad_out = live * cotangent.astype(jnp.float32)
    grad_ffn_full = feature_gather(grad_out.astype(jnp.bfloat16))
    grad_act = apply_in(grad_ffn_full, 3)
    grad_ffup = (grad_act * (ff_gate * sig_gate)).astype(jnp.bfloat16)
    grad_ffgate = (grad_act * ff_up * sig_gate * (1.0 + ff_gate * (1.0 - sig_gate))).astype(
        jnp.bfloat16
    )
    grad_pair = jnp.concatenate([grad_ffgate, grad_ffup], axis=1)
    ffn_grads = weight_grads((hidden2, grad_ffn_full), (grad_pair, activated))
    grad_input2, gain_ffn_grad = norm_back(
        apply_out(grad_pair, 1), resid_full * inverse2, inverse2, gain_ffn, local
    )
    grad_resid = grad_out + grad_input2
    grad_branch_full = feature_gather(grad_resid.astype(jnp.bfloat16))
    grad_mixed = apply_in(grad_branch_full, 2)
    grad_attended = (grad_mixed * gate_sig).astype(jnp.bfloat16)
    grad_gate_raw = (grad_mixed * attended * gate_sig * (1.0 - gate_sig)).astype(jnp.bfloat16)
    grad_query, grad_keys, grad_values = attend_backward(
        query, keys, values, allowed, logsum, grad_attended, kv_heads, head_dim
    )
    unused_query, query_back = jax.vjp(prepare, query_raw, gain_query)
    grad_query_raw, grad_gain_query = query_back(grad_query)
    unused_key, key_back = jax.vjp(prepare, key_raw, gain_key)
    grad_key_raw, grad_gain_key = key_back(grad_keys)
    grad_joint = jnp.concatenate(
        [
            grad_query_raw.astype(jnp.bfloat16),
            grad_gate_raw,
            grad_key_raw.astype(jnp.bfloat16),
            grad_values,
        ],
        axis=1,
    )
    attn_grads = weight_grads((hidden1, grad_branch_full), (grad_joint, mixed))
    grad_input1, gain_attn_grad = norm_back(
        apply_out(grad_joint, 0), inputs * inverse1, inverse1, gain_attn, local
    )
    grad_tokens = grad_resid + grad_input1
    gains = lax.psum(
        (gain_attn_grad, gain_ffn_grad, grad_gain_query, grad_gain_key), ("row", "col")
    )
    second_cut = 2 * query_width
    third_cut = 2 * query_width + key_width
    fourth_cut = 2 * query_width + 2 * key_width
    return (
        output,
        grad_tokens,
        gains[0],
        gains[1],
        gains[2],
        gains[3],
        attn_grads[:, :query_width],
        attn_grads[:, query_width:second_cut],
        attn_grads[:, second_cut:third_cut],
        attn_grads[:, third_cut:fourth_cut],
        attn_grads[:, fourth_cut:],
        ffn_grads[:, :hidden_width],
        ffn_grads[:, hidden_width : 2 * hidden_width],
        ffn_grads[:, 2 * hidden_width :],
    )


def plain(mesh):
    in_specs = (
        P("row", "col"),
        P("row", "col"),
        P("row"),
        P(),
        P(),
        P(),
        P(),
        P("row", "col"),
        P("row", "col"),
        P("row", "col"),
        P("row", "col"),
        P("row", "col"),
        P("row", "col"),
        P("row", "col"),
        P("row", "col"),
    )
    out_specs = (
        P("row", "col"),
        P("row", "col"),
        P(),
        P(),
        P(),
        P(),
        P("row", "col"),
        P("row", "col"),
        P("row", "col"),
        P("row", "col"),
        P("row", "col"),
        P("row", "col"),
        P("row", "col"),
        P("row", "col"),
    )
    return jax.shard_map(body, mesh=mesh, in_specs=in_specs, out_specs=out_specs, check_vma=False)


def tie(*values):
    return lax.optimization_barrier(values)


def flip(values, axis):
    return lax.ppermute(values, axis, [(0, 1), (1, 0)])


def flip_both(first, first_axis, second, second_axis):
    first, second = tie(first, second)
    return tie(flip(first, first_axis), flip(second, second_axis))


def spread(own):
    half = own.shape[0] // 2
    via_y, via_x = flip_both(own, "y", own, "x")
    first, second = flip_both(via_y[:half], "x", via_x[half:], "y")
    held = ((own, via_y), (via_x, jnp.concatenate([first, second], axis=0)))
    return tuple(
        tuple(block for values in pair for block in (values, flip(values, "core")))
        for pair in held
    )


def pack_kernel(normed, place_ref, gain_ref, *refs):
    blocks, out_ref = refs[:4], refs[5]
    width = blocks[0].shape[1]
    place = place_ref[0]
    if normed:
        values = [block[...].astype(jnp.float32) for block in blocks]
        squares = sum(jnp.sum(v * v, axis=1, keepdims=True) for v in values)
        inverse = lax.rsqrt(squares / (4 * width) + eps_norm)
        refs[6][...] = inverse
    for index in range(4):
        columns = pl.ds(pl.multiple_of((place ^ index) * width, width), width)
        if normed:
            result = values[index] * inverse * gain_ref[:, columns]
            out_ref[:, columns] = result.astype(out_ref.dtype)
        else:
            out_ref[:, columns] = blocks[index][...]


def pack(blocks, place, gain, normed, step, target):
    count, width = blocks[0].shape
    tile = 256
    tiles = count // tile
    out_shape = [jax.ShapeDtypeStruct((2 * count, 4 * width), jnp.bfloat16)]
    out_specs = [pl.BlockSpec((tile, 4 * width), lambda i: (i + step * tiles, 0))]
    if normed:
        out_shape.append(jax.ShapeDtypeStruct((count, 1), jnp.float32))
        out_specs.append(pl.BlockSpec((tile, 1), lambda i: (i, 0)))
    aliases = {}
    if target is None:
        target = place.reshape(1)
    else:
        aliases = {6: 0}
    return pl.pallas_call(
        partial(pack_kernel, normed),
        grid=(tiles,),
        in_specs=[
            pl.BlockSpec(memory_space=pltpu.SMEM),
            pl.BlockSpec((1, 4 * width), lambda i: (0, 0)),
        ]
        + [pl.BlockSpec((tile, width), lambda i: (i, 0))] * 4
        + [pl.BlockSpec(memory_space=pl.ANY if aliases else pltpu.SMEM)],
        out_specs=out_specs,
        out_shape=out_shape,
        input_output_aliases=aliases,
        cost_estimate=pl.CostEstimate(
            flops=0, bytes_accessed=count * width * 16, transcendentals=0
        ),
    )(place.reshape(1), gain.reshape(1, -1), *blocks, target)


def gather_normed(own, place, gain):
    first, second = spread(own)
    target, inverse = pack(first, place, gain, True, 0, None)
    normed, unused = pack(second, place, gain, True, 1, target)
    return (normed, inverse)


def gather_plain(own, place, gain):
    first, second = spread(own)
    target = pack(first, place, gain, False, 0, None)[0]
    return pack(second, place, gain, False, 1, target)[0]


def halves(weights, across):
    keep, give = [], []
    for weight in weights:
        width = weight.shape[1] // 2
        keep.append(lax.dynamic_slice_in_dim(weight, across * width, width, 1))
        give.append(lax.dynamic_slice_in_dim(weight, (1 - across) * width, width, 1))
    return (keep, give)


def weight_gather(keep, give, across):
    keep = jnp.concatenate(keep, axis=1)
    got = flip(jnp.concatenate(give, axis=1), "x")
    top = jnp.where(across == 0, keep, got)
    bottom = jnp.where(across == 0, got, keep)
    return lax.all_gather(jnp.concatenate([top, bottom], axis=0), "z", axis=0, tiled=True)


def grad_scatter(grads, across):
    summed = lax.psum_scatter(grads, "z", scatter_dimension=0, tiled=True)
    rows = summed.shape[0] // 2
    keep = lax.dynamic_slice_in_dim(summed, across * rows, rows, 0)
    got = flip(lax.dynamic_slice_in_dim(summed, (1 - across) * rows, rows, 0), "x")
    return (jnp.where(across == 0, keep, got), jnp.where(across == 0, got, keep))


def feature_fold(pairs, place):
    def product(index):
        total = None
        for operand, weight in pairs:
            rows = weight.shape[0] // 4
            block = lax.dynamic_slice_in_dim(weight, (place ^ index) * rows, rows, 0)
            term = lax.dot_general(
                operand, block, (((1,), (1,)), ((), ())), preferred_element_type=jnp.float32
            )
            total = term if total is None else total + term
        return total

    low = jnp.bfloat16
    sent = [flip(product(index).astype(low), "core") for index in (3, 1)]
    far = (product(2) + sent[0]).astype(low)
    near = (product(0) + sent[1]).astype(low)
    count = far.shape[0] // 2
    half = count // 2
    upper, lower = flip_both(
        jnp.stack([near[count : count + half], far[count : count + half]]),
        "x",
        jnp.stack([far[half:count], far[count + half :]]),
        "y",
    )
    upper_near = near[:half].astype(jnp.float32) + upper[0]
    upper_far = (far[:half].astype(jnp.float32) + upper[1]).astype(low)
    lower_own = near[half:count].astype(jnp.float32) + lower[0]
    lower_other = (near[count + half :].astype(jnp.float32) + lower[1]).astype(low)
    upper_got, lower_got = flip_both(upper_far, "y", lower_other, "x")
    return jnp.concatenate([upper_near + upper_got, lower_own + lower_got], axis=0)


def norm_back_own(grad_own, values_own, inverse, gain_own, width):
    unit = values_own * inverse
    scaled = grad_own * gain_own
    dots = jnp.sum(scaled * unit, axis=1, keepdims=True)
    dots = dots + flip(dots, "core")
    dots = dots + flip(dots, "y")
    grad_input = inverse * (scaled - unit * (dots / width))
    return (grad_input, jnp.sum(grad_own * unit, axis=0))


def dot_in(operand, weight):
    return jnp.dot(operand, weight, preferred_element_type=jnp.float32)


def dot_grad(first, second):
    return lax.dot_general(
        first, second, (((0,), (0,)), ((), ())), preferred_element_type=jnp.float32
    ).astype(jnp.bfloat16)


def row_tables(segments, head_dim):
    count = segments.shape[0]
    index = jnp.arange(count, dtype=jnp.int32)
    previous = jnp.concatenate([jnp.full((1,), -1, jnp.int32), segments[:-1]])
    starts = lax.cummax(jnp.where(segments != previous, index, 0), axis=0)
    position = (index - starts).astype(jnp.float32)
    half = head_dim // 2
    freqs = jnp.power(rope_base, -(jnp.arange(half, dtype=jnp.float32) * 2.0 / head_dim))
    angle = position[:, None] * freqs[None, :]
    cosine, sine = jnp.cos(angle), jnp.sin(angle)
    return (
        jnp.concatenate([cosine, cosine], axis=1),
        jnp.concatenate([-sine, sine], axis=1),
        jnp.where(segments > 0, starts, index)[None, :],
    )


def product_nt(first, second):
    return lax.dot_general(
        first, second, (((1,), (1,)), ((), ())), preferred_element_type=jnp.float32
    )


def product_tn(first, second):
    return lax.dot_general(
        first, second, (((0,), (0,)), ((), ())), preferred_element_type=jnp.float32
    )


def product_nn(first, second):
    return lax.dot_general(
        first, second, (((1,), (0,)), ((), ())), preferred_element_type=jnp.float32
    )


def prepare_tile(raw, gain, cosine, sine):
    inverse = lax.rsqrt(jnp.mean(raw * raw, axis=1, keepdims=True) + eps_norm)
    normed = raw * inverse * gain
    turned = pltpu.roll(normed, raw.shape[1] // 2, 1)
    return (normed * cosine + turned * sine).astype(jnp.bfloat16)


def prepare_back(raw, gain, cosine, sine, grad):
    inverse = lax.rsqrt(jnp.mean(raw * raw, axis=1, keepdims=True) + eps_norm)
    unit = raw * inverse
    grad_normed = grad * cosine + pltpu.roll(grad * sine, raw.shape[1] // 2, 1)
    scaled = grad_normed * gain
    grad_raw = inverse * (scaled - unit * jnp.mean(scaled * unit, axis=1, keepdims=True))
    return (grad_raw.astype(jnp.bfloat16), jnp.sum(grad_normed * unit, axis=0, keepdims=True))


def allowed_tile(first_ref, start, tile, reach):
    rows = lax.broadcasted_iota(jnp.int32, (reach, tile), 0)
    columns = lax.broadcasted_iota(jnp.int32, (reach, tile), 1) + start
    return (rows >= first_ref[0, :, pl.ds(start, tile)]) & (rows <= columns)


def attend_kernel(
    heads, tile, joint_ref, cos_ref, sin_ref, first_ref, gain_query_ref, gain_key_ref,
    mixed_ref, attended_ref, query_ref, key_ref, logsum_ref,
):
    count, head_dim = cos_ref.shape
    scale = head_dim ** (-0.5)
    low = jnp.bfloat16
    key_at = 2 * heads * head_dim
    tiles = count // tile
    for part in range(tiles):
        rows = pl.ds(part * tile, tile)
        key_ref[rows, :] = prepare_tile(
            joint_ref[rows, key_at : key_at + head_dim],
            gain_key_ref[...],
            cos_ref[rows, :],
            sin_ref[rows, :],
        )
    for head in range(heads):
        columns = slice(head * head_dim, (head + 1) * head_dim)
        gates = slice((heads + head) * head_dim, (heads + head + 1) * head_dim)
        for part in range(tiles):
            rows = pl.ds(part * tile, tile)
            reach = (part + 1) * tile
            query = prepare_tile(
                joint_ref[rows, columns], gain_query_ref[...], cos_ref[rows, :], sin_ref[rows, :]
            )
            query_ref[rows, columns] = query
            scores = product_nt(key_ref[:reach, :], query) * scale
            scores = jnp.where(allowed_tile(first_ref, part * tile, tile, reach), scores, -1e30)
            peak = jnp.max(scores, axis=0, keepdims=True)
            weights = jnp.exp(scores - peak)
            total = jnp.sum(weights, axis=0, keepdims=True)
            probs = (weights * (1.0 / total)).astype(low)
            logsum_ref[0, head : head + 1, rows] = peak + jnp.log(total)
            values = joint_ref[:reach, key_at + head_dim : key_at + 2 * head_dim].astype(low)
            attended = product_tn(values, probs).T
            attended_ref[rows, columns] = attended
            gate = joint_ref[rows, gates]
            mixed_ref[rows, columns] = (attended * jax.nn.sigmoid(gate)).astype(low)


def attend_back_kernel(
    heads, tile, joint_ref, cos_ref, sin_ref, first_ref, gain_query_ref, gain_key_ref,
    attended_ref, query_ref, key_ref, logsum_ref, grad_mixed_ref,
    grad_joint_ref, grad_gain_ref, grad_key_acc, grad_value_acc,
):
    count, head_dim = cos_ref.shape
    scale = head_dim ** (-0.5)
    low = jnp.bfloat16
    key_at = 2 * heads * head_dim
    value_at = key_at + head_dim
    tiles = count // tile
    gain_query = jnp.zeros((1, head_dim), jnp.float32)
    gain_key = jnp.zeros((1, head_dim), jnp.float32)
    for head in range(heads):
        columns = slice(head * head_dim, (head + 1) * head_dim)
        gates = slice((heads + head) * head_dim, (heads + head + 1) * head_dim)
        for part in reversed(range(tiles)):
            rows = pl.ds(part * tile, tile)
            reach = (part + 1) * tile
            fresh = head == 0 and part == tiles - 1
            gate = jax.nn.sigmoid(joint_ref[rows, gates])
            grad_mixed = grad_mixed_ref[rows, columns]
            gated = grad_mixed * gate
            grad_attended = gated.astype(low)
            grad_joint_ref[rows, gates] = (gated * attended_ref[rows, columns] * (1.0 - gate)).astype(
                low
            )
            query = query_ref[rows, columns]
            keys = key_ref[:reach, :]
            values = joint_ref[:reach, value_at : value_at + head_dim].astype(low)
            scores = product_nt(keys, query) * scale
            logsum = logsum_ref[0, head : head + 1, rows]
            probs = jnp.where(
                allowed_tile(first_ref, part * tile, tile, reach), jnp.exp(scores - logsum), 0.0
            )
            grad_value = product_nn(probs.astype(low), grad_attended)
            grad_probs = product_nt(values, grad_attended)
            delta = jnp.sum(probs * grad_probs, axis=0, keepdims=True)
            grad_scores = (probs * (grad_probs - delta)).astype(low)
            grad_key = product_nn(grad_scores, query)
            if fresh:
                grad_value_acc[...] = grad_value
                grad_key_acc[...] = grad_key
            else:
                grad_value_acc[:reach, :] += grad_value
                grad_key_acc[:reach, :] += grad_key
            grad_query = product_tn(keys, grad_scores).T * scale
            grad_raw, gain_part = prepare_back(
                joint_ref[rows, columns],
                gain_query_ref[...],
                cos_ref[rows, :],
                sin_ref[rows, :],
                grad_query,
            )
            grad_joint_ref[rows, columns] = grad_raw
            gain_query = gain_query + gain_part
    for part in range(tiles):
        rows = pl.ds(part * tile, tile)
        grad_raw, gain_part = prepare_back(
            joint_ref[rows, key_at:value_at],
            gain_key_ref[...],
            cos_ref[rows, :],
            sin_ref[rows, :],
            grad_key_acc[rows, :] * scale,
        )
        grad_joint_ref[rows, key_at:value_at] = grad_raw
        gain_key = gain_key + gain_part
        grad_joint_ref[rows, value_at : value_at + head_dim] = grad_value_acc[rows, :].astype(low)
    both = jnp.concatenate([gain_query, gain_key], axis=0)

    @pl.when(pl.program_id(0) == 0)
    def begin():
        grad_gain_ref[...] = both

    @pl.when(pl.program_id(0) > 0)
    def add():
        grad_gain_ref[...] += both


def attend_specs(count, head_dim, heads, joint_width):
    wide = lambda width: pl.BlockSpec((count, width), lambda s: (s, 0))
    row = pl.BlockSpec((1, head_dim), lambda s: (0, 0))
    lead = [
        wide(joint_width),
        wide(head_dim),
        wide(head_dim),
        pl.BlockSpec((1, 1, count), lambda s: (s, 0, 0)),
        row,
        row,
    ]
    kept = [
        wide(heads * head_dim),
        wide(heads * head_dim),
        wide(head_dim),
        pl.BlockSpec((1, heads, count), lambda s: (s, 0, 0)),
    ]
    return (lead, kept, wide)


def attend_fwd(joint, cosine, sine, first, gain_query, gain_key, heads, count):
    head_dim = cosine.shape[1]
    lead, kept, wide = attend_specs(count, head_dim, heads, joint.shape[1])
    total = joint.shape[0]
    shape = jax.ShapeDtypeStruct
    return pl.pallas_call(
        partial(attend_kernel, heads, 256),
        grid=(total // count,),
        in_specs=lead,
        out_specs=[wide(heads * head_dim)] + kept,
        out_shape=[
            shape((total, heads * head_dim), jnp.bfloat16),
            shape((total, heads * head_dim), jnp.float32),
            shape((total, heads * head_dim), jnp.bfloat16),
            shape((total, head_dim), jnp.bfloat16),
            shape((total // count, heads, count), jnp.float32),
        ],
        compiler_params=pltpu.CompilerParams(vmem_limit_bytes=40 * 1024 * 1024),
        cost_estimate=pl.CostEstimate(
            flops=4 * total * count * heads * head_dim,
            bytes_accessed=total * head_dim * 60,
            transcendentals=total * count * heads,
        ),
    )(joint, cosine, sine, first, gain_query.reshape(1, -1), gain_key.reshape(1, -1))


def attend_bwd(joint, cosine, sine, first, gain_query, gain_key, kept_values, grad_mixed, count):
    head_dim = cosine.shape[1]
    heads = grad_mixed.shape[1] // head_dim
    lead, kept, wide = attend_specs(count, head_dim, heads, joint.shape[1])
    total = joint.shape[0]
    shape = jax.ShapeDtypeStruct
    return pl.pallas_call(
        partial(attend_back_kernel, heads, 256),
        grid=(total // count,),
        in_specs=lead + kept + [wide(heads * head_dim)],
        out_specs=[wide(joint.shape[1]), pl.BlockSpec((2, head_dim), lambda s: (0, 0))],
        out_shape=[shape(joint.shape, jnp.bfloat16), shape((2, head_dim), jnp.float32)],
        scratch_shapes=[
            pltpu.VMEM((count, head_dim), jnp.float32),
            pltpu.VMEM((count, head_dim), jnp.float32),
        ],
        compiler_params=pltpu.CompilerParams(vmem_limit_bytes=48 * 1024 * 1024),
        cost_estimate=pl.CostEstimate(
            flops=10 * total * count * heads * head_dim,
            bytes_accessed=total * head_dim * 80,
            transcendentals=total * count * heads,
        ),
    )(
        joint, cosine, sine, first, gain_query.reshape(1, -1), gain_key.reshape(1, -1),
        *kept_values, grad_mixed,
    )


def sum_all(values):
    values = values + flip(values, "x")
    for step in (1, 2):
        values = values + lax.ppermute(values, "z", [(i, i ^ step) for i in range(4)])
    return values


def fast_body(
    tokens,
    cotangent,
    segment_ids,
    gain_attn,
    gain_ffn,
    gain_query,
    gain_key,
    w_query,
    w_gate,
    w_key,
    w_value,
    w_out,
    w_ffgate,
    w_up,
    w_down,
):
    across = lax.axis_index("x")
    place = lax.axis_index("y") * 2 + lax.axis_index("core")
    count, local = tokens.shape
    width = gain_attn.shape[0]
    head_dim = gain_query.shape[0]
    low = jnp.bfloat16
    query_width = w_query.shape[1] // 2
    key_width = w_key.shape[1] // 2
    heads = query_width // head_dim
    hidden_width = w_ffgate.shape[1] // 2
    chunk = hidden_width // 2
    live = (segment_ids > 0).astype(jnp.float32)[:, None]
    offset = place * local
    gain_attn_own = lax.dynamic_slice_in_dim(gain_attn, offset, local, 0)
    gain_ffn_own = lax.dynamic_slice_in_dim(gain_ffn, offset, local, 0)

    keep, give = halves([w_query, w_gate, w_key, w_value], across)
    attn_weight = weight_gather(keep, give, across)
    hidden1, inverse1 = gather_normed(tokens, place, gain_attn)
    keep, give = halves([w_out], across)
    out_weight = weight_gather(keep, give, across)
    keep, give = halves([w_down], across)
    down_weight = weight_gather(keep, give, across)
    keep, give = halves([w_ffgate, w_up], across)
    pair_weights = []
    for part in range(2):
        cut = slice(part * chunk, (part + 1) * chunk)
        pair_weights.append(
            weight_gather([v[:, cut] for v in keep], [v[:, cut] for v in give], across)
        )

    segments = jnp.stack([segment_ids, flip(segment_ids, "x")])
    cosine, sine, first = jax.vmap(partial(row_tables, head_dim=head_dim))(segments)
    cosine = cosine.reshape(2 * count, head_dim)
    sine = sine.reshape(2 * count, head_dim)

    grad_out = live * cotangent.astype(jnp.float32)
    grad_out_low, hidden1 = tie(grad_out.astype(low), hidden1)
    grad_out_full = gather_plain(grad_out_low, place, gain_ffn)

    joint = dot_in(hidden1, attn_weight)
    mixed, *kept = attend_fwd(joint, cosine, sine, first, gain_query, gain_key, heads, count)
    mixed, grad_out_full = tie(mixed, grad_out_full)
    resid = tokens.astype(jnp.float32) + feature_fold([(mixed, out_weight)], place)
    grad_act = dot_in(grad_out_full, down_weight)
    resid_low, grad_act = tie(resid.astype(low), grad_act)
    hidden2, inverse2 = gather_normed(resid_low, place, gain_ffn)

    activated, grad_pairs = [], []
    for part in range(2):
        ffn_joint = dot_in(hidden2, pair_weights[part])
        ff_gate = ffn_joint[:, :chunk]
        ff_up = ffn_joint[:, chunk:]
        sig_gate = jax.nn.sigmoid(ff_gate)
        activated.append((ff_gate * sig_gate * ff_up).astype(low))
        grad_part = grad_act[:, part * chunk : (part + 1) * chunk]
        grad_ffup = (grad_part * (ff_gate * sig_gate)).astype(low)
        grad_ffgate = (grad_part * ff_up * sig_gate * (1.0 + ff_gate * (1.0 - sig_gate))).astype(
            low
        )
        grad_pairs.append(jnp.concatenate([grad_ffgate, grad_ffup], axis=1))
    activated = jnp.concatenate(activated, axis=1)
    pair_grads = [dot_grad(hidden2, grad_pair) for grad_pair in grad_pairs]
    down_grad = dot_grad(grad_out_full, activated)
    pair_sums = [grad_scatter(grads, across) for grads in pair_grads]
    down_sum = grad_scatter(down_grad, across)

    grad_hidden2 = feature_fold(list(zip(grad_pairs, pair_weights)), place)
    grad_input2, gain_ffn_grad = norm_back_own(
        grad_hidden2, resid_low.astype(jnp.float32), inverse2, gain_ffn_own, width
    )
    grad_resid = grad_out + grad_input2
    grad_branch_full = gather_plain(grad_resid.astype(low), place, gain_ffn)
    grad_branch_full, activated = tie(grad_branch_full, activated)
    ffn_out = feature_fold([(activated, down_weight)], place)
    output = (live * (resid + ffn_out)).astype(low)
    grad_mixed = dot_in(grad_branch_full, out_weight)
    out_sum = grad_scatter(dot_grad(grad_branch_full, mixed), across)
    grad_joint, grad_head_gains = attend_bwd(
        joint, cosine, sine, first, gain_query, gain_key, kept, grad_mixed, count
    )
    attn_sum = grad_scatter(dot_grad(hidden1, grad_joint), across)
    grad_hidden1 = feature_fold([(grad_joint, attn_weight)], place)
    grad_input1, gain_attn_grad = norm_back_own(
        grad_hidden1, tokens.astype(jnp.float32), inverse1, gain_attn_own, width
    )
    grad_tokens = grad_resid + grad_input1

    own_gains = sum_all(jnp.stack([gain_attn_grad, gain_ffn_grad]))
    head_gains = sum_all(grad_head_gains)
    for axis in ("core", "y"):
        head_gains = head_gains + flip(head_gains, axis)
    spot = lax.dynamic_update_slice_in_dim(
        jnp.zeros((2, width), jnp.float32), own_gains, offset, 1
    )
    for axis in ("core", "y"):
        spot = spot + flip(spot, axis)

    def join(sums, low_cut, high_cut):
        return jnp.concatenate([s[:, low_cut:high_cut] for s in sums], axis=1).astype(jnp.float32)

    def join_parts(low_cut, high_cut):
        return jnp.concatenate(
            [pair_sums[part][side][:, low_cut:high_cut] for side in range(2) for part in range(2)],
            axis=1,
        ).astype(jnp.float32)

    cuts = (
        0,
        query_width,
        2 * query_width,
        2 * query_width + key_width,
        2 * query_width + 2 * key_width,
    )
    return (
        output,
        grad_tokens,
        spot[0],
        spot[1],
        head_gains[0],
        head_gains[1],
        join(attn_sum, cuts[0], cuts[1]),
        join(attn_sum, cuts[1], cuts[2]),
        join(attn_sum, cuts[2], cuts[3]),
        join(attn_sum, cuts[3], cuts[4]),
        join(out_sum, 0, query_width),
        join_parts(0, chunk),
        join_parts(chunk, 2 * chunk),
        join(down_sum, 0, hidden_width),
    )


def solution(mesh):
    rows, columns = mesh.devices.shape

    def run(*args):
        head_dim = args[5].shape[0]
        query_width, key_width = args[7].shape[1], args[9].shape[1]
        one_key_head = key_width == 2 * columns * head_dim and query_width % key_width == 0
        if not (rows == 8 and columns == 4 and one_key_head):
            return plain(mesh)(*args)
        names = ("z", "x", "y", "core")
        inner = Mesh(mesh.devices.reshape(4, 2, 2, 2), names)
        block = P(("z", "x"), ("y", "core"))
        whole = P()
        in_specs = (block, block, P(("z", "x"))) + (whole,) * 4 + (block,) * 8
        out_specs = (block, block) + (whole,) * 4 + (block,) * 8
        return jax.shard_map(
            fast_body, mesh=inner, in_specs=in_specs, out_specs=out_specs, check_vma=False
        )(*args)

    return run
```

```python
from functools import partial

import jax
import jax.numpy as jnp
from jax import lax
from jax.experimental import pallas as pl
from jax.experimental.pallas import tpu as pltpu
from jax.sharding import Mesh
from jax.sharding import PartitionSpec as P

eps_norm = 1e-06
rope_base = 1000000.0


def norm_rows(values, gain):
    inverse = lax.rsqrt(jnp.mean(values * values, axis=-1, keepdims=True) + eps_norm)
    return (values * inverse * gain, inverse)


def rope_tables(segments, head_dim):
    count = segments.shape[0]
    index = jnp.arange(count, dtype=jnp.int32)
    previous = jnp.concatenate([jnp.full((1,), -1, jnp.int32), segments[:-1]])
    starts = lax.cummax(jnp.where(segments != previous, index, 0), axis=0)
    position = (index - starts).astype(jnp.float32)
    half = head_dim // 2
    freqs = jnp.power(rope_base, -(jnp.arange(half, dtype=jnp.float32) * 2.0 / head_dim))
    angle = position[:, None] * freqs[None, :]
    angle = jnp.concatenate([angle, angle], axis=1)
    return (jnp.cos(angle), jnp.sin(angle))


def attend_mask(segments):
    count = segments.shape[0]
    index = jnp.arange(count, dtype=jnp.int32)
    earlier = index[None, :] < index[:, None]
    same = (segments[None, :] == segments[:, None]) & (segments[None, :] > 0)
    return (index[None, :] == index[:, None]) | earlier & same


def head_prepare(raw, gain, cosine, sine):
    count = raw.shape[0]
    head_dim = gain.shape[0]
    heads = raw.reshape(count, -1, head_dim)
    inverse = lax.rsqrt(jnp.mean(heads * heads, axis=-1, keepdims=True) + eps_norm)
    normed = heads * inverse * gain
    half = head_dim // 2
    turned = jnp.concatenate([-normed[..., half:], normed[..., :half]], axis=-1)
    return (normed * cosine[:, None, :] + turned * sine[:, None, :]).reshape(count, -1)


def feature_gather(values):
    return lax.all_gather(values, "col", axis=1, tiled=True)


def feature_sum(values):
    return lax.psum_scatter(
        values.astype(jnp.bfloat16), "col", scatter_dimension=1, tiled=True
    ).astype(jnp.float32)


def rows_in(operand, weight):
    return jnp.dot(
        operand,
        lax.all_gather(weight, "row", axis=0, tiled=True),
        preferred_element_type=jnp.float32,
    )


def rows_out(operand, weight):
    return lax.dot_general(
        operand,
        lax.all_gather(weight, "row", axis=0, tiled=True),
        (((1,), (1,)), ((), ())),
        preferred_element_type=jnp.float32,
    )


def weight_grads(firsts, seconds):
    blocks = []
    for first, second in zip(firsts, seconds):
        blocks.append(
            lax.dot_general(
                first, second, (((0,), (0,)), ((), ())), preferred_element_type=jnp.float32
            )
        )
    return lax.psum_scatter(
        jnp.concatenate(blocks, axis=1).astype(jnp.bfloat16), "row", scatter_dimension=0, tiled=True
    ).astype(jnp.float32)


def norm_back(partial_grad, unit, inverse, gain, local):
    offset = lax.axis_index("col") * local
    width = unit.shape[1]
    unit_own = lax.dynamic_slice_in_dim(unit, offset, local, 1)
    grad_own = feature_sum(partial_grad)
    gain_own = lax.dynamic_slice_in_dim(gain, offset, local, 0)
    scaled = grad_own * gain_own
    dots = lax.psum(jnp.sum(scaled * unit_own, axis=1), "col")[:, None] / width
    grad_input = inverse * (scaled - unit_own * dots)
    gain_grad = lax.dynamic_update_slice_in_dim(
        jnp.zeros((width,), jnp.float32), jnp.sum(grad_own * unit_own, axis=0), offset, 0
    )
    return (grad_input, gain_grad)


def attend_scores(query, keys, allowed, kv_heads, head_dim):
    count = query.shape[0]
    grouped = query.reshape(count, kv_heads, -1, head_dim)
    keyed = keys.reshape(count, kv_heads, head_dim)
    scores = jnp.einsum(
        "qgrd,kgd->grqk", grouped, keyed, preferred_element_type=jnp.float32
    ) * head_dim ** (-0.5)
    return (jnp.where(allowed, scores, -1e30), grouped, keyed)


def attend_forward(query, keys, values, allowed, kv_heads, head_dim):
    count = query.shape[0]
    scores, grouped, keyed = attend_scores(query, keys, allowed, kv_heads, head_dim)
    peak = jnp.max(scores, axis=-1, keepdims=True)
    weights = jnp.exp(scores - peak)
    total = jnp.sum(weights, axis=-1, keepdims=True)
    probs = (weights / total).astype(jnp.bfloat16)
    valued = values.reshape(count, kv_heads, head_dim)
    attended = jnp.einsum("grqk,kgd->qgrd", probs, valued, preferred_element_type=jnp.float32)
    return (attended.reshape(count, -1), peak + jnp.log(total))


def attend_backward(query, keys, values, allowed, logsum, grad_attended, kv_heads, head_dim):
    count = query.shape[0]
    scores, grouped, keyed = attend_scores(query, keys, allowed, kv_heads, head_dim)
    probs_exact = jnp.exp(scores - logsum)
    probs = probs_exact.astype(jnp.bfloat16)
    valued = values.reshape(count, kv_heads, head_dim)
    grad_grouped = grad_attended.reshape(count, kv_heads, -1, head_dim)
    grad_values = jnp.einsum(
        "grqk,qgrd->kgd", probs, grad_grouped, preferred_element_type=jnp.float32
    )
    grad_probs = jnp.einsum(
        "qgrd,kgd->grqk", grad_grouped, valued, preferred_element_type=jnp.float32
    )
    delta = jnp.sum(probs_exact * grad_probs, axis=-1, keepdims=True)
    grad_scores = (probs_exact * (grad_probs - delta)).astype(jnp.bfloat16)
    grad_query = jnp.einsum(
        "grqk,kgd->qgrd", grad_scores, keyed, preferred_element_type=jnp.float32
    ) * head_dim ** (-0.5)
    grad_keys = jnp.einsum(
        "grqk,qgrd->kgd", grad_scores, grouped, preferred_element_type=jnp.float32
    ) * head_dim ** (-0.5)
    return (
        grad_query.reshape(count, -1),
        grad_keys.reshape(count, -1),
        grad_values.reshape(count, -1).astype(jnp.bfloat16),
    )


def body(
    tokens,
    cotangent,
    segment_ids,
    gain_attn,
    gain_ffn,
    gain_query,
    gain_key,
    w_query,
    w_gate,
    w_key,
    w_value,
    w_out,
    w_ffgate,
    w_up,
    w_down,
):
    local = tokens.shape[1]
    head_dim = gain_query.shape[0]
    query_width = w_query.shape[1]
    key_width = w_key.shape[1]
    kv_heads = key_width // head_dim
    hidden_width = w_ffgate.shape[1]
    live = (segment_ids > 0).astype(jnp.float32)[:, None]
    cosine, sine = rope_tables(segment_ids, head_dim)
    allowed = attend_mask(segment_ids)
    attn_weight = jnp.concatenate([w_query, w_gate, w_key, w_value], axis=1)
    ffn_weight = jnp.concatenate([w_ffgate, w_up], axis=1)
    blocks = (attn_weight, ffn_weight, w_out, w_down)

    def apply_in(operand, which_block):
        return rows_in(operand, blocks[which_block])

    def apply_out(operand, which_block):
        return rows_out(operand, blocks[which_block])

    inputs = feature_gather(tokens).astype(jnp.float32)
    normed1, inverse1 = norm_rows(inputs, gain_attn)
    hidden1 = normed1.astype(jnp.bfloat16)
    joint = apply_in(hidden1, 0)
    query_raw = joint[:, :query_width]
    gate_raw = joint[:, query_width : 2 * query_width]
    key_raw = joint[:, 2 * query_width : 2 * query_width + key_width]
    values = joint[:, 2 * query_width + key_width :].astype(jnp.bfloat16)
    prepare = partial(head_prepare, cosine=cosine, sine=sine)
    query = prepare(query_raw, gain_query).astype(jnp.bfloat16)
    keys = prepare(key_raw, gain_key).astype(jnp.bfloat16)
    attended, logsum = attend_forward(query, keys, values, allowed, kv_heads, head_dim)
    gate_sig = jax.nn.sigmoid(gate_raw)
    mixed = (attended * gate_sig).astype(jnp.bfloat16)
    resid = tokens.astype(jnp.float32) + feature_sum(apply_out(mixed, 2))
    resid_full = feature_gather(resid.astype(jnp.bfloat16)).astype(jnp.float32)
    normed2, inverse2 = norm_rows(resid_full, gain_ffn)
    hidden2 = normed2.astype(jnp.bfloat16)
    ffn_joint = apply_in(hidden2, 1)
    ff_gate = ffn_joint[:, :hidden_width]
    ff_up = ffn_joint[:, hidden_width:]
    sig_gate = jax.nn.sigmoid(ff_gate)
    activated = (jax.nn.silu(ff_gate) * ff_up).astype(jnp.bfloat16)
    ffn_out = feature_sum(apply_out(activated, 3))
    output = (live * (resid + ffn_out)).astype(jnp.bfloat16)
    grad_out = live * cotangent.astype(jnp.float32)
    grad_ffn_full = feature_gather(grad_out.astype(jnp.bfloat16))
    grad_act = apply_in(grad_ffn_full, 3)
    grad_ffup = (grad_act * (ff_gate * sig_gate)).astype(jnp.bfloat16)
    grad_ffgate = (grad_act * ff_up * sig_gate * (1.0 + ff_gate * (1.0 - sig_gate))).astype(
        jnp.bfloat16
    )
    grad_pair = jnp.concatenate([grad_ffgate, grad_ffup], axis=1)
    ffn_grads = weight_grads((hidden2, grad_ffn_full), (grad_pair, activated))
    grad_input2, gain_ffn_grad = norm_back(
        apply_out(grad_pair, 1), resid_full * inverse2, inverse2, gain_ffn, local
    )
    grad_resid = grad_out + grad_input2
    grad_branch_full = feature_gather(grad_resid.astype(jnp.bfloat16))
    grad_mixed = apply_in(grad_branch_full, 2)
    grad_attended = (grad_mixed * gate_sig).astype(jnp.bfloat16)
    grad_gate_raw = (grad_mixed * attended * gate_sig * (1.0 - gate_sig)).astype(jnp.bfloat16)
    grad_query, grad_keys, grad_values = attend_backward(
        query, keys, values, allowed, logsum, grad_attended, kv_heads, head_dim
    )
    unused_query, query_back = jax.vjp(prepare, query_raw, gain_query)
    grad_query_raw, grad_gain_query = query_back(grad_query)
    unused_key, key_back = jax.vjp(prepare, key_raw, gain_key)
    grad_key_raw, grad_gain_key = key_back(grad_keys)
    grad_joint = jnp.concatenate(
        [
            grad_query_raw.astype(jnp.bfloat16),
            grad_gate_raw,
            grad_key_raw.astype(jnp.bfloat16),
            grad_values,
        ],
        axis=1,
    )
    attn_grads = weight_grads((hidden1, grad_branch_full), (grad_joint, mixed))
    grad_input1, gain_attn_grad = norm_back(
        apply_out(grad_joint, 0), inputs * inverse1, inverse1, gain_attn, local
    )
    grad_tokens = grad_resid + grad_input1
    gains = lax.psum(
        (gain_attn_grad, gain_ffn_grad, grad_gain_query, grad_gain_key), ("row", "col")
    )
    second_cut = 2 * query_width
    third_cut = 2 * query_width + key_width
    fourth_cut = 2 * query_width + 2 * key_width
    return (
        output,
        grad_tokens,
        gains[0],
        gains[1],
        gains[2],
        gains[3],
        attn_grads[:, :query_width],
        attn_grads[:, query_width:second_cut],
        attn_grads[:, second_cut:third_cut],
        attn_grads[:, third_cut:fourth_cut],
        attn_grads[:, fourth_cut:],
        ffn_grads[:, :hidden_width],
        ffn_grads[:, hidden_width : 2 * hidden_width],
        ffn_grads[:, 2 * hidden_width :],
    )


def plain(mesh):
    in_specs = (
        P("row", "col"),
        P("row", "col"),
        P("row"),
        P(),
        P(),
        P(),
        P(),
        P("row", "col"),
        P("row", "col"),
        P("row", "col"),
        P("row", "col"),
        P("row", "col"),
        P("row", "col"),
        P("row", "col"),
        P("row", "col"),
    )
    out_specs = (
        P("row", "col"),
        P("row", "col"),
        P(),
        P(),
        P(),
        P(),
        P("row", "col"),
        P("row", "col"),
        P("row", "col"),
        P("row", "col"),
        P("row", "col"),
        P("row", "col"),
        P("row", "col"),
        P("row", "col"),
    )
    return jax.shard_map(body, mesh=mesh, in_specs=in_specs, out_specs=out_specs, check_vma=False)


def tie(*values):
    return lax.optimization_barrier(values)


def flip(values, axis):
    return lax.ppermute(values, axis, [(0, 1), (1, 0)])


light = pl.CostEstimate(flops=0, bytes_accessed=0, transcendentals=0)


class Line:
    def __init__(self):
        self.token = jnp.zeros((8, 128), jnp.float32)

    def enter(self, *values):
        *values, self.token = lax.optimization_barrier((*values, self.token))
        return values

    def run(self, work, *values):
        result = work(*self.enter(*values))
        if isinstance(result, (tuple, list)):
            return self.enter(*result)
        return self.enter(result)[0]


def pack_kernel(normed, place_ref, gain_ref, *refs):
    blocks, out_ref = refs[:4], refs[5]
    width = blocks[0].shape[1]
    place = place_ref[0]
    if normed:
        values = [block[...].astype(jnp.float32) for block in blocks]
        squares = sum(jnp.sum(v * v, axis=1, keepdims=True) for v in values)
        inverse = lax.rsqrt(squares / (4 * width) + eps_norm)
        refs[6][...] = inverse
    for index in range(4):
        columns = pl.ds(pl.multiple_of((place ^ index) * width, width), width)
        if normed:
            result = values[index] * inverse * gain_ref[:, columns]
            out_ref[:, columns] = result.astype(out_ref.dtype)
        else:
            out_ref[:, columns] = blocks[index][...]


def pack(blocks, place, gain, normed, step, target):
    count, width = blocks[0].shape
    tile = 256
    tiles = count // tile
    out_shape = [jax.ShapeDtypeStruct((2 * count, 4 * width), jnp.bfloat16)]
    out_specs = [pl.BlockSpec((tile, 4 * width), lambda i: (i + step * tiles, 0))]
    if normed:
        out_shape.append(jax.ShapeDtypeStruct((count, 1), jnp.float32))
        out_specs.append(pl.BlockSpec((tile, 1), lambda i: (i, 0)))
    aliases = {}
    if target is None:
        target = place.reshape(1)
    else:
        aliases = {6: 0}
    return pl.pallas_call(
        partial(pack_kernel, normed),
        grid=(tiles,),
        in_specs=[
            pl.BlockSpec(memory_space=pltpu.SMEM),
            pl.BlockSpec((1, 4 * width), lambda i: (0, 0)),
        ]
        + [pl.BlockSpec((tile, width), lambda i: (i, 0))] * 4
        + [pl.BlockSpec(memory_space=pl.ANY if aliases else pltpu.SMEM)],
        out_specs=out_specs,
        out_shape=out_shape,
        input_output_aliases=aliases,
        cost_estimate=light,
    )(place.reshape(1), gain.reshape(1, -1), *blocks, target)


def direct(own):
    return (flip(own, "y"), flip(own, "x"), flip(own, "core"))


def relay(own, via_y, via_x, own_core, place, gain, normed):
    half = own.shape[0] // 2
    upper = flip(via_y[:half], "x")
    lower = flip(via_x[half:], "y")
    x_core = flip(via_x, "core")
    near = pack((own, own_core, via_y, flip(via_y, "core")), place, gain, normed, 0, None)
    return (via_x, x_core, upper, lower, *near)


def diagonal(via_x, x_core, upper, lower, target, place, gain, normed):
    crossed = jnp.concatenate([upper, lower], axis=0)
    far = (via_x, x_core, crossed, flip(crossed, "core"))
    return pack(far, place, gain, normed, 1, target)[0]


def halves_kernel(count, across_ref, *refs):
    across = across_ref[0]
    keep_ref, give_ref = refs[count:]
    at = 0
    for weight_ref in refs[:count]:
        width = weight_ref.shape[1] // 2
        for target, side in ((keep_ref, across), (give_ref, 1 - across)):
            target[:, at : at + width] = weight_ref[:, pl.ds(pl.multiple_of(side * width, width), width)]
        at += width


def halves(weights, across):
    rows = weights[0].shape[0]
    width = sum(weight.shape[1] for weight in weights) // 2
    shape = jax.ShapeDtypeStruct((rows, width), jnp.bfloat16)
    whole = pl.BlockSpec(memory_space=pltpu.VMEM)
    return pl.pallas_call(
        partial(halves_kernel, len(weights)),
        in_specs=[pl.BlockSpec(memory_space=pltpu.SMEM)] + [whole] * len(weights),
        out_specs=[whole, whole],
        out_shape=[shape, shape],
        cost_estimate=light,
    )(across.reshape(1), *weights)


def weight_rows(keep, got, across):
    top = jnp.where(across == 0, keep, got)
    bottom = jnp.where(across == 0, got, keep)
    return jnp.concatenate([top, bottom], axis=0)


def weight_gather(rows):
    return lax.all_gather(rows, "z", axis=0, tiled=True)


def grad_scatter(grads):
    return lax.psum_scatter(grads, "z", scatter_dimension=0, tiled=True)


def keep_rows(summed, across):
    rows = summed.shape[0] // 2
    return lax.dynamic_slice_in_dim(summed, across * rows, rows, 0)


def give_rows(summed, across):
    return keep_rows(summed, 1 - across)


def z_flip(values, step):
    return lax.ppermute(values, "z", [(i, i ^ step) for i in range(4)])


vmem = pltpu.CompilerParams(vmem_limit_bytes=56 * 1024 * 1024)


def fold_dot(operand, weight, place, index, column):
    rows, width = weight.shape[0] // 4, operand.shape[1]
    block = lax.dynamic_slice(
        weight, ((place ^ index) * rows, jnp.int32(column * width)), (rows, width)
    )
    return product_nt(operand, block)


def fold_sent(operand, weight, place, column=0):
    return tuple(
        flip(fold_dot(operand, weight, place, index, column).astype(jnp.bfloat16), "core")
        for index in (3, 1)
    )


def fold_held(operand, weight, place, far_got, near_got, column=0):
    low = jnp.bfloat16
    far = (fold_dot(operand, weight, place, 2, column) + far_got).astype(low)
    near = (fold_dot(operand, weight, place, 0, column) + near_got).astype(low)
    count = far.shape[0] // 2
    half = count // 2
    upper = jnp.stack([near[count : count + half], far[count : count + half]])
    lower = jnp.stack([far[half:count], far[count + half :]])
    return (near, far, upper, lower)


def fold_begin(operand, weight, place, column=0):
    return fold_held(operand, weight, place, *fold_sent(operand, weight, place, column), column)


def fold_cross(near, far, upper, lower):
    return (near, far, flip(upper, "x"), flip(lower, "y"))


def fold_close(near, far, upper, lower):
    low, wide = jnp.bfloat16, jnp.float32
    count = far.shape[0] // 2
    half = count // 2
    upper_near = near[:half].astype(wide) + upper[0]
    upper_far = (far[:half].astype(wide) + upper[1]).astype(low)
    lower_own = near[half:count].astype(wide) + lower[0]
    lower_other = (near[count + half :].astype(wide) + lower[1]).astype(low)
    return (upper_near, flip(upper_far, "y"), lower_own, flip(lower_other, "x"))


def fold_end(upper_near, upper_got, lower_own, lower_got):
    return jnp.concatenate([upper_near + upper_got, lower_own + lower_got], axis=0)


def matmul_kernel(form, operand_ref, weight_ref, out_ref):
    out_ref[...] = form(operand_ref[...], weight_ref[...]).astype(out_ref.dtype)


def dot_in(operand, weight, width, column=0):
    count, depth = operand.shape
    tile = 512
    return pl.pallas_call(
        partial(matmul_kernel, product_nn),
        grid=(count // tile,),
        in_specs=[
            pl.BlockSpec((tile, depth), lambda i: (i, 0)),
            pl.BlockSpec((depth, width), lambda i: (0, column)),
        ],
        out_specs=pl.BlockSpec((tile, width), lambda i: (i, 0)),
        out_shape=jax.ShapeDtypeStruct((count, width), jnp.float32),
        compiler_params=vmem,
        cost_estimate=light,
    )(operand, weight)


def dot_grad(first, second, width=None, column=0):
    count, rows = first.shape
    width = second.shape[1] if width is None else width
    tile = 512
    return pl.pallas_call(
        partial(matmul_kernel, product_tn),
        grid=(rows // tile,),
        in_specs=[
            pl.BlockSpec((count, tile), lambda i: (0, i)),
            pl.BlockSpec((count, width), lambda i: (0, column)),
        ],
        out_specs=pl.BlockSpec((tile, width), lambda i: (i, 0)),
        out_shape=jax.ShapeDtypeStruct((rows, width), jnp.bfloat16),
        compiler_params=vmem,
        cost_estimate=light,
    )(first, second)


def ffn_kernel(hidden_ref, weight_ref, grad_ref, activated_ref, pair_ref):
    width = activated_ref.shape[1]
    low = jnp.bfloat16
    step = 256
    for at in range(0, width, step):
        ff_gate = product_nn(hidden_ref[...], weight_ref[:, at : at + step])
        ff_up = product_nn(hidden_ref[...], weight_ref[:, width + at : width + at + step])
        grad = grad_ref[:, at : at + step]
        sig_gate = jax.nn.sigmoid(ff_gate)
        passed = ff_gate * sig_gate
        activated_ref[:, at : at + step] = (passed * ff_up).astype(low)
        pair_ref[:, width + at : width + at + step] = (grad * passed).astype(low)
        pair_ref[:, at : at + step] = (
            grad * ff_up * sig_gate * (1.0 + ff_gate * (1.0 - sig_gate))
        ).astype(low)


def ffn(hidden, weight, grad):
    count, depth = hidden.shape
    width = weight.shape[1] // 2
    tile = 256
    return pl.pallas_call(
        ffn_kernel,
        grid=(count // tile,),
        in_specs=[
            pl.BlockSpec((tile, depth), lambda i: (i, 0)),
            pl.BlockSpec((depth, 2 * width), lambda i: (0, 0)),
            pl.BlockSpec((tile, width), lambda i: (i, 0)),
        ],
        out_specs=[
            pl.BlockSpec((tile, width), lambda i: (i, 0)),
            pl.BlockSpec((tile, 2 * width), lambda i: (i, 0)),
        ],
        out_shape=[
            jax.ShapeDtypeStruct((count, width), jnp.bfloat16),
            jax.ShapeDtypeStruct((count, 2 * width), jnp.bfloat16),
        ],
        compiler_params=vmem,
        cost_estimate=light,
    )(hidden, weight, grad)


def row_tables(segments, head_dim):
    count = segments.shape[0]
    index = jnp.arange(count, dtype=jnp.int32)
    previous = jnp.concatenate([jnp.full((1,), -1, jnp.int32), segments[:-1]])
    starts = lax.cummax(jnp.where(segments != previous, index, 0), axis=0)
    position = (index - starts).astype(jnp.float32)
    half = head_dim // 2
    freqs = jnp.power(rope_base, -(jnp.arange(half, dtype=jnp.float32) * 2.0 / head_dim))
    angle = position[:, None] * freqs[None, :]
    cosine, sine = jnp.cos(angle), jnp.sin(angle)
    return (
        jnp.concatenate([cosine, cosine], axis=1),
        jnp.concatenate([-sine, sine], axis=1),
        jnp.where(segments > 0, starts, index)[None, :],
    )


def product_nt(first, second):
    return lax.dot_general(
        first, second, (((1,), (1,)), ((), ())), preferred_element_type=jnp.float32
    )


def product_tn(first, second):
    return lax.dot_general(
        first, second, (((0,), (0,)), ((), ())), preferred_element_type=jnp.float32
    )


def product_nn(first, second):
    return lax.dot_general(
        first, second, (((1,), (0,)), ((), ())), preferred_element_type=jnp.float32
    )


def prepare_tile(raw, gain, cosine, sine):
    inverse = lax.rsqrt(jnp.mean(raw * raw, axis=1, keepdims=True) + eps_norm)
    normed = raw * inverse * gain
    turned = pltpu.roll(normed, raw.shape[1] // 2, 1)
    return (normed * cosine + turned * sine).astype(jnp.bfloat16)


def prepare_back(raw, gain, cosine, sine, grad):
    inverse = lax.rsqrt(jnp.mean(raw * raw, axis=1, keepdims=True) + eps_norm)
    unit = raw * inverse
    grad_normed = grad * cosine + pltpu.roll(grad * sine, raw.shape[1] // 2, 1)
    scaled = grad_normed * gain
    grad_raw = inverse * (scaled - unit * jnp.mean(scaled * unit, axis=1, keepdims=True))
    return (grad_raw.astype(jnp.bfloat16), jnp.sum(grad_normed * unit, axis=0, keepdims=True))


def allowed_tile(first_ref, start, tile, reach):
    rows = lax.broadcasted_iota(jnp.int32, (reach, tile), 0)
    columns = lax.broadcasted_iota(jnp.int32, (reach, tile), 1) + start
    return (rows >= first_ref[0, :, pl.ds(start, tile)]) & (rows <= columns)


def attend_kernel(
    heads, tile, joint_ref, cos_ref, sin_ref, first_ref, gain_query_ref, gain_key_ref,
    mixed_ref, attended_ref, query_ref, key_ref, logsum_ref,
):
    count, head_dim = cos_ref.shape
    scale = head_dim ** (-0.5)
    low = jnp.bfloat16
    key_at = 2 * heads * head_dim
    tiles = count // tile
    for part in range(tiles):
        rows = pl.ds(part * tile, tile)
        key_ref[rows, :] = prepare_tile(
            joint_ref[rows, key_at : key_at + head_dim],
            gain_key_ref[...],
            cos_ref[rows, :],
            sin_ref[rows, :],
        )
    for head in range(heads):
        columns = slice(head * head_dim, (head + 1) * head_dim)
        gates = slice((heads + head) * head_dim, (heads + head + 1) * head_dim)
        for part in range(tiles):
            rows = pl.ds(part * tile, tile)
            reach = (part + 1) * tile
            query = prepare_tile(
                joint_ref[rows, columns], gain_query_ref[...], cos_ref[rows, :], sin_ref[rows, :]
            )
            query_ref[rows, columns] = query
            scores = product_nt(key_ref[:reach, :], query) * scale
            scores = jnp.where(allowed_tile(first_ref, part * tile, tile, reach), scores, -1e30)
            peak = jnp.max(scores, axis=0, keepdims=True)
            weights = jnp.exp(scores - peak)
            total = jnp.sum(weights, axis=0, keepdims=True)
            probs = (weights * (1.0 / total)).astype(low)
            logsum_ref[0, head : head + 1, rows] = peak + jnp.log(total)
            values = joint_ref[:reach, key_at + head_dim : key_at + 2 * head_dim].astype(low)
            attended = product_tn(values, probs).T
            attended_ref[rows, columns] = attended
            gate = joint_ref[rows, gates]
            mixed_ref[rows, columns] = (attended * jax.nn.sigmoid(gate)).astype(low)


def attend_back_kernel(
    heads, tile, joint_ref, cos_ref, sin_ref, first_ref, gain_query_ref, gain_key_ref,
    attended_ref, query_ref, key_ref, logsum_ref, grad_mixed_ref,
    grad_joint_ref, grad_gain_ref, grad_key_acc, grad_value_acc,
):
    count, head_dim = cos_ref.shape
    scale = head_dim ** (-0.5)
    low = jnp.bfloat16
    key_at = 2 * heads * head_dim
    value_at = key_at + head_dim
    tiles = count // tile
    gain_query = jnp.zeros((1, head_dim), jnp.float32)
    gain_key = jnp.zeros((1, head_dim), jnp.float32)
    for head in range(heads):
        columns = slice(head * head_dim, (head + 1) * head_dim)
        gates = slice((heads + head) * head_dim, (heads + head + 1) * head_dim)
        for part in reversed(range(tiles)):
            rows = pl.ds(part * tile, tile)
            reach = (part + 1) * tile
            fresh = head == 0 and part == tiles - 1
            gate = jax.nn.sigmoid(joint_ref[rows, gates])
            grad_mixed = grad_mixed_ref[rows, columns]
            gated = grad_mixed * gate
            grad_attended = gated.astype(low)
            grad_joint_ref[rows, gates] = (gated * attended_ref[rows, columns] * (1.0 - gate)).astype(
                low
            )
            query = query_ref[rows, columns]
            keys = key_ref[:reach, :]
            values = joint_ref[:reach, value_at : value_at + head_dim].astype(low)
            scores = product_nt(keys, query) * scale
            logsum = logsum_ref[0, head : head + 1, rows]
            probs = jnp.where(
                allowed_tile(first_ref, part * tile, tile, reach), jnp.exp(scores - logsum), 0.0
            )
            grad_value = product_nn(probs.astype(low), grad_attended)
            grad_probs = product_nt(values, grad_attended)
            delta = jnp.sum(probs * grad_probs, axis=0, keepdims=True)
            grad_scores = (probs * (grad_probs - delta)).astype(low)
            grad_key = product_nn(grad_scores, query)
            if fresh:
                grad_value_acc[...] = grad_value
                grad_key_acc[...] = grad_key
            else:
                grad_value_acc[:reach, :] += grad_value
                grad_key_acc[:reach, :] += grad_key
            grad_query = product_tn(keys, grad_scores).T * scale
            grad_raw, gain_part = prepare_back(
                joint_ref[rows, columns],
                gain_query_ref[...],
                cos_ref[rows, :],
                sin_ref[rows, :],
                grad_query,
            )
            grad_joint_ref[rows, columns] = grad_raw
            gain_query = gain_query + gain_part
    for part in range(tiles):
        rows = pl.ds(part * tile, tile)
        grad_raw, gain_part = prepare_back(
            joint_ref[rows, key_at:value_at],
            gain_key_ref[...],
            cos_ref[rows, :],
            sin_ref[rows, :],
            grad_key_acc[rows, :] * scale,
        )
        grad_joint_ref[rows, key_at:value_at] = grad_raw
        gain_key = gain_key + gain_part
        grad_joint_ref[rows, value_at : value_at + head_dim] = grad_value_acc[rows, :].astype(low)
    both = jnp.concatenate([gain_query, gain_key], axis=0)

    @pl.when(pl.program_id(0) == 0)
    def begin():
        grad_gain_ref[...] = both

    @pl.when(pl.program_id(0) > 0)
    def add():
        grad_gain_ref[...] += both


def attend_specs(count, head_dim, heads, joint_width):
    wide = lambda width: pl.BlockSpec((count, width), lambda s: (s, 0))
    row = pl.BlockSpec((1, head_dim), lambda s: (0, 0))
    lead = [
        wide(joint_width),
        wide(head_dim),
        wide(head_dim),
        pl.BlockSpec((1, 1, count), lambda s: (s, 0, 0)),
        row,
        row,
    ]
    kept = [
        wide(heads * head_dim),
        wide(heads * head_dim),
        wide(head_dim),
        pl.BlockSpec((1, heads, count), lambda s: (s, 0, 0)),
    ]
    return (lead, kept, wide)


def attend_fwd(joint, cosine, sine, first, gain_query, gain_key, heads, count):
    head_dim = cosine.shape[1]
    lead, kept, wide = attend_specs(count, head_dim, heads, joint.shape[1])
    total = joint.shape[0]
    shape = jax.ShapeDtypeStruct
    return pl.pallas_call(
        partial(attend_kernel, heads, 256),
        grid=(total // count,),
        in_specs=lead,
        out_specs=[wide(heads * head_dim)] + kept,
        out_shape=[
            shape((total, heads * head_dim), jnp.bfloat16),
            shape((total, heads * head_dim), jnp.float32),
            shape((total, heads * head_dim), jnp.bfloat16),
            shape((total, head_dim), jnp.bfloat16),
            shape((total // count, heads, count), jnp.float32),
        ],
        compiler_params=pltpu.CompilerParams(vmem_limit_bytes=40 * 1024 * 1024),
        cost_estimate=light,
    )(joint, cosine, sine, first, gain_query.reshape(1, -1), gain_key.reshape(1, -1))


def attend_bwd(joint, cosine, sine, first, gain_query, gain_key, kept_values, grad_mixed, count):
    head_dim = cosine.shape[1]
    heads = grad_mixed.shape[1] // head_dim
    lead, kept, wide = attend_specs(count, head_dim, heads, joint.shape[1])
    total = joint.shape[0]
    shape = jax.ShapeDtypeStruct
    return pl.pallas_call(
        partial(attend_back_kernel, heads, 256),
        grid=(total // count,),
        in_specs=lead + kept + [wide(heads * head_dim)],
        out_specs=[wide(joint.shape[1]), pl.BlockSpec((2, head_dim), lambda s: (0, 0))],
        out_shape=[shape(joint.shape, jnp.bfloat16), shape((2, head_dim), jnp.float32)],
        scratch_shapes=[
            pltpu.VMEM((count, head_dim), jnp.float32),
            pltpu.VMEM((count, head_dim), jnp.float32),
        ],
        compiler_params=pltpu.CompilerParams(vmem_limit_bytes=48 * 1024 * 1024),
        cost_estimate=light,
    )(
        joint, cosine, sine, first, gain_query.reshape(1, -1), gain_key.reshape(1, -1),
        *kept_values, grad_mixed,
    )


def fast_body(
    tokens,
    cotangent,
    segment_ids,
    gain_attn,
    gain_ffn,
    gain_query,
    gain_key,
    w_query,
    w_gate,
    w_key,
    w_value,
    w_out,
    w_ffgate,
    w_up,
    w_down,
):
    across = lax.axis_index("x")
    place = lax.axis_index("y") * 2 + lax.axis_index("core")
    count, local = tokens.shape
    width = gain_attn.shape[0]
    head_dim = gain_query.shape[0]
    low = jnp.bfloat16
    query_width = w_query.shape[1] // 2
    key_width = w_key.shape[1] // 2
    heads = query_width // head_dim
    hidden_width = w_ffgate.shape[1] // 2
    live = (segment_ids > 0).astype(jnp.float32)[:, None]
    offset = place * local
    gain_attn_own = lax.dynamic_slice_in_dim(gain_attn, offset, local, 0)
    gain_ffn_own = lax.dynamic_slice_in_dim(gain_ffn, offset, local, 0)

    line = Line()
    half = count // 2
    joint_width = 2 * query_width + 2 * key_width
    rows_of = partial(weight_rows, across=across)

    first_columns = [w_query, w_gate, w_key, w_value, w_out]

    def open_first(tokens, *weights):
        upper_y = flip(tokens[:half], "y")
        keep, give = halves(weights, across)
        got = flip(give, "x")
        return (rows_of(keep, got), upper_y)

    first_rows, upper_y = line.run(open_first, tokens, *first_columns)
    first_weight = weight_gather(first_rows)
    grad_out = live * cotangent.astype(jnp.float32)
    grad_out_low = grad_out.astype(low)

    def open_second(tokens, segment_ids, upper_y, w_ffgate, w_up, w_down):
        lower_y = flip(tokens[half:], "y")
        via_x = flip(tokens, "x")
        own_core = flip(tokens, "core")
        other = flip(segment_ids, "x")
        via_y = jnp.concatenate([upper_y, lower_y], axis=0)
        return (via_y, via_x, own_core, other, *halves([w_ffgate, w_up], across), *halves([w_down], across))

    via_y, via_x, own_core, segment_other, keep_pair, give_pair, keep_down, give_down = line.run(
        open_second, tokens, segment_ids, upper_y, w_ffgate, w_up, w_down
    )

    def open_third(tokens, via_y, via_x, own_core, keep_down, give_down):
        steps = relay(tokens, via_y, via_x, own_core, place, gain_attn, True)
        return (rows_of(keep_down, flip(give_down, "x")), *steps)

    down_rows, *steps, target, inverse1 = line.run(
        open_third, tokens, via_y, via_x, own_core, keep_down, give_down
    )
    down_weight = weight_gather(down_rows)

    def open_fourth(keep_pair, give_pair, segment_ids, segment_other, *steps):
        hidden1 = diagonal(*steps, place, gain_attn, True)
        pair_rows = rows_of(keep_pair, flip(give_pair, "x"))
        segments = jnp.stack([segment_ids, segment_other])
        cosine, sine, first = jax.vmap(partial(row_tables, head_dim=head_dim))(segments)
        cosine = cosine.reshape(2 * count, head_dim)
        sine = sine.reshape(2 * count, head_dim)
        return (hidden1, pair_rows, cosine, sine, first)

    hidden1, pair_rows, cosine, sine, first = line.run(
        open_fourth, keep_pair, give_pair, segment_ids, segment_other, *steps, target
    )
    pair_weight = weight_gather(pair_rows)
    out_column = joint_width // query_width

    def attend(hidden1, first_weight, grad_out_low):
        via_out = direct(grad_out_low)
        joint = dot_in(hidden1, first_weight, joint_width)
        mixed, *kept = attend_fwd(
            joint, cosine, sine, first, gain_query, gain_key, heads, count
        )
        return (joint, mixed, *kept, *via_out)

    joint, mixed, *rest = line.run(attend, hidden1, first_weight, grad_out_low)
    kept, via_out = rest[:4], rest[4:]

    def begin_out(mixed, first_weight, grad_out_low, *via_out):
        steps = relay(grad_out_low, *via_out, place, gain_ffn, False)
        return (*fold_begin(mixed, first_weight, place, out_column), *steps)

    sums = line.run(begin_out, mixed, first_weight, grad_out_low, *via_out)
    sums, steps = sums[:4], sums[4:]

    def cross_out(*values):
        return (*fold_cross(*values[:4]), diagonal(*values[4:], place, gain_ffn, False))

    *sums, grad_out_full = line.run(cross_out, *sums, *steps)
    ends = line.run(fold_close, *sums)

    def residual(values, *ends):
        total = values.astype(jnp.float32) + fold_end(*ends)
        return (total, total.astype(low))

    resid, resid_low = line.run(residual, tokens, *ends)

    def start_resid(resid_low, grad_out_full, down_weight):
        return (*direct(resid_low), dot_in(grad_out_full, down_weight, hidden_width))

    *via_resid, grad_act = line.run(start_resid, resid_low, grad_out_full, down_weight)
    *steps, target, inverse2 = line.run(
        lambda *v: relay(*v, place, gain_ffn, True), resid_low, *via_resid
    )
    hidden2 = line.run(lambda *v: diagonal(*v, place, gain_ffn, True), *steps, target)
    activated, grad_pair = line.run(ffn, hidden2, pair_weight, grad_act)
    gate_grad = line.run(lambda h, g: dot_grad(h, g, hidden_width), hidden2, grad_pair)
    gate_sum = grad_scatter(gate_grad)
    sums = line.run(lambda g, w: fold_begin(g, w, place), grad_pair, pair_weight)
    sums = line.run(fold_cross, *sums)

    def close_pair(hidden2, grad_pair, *sums):
        return (*fold_close(*sums), dot_grad(hidden2, grad_pair, hidden_width, 1))

    *ends, up_grad = line.run(close_pair, hidden2, grad_pair, *sums)
    gate_sum, = line.enter(gate_sum)
    up_sum = grad_scatter(up_grad)
    grad_hidden2 = line.run(fold_end, *ends)

    def partial_dots(grad_own, values, inverse, gain_own):
        dots = jnp.sum(grad_own * gain_own * values.astype(jnp.float32) * inverse, axis=1)
        dots = dots.reshape(-1, 128)
        dots = dots + flip(dots, "core")
        return dots + flip(dots, "y")

    def norm_back(grad_own, values, inverse, gain_own, dots, extra):
        unit = values.astype(jnp.float32) * inverse
        dots = dots.reshape(-1, 1) / width
        grad_input = inverse * (grad_own * gain_own - unit * dots) + extra
        return (grad_input, grad_input.astype(low))

    def gain_part(grad_own, values, inverse):
        return jnp.sum(grad_own * (values.astype(jnp.float32) * inverse), axis=0).reshape(-1, 128)

    def back_dots(grad_own, values, inverse, gain_own):
        return (
            partial_dots(grad_own, values, inverse, gain_own),
            gain_part(grad_own, values, inverse),
        )

    dots, gain_ffn_grad = line.run(back_dots, grad_hidden2, resid_low, inverse2, gain_ffn_own)
    grad_resid, grad_branch = line.run(
        norm_back, grad_hidden2, resid_low, inverse2, gain_ffn_own, dots, grad_out
    )

    def start_branch(grad_branch, grad_out_full, activated):
        return (*direct(grad_branch), dot_grad(grad_out_full, activated))

    *via_branch, down_grad = line.run(start_branch, grad_branch, grad_out_full, activated)
    down_sum = grad_scatter(down_grad)

    def relay_branch(grad_branch, gate_sum, activated, down_weight, *via_branch):
        steps = relay(grad_branch, *via_branch, place, gain_ffn, False)
        got = fold_sent(activated, down_weight, place)
        return (flip(give_rows(gate_sum, across), "x"), *got, *steps)

    got_gate, far_got, near_got, *steps = line.run(
        relay_branch, grad_branch, gate_sum, activated, down_weight, *via_branch
    )
    grad_branch_full = line.run(lambda *v: diagonal(*v, place, gain_ffn, False), *steps)

    def mix_back(grad_branch_full, first_weight, mixed):
        return (
            dot_in(grad_branch_full, first_weight, query_width, out_column),
            dot_grad(grad_branch_full, mixed),
        )

    grad_mixed, out_grad = line.run(mix_back, grad_branch_full, first_weight, mixed)
    out_sum = grad_scatter(out_grad)
    sums_ffn = line.run(
        lambda *v: fold_held(v[0], v[1], place, *v[2:]), activated, down_weight, far_got, near_got
    )

    def attend_back(joint, grad_mixed, up_sum, *sums):
        grad_joint, head_gains = attend_bwd(
            joint, cosine, sine, first, gain_query, gain_key, kept, grad_mixed, count
        )
        return (
            grad_joint,
            head_gains,
            *fold_cross(*sums),
            flip(give_rows(up_sum, across), "x"),
        )

    grad_joint, head_gains, *sums_ffn, got_up = line.run(
        attend_back, joint, grad_mixed, up_sum, *sums_ffn
    )

    def close_ffn(hidden1, grad_joint, gain_ffn_grad, head_gains, *sums):
        early = jnp.concatenate([gain_ffn_grad, head_gains], axis=0)
        early = early + flip(early, "x")
        return (*fold_close(*sums), dot_grad(hidden1, grad_joint), early)

    *ends_ffn, attn_grads, early = line.run(
        close_ffn, hidden1, grad_joint, gain_ffn_grad, head_gains, *sums_ffn
    )
    attn_sum = grad_scatter(attn_grads)

    def fold_attn(grad_joint, first_weight, early, down_sum):
        early = early + z_flip(early, 1)
        early = early + z_flip(early, 2)
        got_down = flip(give_rows(down_sum, across), "x")
        return (early, got_down, *fold_begin(grad_joint, first_weight, place))

    early, got_down, *sums = line.run(fold_attn, grad_joint, first_weight, early, down_sum)

    def join(rows, got, low_cut, high_cut):
        keep = keep_rows(rows, across)[:, low_cut:high_cut]
        got = got[:, low_cut:high_cut]
        first, second = jnp.where(across == 0, keep, got), jnp.where(across == 0, got, keep)
        return jnp.concatenate([first, second], axis=1).astype(jnp.float32)

    def join_all(rows, got):
        return join(rows, got, 0, rows.shape[1])

    def cross_attn(resid, gate_sum, got_gate, up_sum, got_up, out_sum, *values):
        output = (live * (resid + fold_end(*values[4:]))).astype(low)
        return (
            output,
            join_all(gate_sum, got_gate),
            join_all(up_sum, got_up),
            flip(give_rows(out_sum, across), "x"),
            *fold_cross(*values[:4]),
        )

    output, ffgate_grad, up_grad, got_out, *sums = line.run(
        cross_attn, resid, gate_sum, got_gate, up_sum, got_up, out_sum, *sums, *ends_ffn
    )

    def close_attn(down_sum, got_down, out_sum, got_out, *sums):
        return (join_all(down_sum, got_down), join_all(out_sum, got_out), *fold_close(*sums))

    down_part, out_part, *ends = line.run(
        close_attn, down_sum, got_down, out_sum, got_out, *sums
    )

    def last_dots(tokens, inverse1, *ends):
        grad_own = fold_end(*ends)
        late = gain_part(grad_own, tokens, inverse1)
        return (
            grad_own,
            partial_dots(grad_own, tokens, inverse1, gain_attn_own),
            late + flip(late, "x"),
        )

    grad_hidden1, dots, late = line.run(last_dots, tokens, inverse1, *ends)

    def last_norm(grad_hidden1, tokens, inverse1, dots, grad_resid, late):
        grad_tokens, unused = norm_back(
            grad_hidden1, tokens, inverse1, gain_attn_own, dots, grad_resid
        )
        late = late + z_flip(late, 1)
        return (grad_tokens, late)

    grad_tokens, late = line.run(
        last_norm, grad_hidden1, tokens, inverse1, dots, grad_resid, late
    )
    late, got_attn = line.run(
        lambda v, s: (v + z_flip(v, 2), flip(give_rows(s, across), "x")), late, attn_sum
    )
    cuts = (
        0,
        query_width,
        2 * query_width,
        2 * query_width + key_width,
        2 * query_width + 2 * key_width,
    )
    blocks = local // 128

    def last_parts(attn_sum, got_attn, late, early):
        own = jnp.stack([late, early[:blocks]])
        spot = lax.dynamic_update_slice_in_dim(
            jnp.zeros((2, width // 128, 128), jnp.float32), own, offset // 128, 1
        ).reshape(-1, 128)
        spot = jnp.concatenate([spot, early[blocks:]], axis=0)
        spot = spot + flip(spot, "core")
        spot = spot + flip(spot, "y")
        return (spot, *[join(attn_sum, got_attn, cuts[i], cuts[i + 1]) for i in range(4)])

    spot, *attn_parts = line.run(last_parts, attn_sum, got_attn, late, early)
    lines = width // 128
    return (
        output,
        grad_tokens,
        spot[:lines].reshape(width),
        spot[lines : 2 * lines].reshape(width),
        spot[2 * lines],
        spot[2 * lines + 1],
        *attn_parts,
        out_part,
        ffgate_grad,
        up_grad,
        down_part,
    )


def solution(mesh):
    rows, columns = mesh.devices.shape

    def run(*args):
        head_dim = args[5].shape[0]
        query_width, key_width = args[7].shape[1], args[9].shape[1]
        one_key_head = key_width == 2 * columns * head_dim and query_width % key_width == 0
        if not (rows == 8 and columns == 4 and one_key_head):
            return plain(mesh)(*args)
        names = ("z", "x", "y", "core")
        inner = Mesh(mesh.devices.reshape(4, 2, 2, 2), names)
        block = P(("z", "x"), ("y", "core"))
        whole = P()
        in_specs = (block, block, P(("z", "x"))) + (whole,) * 4 + (block,) * 8
        out_specs = (block, block) + (whole,) * 4 + (block,) * 8
        return jax.shard_map(
            fast_body, mesh=inner, in_specs=in_specs, out_specs=out_specs, check_vma=False
        )(*args)

    return run
```

```python
from functools import partial

import jax
import jax.numpy as jnp
from jax import lax
from jax.experimental import pallas as pl
from jax.experimental.pallas import tpu as pltpu
from jax.sharding import Mesh
from jax.sharding import PartitionSpec as P

eps_norm = 1e-06
rope_base = 1000000.0


def norm_rows(values, gain):
    inverse = lax.rsqrt(jnp.mean(values * values, axis=-1, keepdims=True) + eps_norm)
    return (values * inverse * gain, inverse)


def rope_tables(segments, head_dim):
    count = segments.shape[0]
    index = jnp.arange(count, dtype=jnp.int32)
    previous = jnp.concatenate([jnp.full((1,), -1, jnp.int32), segments[:-1]])
    starts = lax.cummax(jnp.where(segments != previous, index, 0), axis=0)
    position = (index - starts).astype(jnp.float32)
    half = head_dim // 2
    freqs = jnp.power(rope_base, -(jnp.arange(half, dtype=jnp.float32) * 2.0 / head_dim))
    angle = position[:, None] * freqs[None, :]
    angle = jnp.concatenate([angle, angle], axis=1)
    return (jnp.cos(angle), jnp.sin(angle))


def attend_mask(segments):
    count = segments.shape[0]
    index = jnp.arange(count, dtype=jnp.int32)
    earlier = index[None, :] < index[:, None]
    same = (segments[None, :] == segments[:, None]) & (segments[None, :] > 0)
    return (index[None, :] == index[:, None]) | earlier & same


def head_prepare(raw, gain, cosine, sine):
    count = raw.shape[0]
    head_dim = gain.shape[0]
    heads = raw.reshape(count, -1, head_dim)
    inverse = lax.rsqrt(jnp.mean(heads * heads, axis=-1, keepdims=True) + eps_norm)
    normed = heads * inverse * gain
    half = head_dim // 2
    turned = jnp.concatenate([-normed[..., half:], normed[..., :half]], axis=-1)
    return (normed * cosine[:, None, :] + turned * sine[:, None, :]).reshape(count, -1)


def feature_gather(values):
    return lax.all_gather(values, "col", axis=1, tiled=True)


def feature_sum(values):
    return lax.psum_scatter(
        values.astype(jnp.bfloat16), "col", scatter_dimension=1, tiled=True
    ).astype(jnp.float32)


def rows_in(operand, weight):
    return jnp.dot(
        operand,
        lax.all_gather(weight, "row", axis=0, tiled=True),
        preferred_element_type=jnp.float32,
    )


def rows_out(operand, weight):
    return lax.dot_general(
        operand,
        lax.all_gather(weight, "row", axis=0, tiled=True),
        (((1,), (1,)), ((), ())),
        preferred_element_type=jnp.float32,
    )


def weight_grads(firsts, seconds):
    blocks = []
    for first, second in zip(firsts, seconds):
        blocks.append(
            lax.dot_general(
                first, second, (((0,), (0,)), ((), ())), preferred_element_type=jnp.float32
            )
        )
    return lax.psum_scatter(
        jnp.concatenate(blocks, axis=1).astype(jnp.bfloat16), "row", scatter_dimension=0, tiled=True
    ).astype(jnp.float32)


def norm_back(partial_grad, unit, inverse, gain, local):
    offset = lax.axis_index("col") * local
    width = unit.shape[1]
    unit_own = lax.dynamic_slice_in_dim(unit, offset, local, 1)
    grad_own = feature_sum(partial_grad)
    gain_own = lax.dynamic_slice_in_dim(gain, offset, local, 0)
    scaled = grad_own * gain_own
    dots = lax.psum(jnp.sum(scaled * unit_own, axis=1), "col")[:, None] / width
    grad_input = inverse * (scaled - unit_own * dots)
    gain_grad = lax.dynamic_update_slice_in_dim(
        jnp.zeros((width,), jnp.float32), jnp.sum(grad_own * unit_own, axis=0), offset, 0
    )
    return (grad_input, gain_grad)


def attend_scores(query, keys, allowed, kv_heads, head_dim):
    count = query.shape[0]
    grouped = query.reshape(count, kv_heads, -1, head_dim)
    keyed = keys.reshape(count, kv_heads, head_dim)
    scores = jnp.einsum(
        "qgrd,kgd->grqk", grouped, keyed, preferred_element_type=jnp.float32
    ) * head_dim ** (-0.5)
    return (jnp.where(allowed, scores, -1e30), grouped, keyed)


def attend_forward(query, keys, values, allowed, kv_heads, head_dim):
    count = query.shape[0]
    scores, grouped, keyed = attend_scores(query, keys, allowed, kv_heads, head_dim)
    peak = jnp.max(scores, axis=-1, keepdims=True)
    weights = jnp.exp(scores - peak)
    total = jnp.sum(weights, axis=-1, keepdims=True)
    probs = (weights / total).astype(jnp.bfloat16)
    valued = values.reshape(count, kv_heads, head_dim)
    attended = jnp.einsum("grqk,kgd->qgrd", probs, valued, preferred_element_type=jnp.float32)
    return (attended.reshape(count, -1), peak + jnp.log(total))


def attend_backward(query, keys, values, allowed, logsum, grad_attended, kv_heads, head_dim):
    count = query.shape[0]
    scores, grouped, keyed = attend_scores(query, keys, allowed, kv_heads, head_dim)
    probs_exact = jnp.exp(scores - logsum)
    probs = probs_exact.astype(jnp.bfloat16)
    valued = values.reshape(count, kv_heads, head_dim)
    grad_grouped = grad_attended.reshape(count, kv_heads, -1, head_dim)
    grad_values = jnp.einsum(
        "grqk,qgrd->kgd", probs, grad_grouped, preferred_element_type=jnp.float32
    )
    grad_probs = jnp.einsum(
        "qgrd,kgd->grqk", grad_grouped, valued, preferred_element_type=jnp.float32
    )
    delta = jnp.sum(probs_exact * grad_probs, axis=-1, keepdims=True)
    grad_scores = (probs_exact * (grad_probs - delta)).astype(jnp.bfloat16)
    grad_query = jnp.einsum(
        "grqk,kgd->qgrd", grad_scores, keyed, preferred_element_type=jnp.float32
    ) * head_dim ** (-0.5)
    grad_keys = jnp.einsum(
        "grqk,qgrd->kgd", grad_scores, grouped, preferred_element_type=jnp.float32
    ) * head_dim ** (-0.5)
    return (
        grad_query.reshape(count, -1),
        grad_keys.reshape(count, -1),
        grad_values.reshape(count, -1).astype(jnp.bfloat16),
    )


def body(
    tokens,
    cotangent,
    segment_ids,
    gain_attn,
    gain_ffn,
    gain_query,
    gain_key,
    w_query,
    w_gate,
    w_key,
    w_value,
    w_out,
    w_ffgate,
    w_up,
    w_down,
):
    local = tokens.shape[1]
    head_dim = gain_query.shape[0]
    query_width = w_query.shape[1]
    key_width = w_key.shape[1]
    kv_heads = key_width // head_dim
    hidden_width = w_ffgate.shape[1]
    live = (segment_ids > 0).astype(jnp.float32)[:, None]
    cosine, sine = rope_tables(segment_ids, head_dim)
    allowed = attend_mask(segment_ids)
    attn_weight = jnp.concatenate([w_query, w_gate, w_key, w_value], axis=1)
    ffn_weight = jnp.concatenate([w_ffgate, w_up], axis=1)
    blocks = (attn_weight, ffn_weight, w_out, w_down)

    def apply_in(operand, which_block):
        return rows_in(operand, blocks[which_block])

    def apply_out(operand, which_block):
        return rows_out(operand, blocks[which_block])

    inputs = feature_gather(tokens).astype(jnp.float32)
    normed1, inverse1 = norm_rows(inputs, gain_attn)
    hidden1 = normed1.astype(jnp.bfloat16)
    joint = apply_in(hidden1, 0)
    query_raw = joint[:, :query_width]
    gate_raw = joint[:, query_width : 2 * query_width]
    key_raw = joint[:, 2 * query_width : 2 * query_width + key_width]
    values = joint[:, 2 * query_width + key_width :].astype(jnp.bfloat16)
    prepare = partial(head_prepare, cosine=cosine, sine=sine)
    query = prepare(query_raw, gain_query).astype(jnp.bfloat16)
    keys = prepare(key_raw, gain_key).astype(jnp.bfloat16)
    attended, logsum = attend_forward(query, keys, values, allowed, kv_heads, head_dim)
    gate_sig = jax.nn.sigmoid(gate_raw)
    mixed = (attended * gate_sig).astype(jnp.bfloat16)
    resid = tokens.astype(jnp.float32) + feature_sum(apply_out(mixed, 2))
    resid_full = feature_gather(resid.astype(jnp.bfloat16)).astype(jnp.float32)
    normed2, inverse2 = norm_rows(resid_full, gain_ffn)
    hidden2 = normed2.astype(jnp.bfloat16)
    ffn_joint = apply_in(hidden2, 1)
    ff_gate = ffn_joint[:, :hidden_width]
    ff_up = ffn_joint[:, hidden_width:]
    sig_gate = jax.nn.sigmoid(ff_gate)
    activated = (jax.nn.silu(ff_gate) * ff_up).astype(jnp.bfloat16)
    ffn_out = feature_sum(apply_out(activated, 3))
    output = (live * (resid + ffn_out)).astype(jnp.bfloat16)
    grad_out = live * cotangent.astype(jnp.float32)
    grad_ffn_full = feature_gather(grad_out.astype(jnp.bfloat16))
    grad_act = apply_in(grad_ffn_full, 3)
    grad_ffup = (grad_act * (ff_gate * sig_gate)).astype(jnp.bfloat16)
    grad_ffgate = (grad_act * ff_up * sig_gate * (1.0 + ff_gate * (1.0 - sig_gate))).astype(
        jnp.bfloat16
    )
    grad_pair = jnp.concatenate([grad_ffgate, grad_ffup], axis=1)
    ffn_grads = weight_grads((hidden2, grad_ffn_full), (grad_pair, activated))
    grad_input2, gain_ffn_grad = norm_back(
        apply_out(grad_pair, 1), resid_full * inverse2, inverse2, gain_ffn, local
    )
    grad_resid = grad_out + grad_input2
    grad_branch_full = feature_gather(grad_resid.astype(jnp.bfloat16))
    grad_mixed = apply_in(grad_branch_full, 2)
    grad_attended = (grad_mixed * gate_sig).astype(jnp.bfloat16)
    grad_gate_raw = (grad_mixed * attended * gate_sig * (1.0 - gate_sig)).astype(jnp.bfloat16)
    grad_query, grad_keys, grad_values = attend_backward(
        query, keys, values, allowed, logsum, grad_attended, kv_heads, head_dim
    )
    unused_query, query_back = jax.vjp(prepare, query_raw, gain_query)
    grad_query_raw, grad_gain_query = query_back(grad_query)
    unused_key, key_back = jax.vjp(prepare, key_raw, gain_key)
    grad_key_raw, grad_gain_key = key_back(grad_keys)
    grad_joint = jnp.concatenate(
        [
            grad_query_raw.astype(jnp.bfloat16),
            grad_gate_raw,
            grad_key_raw.astype(jnp.bfloat16),
            grad_values,
        ],
        axis=1,
    )
    attn_grads = weight_grads((hidden1, grad_branch_full), (grad_joint, mixed))
    grad_input1, gain_attn_grad = norm_back(
        apply_out(grad_joint, 0), inputs * inverse1, inverse1, gain_attn, local
    )
    grad_tokens = grad_resid + grad_input1
    gains = lax.psum(
        (gain_attn_grad, gain_ffn_grad, grad_gain_query, grad_gain_key), ("row", "col")
    )
    second_cut = 2 * query_width
    third_cut = 2 * query_width + key_width
    fourth_cut = 2 * query_width + 2 * key_width
    return (
        output,
        grad_tokens,
        gains[0],
        gains[1],
        gains[2],
        gains[3],
        attn_grads[:, :query_width],
        attn_grads[:, query_width:second_cut],
        attn_grads[:, second_cut:third_cut],
        attn_grads[:, third_cut:fourth_cut],
        attn_grads[:, fourth_cut:],
        ffn_grads[:, :hidden_width],
        ffn_grads[:, hidden_width : 2 * hidden_width],
        ffn_grads[:, 2 * hidden_width :],
    )


def plain(mesh):
    in_specs = (
        P("row", "col"),
        P("row", "col"),
        P("row"),
        P(),
        P(),
        P(),
        P(),
        P("row", "col"),
        P("row", "col"),
        P("row", "col"),
        P("row", "col"),
        P("row", "col"),
        P("row", "col"),
        P("row", "col"),
        P("row", "col"),
    )
    out_specs = (
        P("row", "col"),
        P("row", "col"),
        P(),
        P(),
        P(),
        P(),
        P("row", "col"),
        P("row", "col"),
        P("row", "col"),
        P("row", "col"),
        P("row", "col"),
        P("row", "col"),
        P("row", "col"),
        P("row", "col"),
    )
    return jax.shard_map(body, mesh=mesh, in_specs=in_specs, out_specs=out_specs, check_vma=False)


def tie(*values):
    return lax.optimization_barrier(values)


def flip(values, axis):
    return lax.ppermute(values, axis, [(0, 1), (1, 0)])


light = pl.CostEstimate(flops=0, bytes_accessed=0, transcendentals=0)


heavy = light


class Line:
    def __init__(self):
        self.token = jnp.zeros((8, 128), jnp.float32)

    def enter(self, *values):
        *values, self.token = lax.optimization_barrier((*values, self.token))
        return values

    def run(self, work, *values):
        result = work(*self.enter(*values))
        if isinstance(result, (tuple, list)):
            return self.enter(*result)
        return self.enter(result)[0]


def pack_kernel(normed, place_ref, gain_ref, *refs):
    blocks, out_ref = refs[:4], refs[5]
    width = blocks[0].shape[1]
    place = place_ref[0]
    if normed:
        values = [block[...].astype(jnp.float32) for block in blocks]
        squares = sum(jnp.sum(v * v, axis=1, keepdims=True) for v in values)
        inverse = lax.rsqrt(squares / (4 * width) + eps_norm)
        refs[6][...] = inverse
    for index in range(4):
        columns = pl.ds(pl.multiple_of((place ^ index) * width, width), width)
        if normed:
            result = values[index] * inverse * gain_ref[:, columns]
            out_ref[:, columns] = result.astype(out_ref.dtype)
        else:
            out_ref[:, columns] = blocks[index][...]


def pack(blocks, place, gain, normed, step, target):
    count, width = blocks[0].shape
    tile = 256
    tiles = count // tile
    out_shape = [jax.ShapeDtypeStruct((2 * count, 4 * width), jnp.bfloat16)]
    out_specs = [pl.BlockSpec((tile, 4 * width), lambda i: (i + step * tiles, 0))]
    if normed:
        out_shape.append(jax.ShapeDtypeStruct((count, 1), jnp.float32))
        out_specs.append(pl.BlockSpec((tile, 1), lambda i: (i, 0)))
    aliases = {}
    if target is None:
        target = place.reshape(1)
    else:
        aliases = {6: 0}
    return pl.pallas_call(
        partial(pack_kernel, normed),
        grid=(tiles,),
        in_specs=[
            pl.BlockSpec(memory_space=pltpu.SMEM),
            pl.BlockSpec((1, 4 * width), lambda i: (0, 0)),
        ]
        + [pl.BlockSpec((tile, width), lambda i: (i, 0))] * 4
        + [pl.BlockSpec(memory_space=pl.ANY if aliases else pltpu.SMEM)],
        out_specs=out_specs,
        out_shape=out_shape,
        input_output_aliases=aliases,
        cost_estimate=light,
    )(place.reshape(1), gain.reshape(1, -1), *blocks, target)


def direct(own):
    return (flip(own, "y"), flip(own, "x"), flip(own, "core"))


def relay(own, via_y, via_x, own_core, place, gain, normed):
    half = own.shape[0] // 2
    upper = flip(via_y[:half], "x")
    lower = flip(via_x[half:], "y")
    x_core = flip(via_x, "core")
    near = pack((own, own_core, via_y, flip(via_y, "core")), place, gain, normed, 0, None)
    return (via_x, x_core, upper, lower, *near)


def diagonal(via_x, x_core, upper, lower, target, place, gain, normed):
    crossed = jnp.concatenate([upper, lower], axis=0)
    far = (via_x, x_core, crossed, flip(crossed, "core"))
    return pack(far, place, gain, normed, 1, target)[0]


def halves_kernel(count, across_ref, *refs):
    across = across_ref[0]
    keep_ref, give_ref = refs[count:]
    at = 0
    for weight_ref in refs[:count]:
        width = weight_ref.shape[1] // 2
        for target, side in ((keep_ref, across), (give_ref, 1 - across)):
            target[:, at : at + width] = weight_ref[:, pl.ds(pl.multiple_of(side * width, width), width)]
        at += width


def halves(weights, across):
    rows = weights[0].shape[0]
    width = sum(weight.shape[1] for weight in weights) // 2
    shape = jax.ShapeDtypeStruct((rows, width), jnp.bfloat16)
    whole = pl.BlockSpec(memory_space=pltpu.VMEM)
    return pl.pallas_call(
        partial(halves_kernel, len(weights)),
        in_specs=[pl.BlockSpec(memory_space=pltpu.SMEM)] + [whole] * len(weights),
        out_specs=[whole, whole],
        out_shape=[shape, shape],
        cost_estimate=light,
    )(across.reshape(1), *weights)


def weight_rows(keep, got, across):
    top = jnp.where(across == 0, keep, got)
    bottom = jnp.where(across == 0, got, keep)
    return jnp.concatenate([top, bottom], axis=0)


def weight_gather(rows):
    return lax.all_gather(rows, "z", axis=0, tiled=True)


def grad_scatter(grads):
    return lax.psum_scatter(grads, "z", scatter_dimension=0, tiled=True)


def keep_rows(summed, across):
    rows = summed.shape[0] // 2
    return lax.dynamic_slice_in_dim(summed, across * rows, rows, 0)


def give_rows(summed, across):
    return keep_rows(summed, 1 - across)


def z_flip(values, step):
    return lax.ppermute(values, "z", [(i, i ^ step) for i in range(4)])


vmem = pltpu.CompilerParams(vmem_limit_bytes=56 * 1024 * 1024)


def fold_turn(near_ref, far_ref, near_turned, far_turned):
    @pl.when(pl.program_id(0) == 0)
    def turn():
        near_turned[...] = near_ref[...].T
        far_turned[...] = far_ref[...].T


def fold_sent_kernel(
    place_ref, operand_ref, near_ref, far_ref, near_out, far_out, near_turned, far_turned
):
    fold_turn(near_ref, far_ref, near_turned, far_turned)
    for weight_ref, out_ref in ((near_turned, near_out), (far_turned, far_out)):
        out_ref[...] = product_nn(operand_ref[...], weight_ref[...]).astype(out_ref.dtype)


def fold_held_kernel(
    place_ref, operand_ref, near_ref, far_ref, near_got, far_got,
    upper_send, upper_keep, lower_send, lower_keep, near_turned, far_turned,
):
    fold_turn(near_ref, far_ref, near_turned, far_turned)
    low = upper_send.dtype
    near = product_nn(operand_ref[...], near_turned[...]) + near_got[...].astype(jnp.float32)
    far = product_nn(operand_ref[...], far_turned[...]) + far_got[...].astype(jnp.float32)
    near, far = near.astype(low), far.astype(low)
    step = pl.program_id(0)

    @pl.when(step == 0)
    def first():
        upper_send[0] = near
        upper_send[1] = far

    @pl.when(step == 1)
    def second():
        upper_keep[0] = near
        upper_keep[1] = far

    @pl.when(step >= 2)
    def third():
        lower_send[...] = far
        lower_keep[...] = near


def fold_rows(i):
    return (1 - i % 2) * 2 + i // 2


def fold_specs(tile, width, rows, column, near, far):
    return [
        pl.BlockSpec((tile, width), lambda i, p: (fold_rows(i), 0)),
        pl.BlockSpec((rows, width), lambda i, p: (p[0] ^ near, column)),
        pl.BlockSpec((rows, width), lambda i, p: (p[0] ^ far, column)),
    ]


def fold_sent(operand, weight, place, column=0):
    count, width = operand.shape
    rows, tile = weight.shape[0] // 4, count // 4
    out = pl.BlockSpec((tile, rows), lambda i, p: (fold_rows(i), 0))
    near, far = pl.pallas_call(
        fold_sent_kernel,
        grid_spec=pltpu.PrefetchScalarGridSpec(
            num_scalar_prefetch=1,
            grid=(4,),
            in_specs=fold_specs(tile, width, rows, column, 1, 3),
            out_specs=[out, out],
            scratch_shapes=[pltpu.VMEM((width, rows), jnp.bfloat16)] * 2,
        ),
        out_shape=[jax.ShapeDtypeStruct((count, rows), jnp.bfloat16)] * 2,
        compiler_params=vmem,
        cost_estimate=light,
    )(place.reshape(1), operand, weight, weight)
    return (near, far)


def fold_swap(operand, weight, place, column=0):
    return tuple(flip(v, "core") for v in fold_sent(operand, weight, place, column))


def fold_held(operand, weight, place, near_got, far_got, column=0):
    count, width = operand.shape
    rows, tile = weight.shape[0] // 4, count // 4
    got = pl.BlockSpec((tile, rows), lambda i, p: (fold_rows(i), 0))
    whole = pl.BlockSpec((2, tile, rows), lambda i, p: (0, 0, 0))
    late = pl.BlockSpec((tile, rows), lambda i, p: (jnp.where(i < 3, 1, 0), 0))
    shape = jax.ShapeDtypeStruct
    return pl.pallas_call(
        fold_held_kernel,
        grid_spec=pltpu.PrefetchScalarGridSpec(
            num_scalar_prefetch=1,
            grid=(4,),
            in_specs=fold_specs(tile, width, rows, column, 0, 2) + [got, got],
            out_specs=[whole, whole, late, late],
            scratch_shapes=[pltpu.VMEM((width, rows), jnp.bfloat16)] * 2,
        ),
        out_shape=[shape((2, tile, rows), jnp.bfloat16)] * 2
        + [shape((2 * tile, rows), jnp.bfloat16)] * 2,
        compiler_params=vmem,
        cost_estimate=light,
    )(place.reshape(1), operand, weight, weight, near_got, far_got)


def fold_cross(upper_send, upper_keep, lower_send, lower_keep):
    return (flip(upper_send, "x"), upper_keep, flip(lower_send, "y"), lower_keep)


def fold_close(upper, upper_keep, lower, lower_keep):
    low, wide = jnp.bfloat16, jnp.float32
    half = lower.shape[0] // 2
    upper_got = flip((upper_keep[1].astype(wide) + upper[1]).astype(low), "y")
    lower_got = flip((lower_keep[half:].astype(wide) + lower[half:]).astype(low), "x")
    return (
        upper_keep[0].astype(wide) + upper[0],
        upper_got,
        lower_keep[:half].astype(wide) + lower[:half],
        lower_got,
    )


def fold_end(upper_near, upper_got, lower_own, lower_got):
    return jnp.concatenate([upper_near + upper_got, lower_own + lower_got], axis=0)


def matmul_kernel(form, operand_ref, weight_ref, out_ref):
    out_ref[...] = form(operand_ref[...], weight_ref[...]).astype(out_ref.dtype)


def dot_in(operand, weight, width, column=0):
    count, depth = operand.shape
    tile = 512
    return pl.pallas_call(
        partial(matmul_kernel, product_nn),
        grid=(count // tile,),
        in_specs=[
            pl.BlockSpec((tile, depth), lambda i: (i, 0)),
            pl.BlockSpec((depth, width), lambda i: (0, column)),
        ],
        out_specs=pl.BlockSpec((tile, width), lambda i: (i, 0)),
        out_shape=jax.ShapeDtypeStruct((count, width), jnp.float32),
        compiler_params=vmem,
        cost_estimate=light,
    )(operand, weight)


def dot_grad(first, second, width=None, column=0, cost=light):
    count, rows = first.shape
    width = second.shape[1] if width is None else width
    tile = 512
    return pl.pallas_call(
        partial(matmul_kernel, product_tn),
        grid=(rows // tile,),
        in_specs=[
            pl.BlockSpec((count, tile), lambda i: (0, i)),
            pl.BlockSpec((count, width), lambda i: (0, column)),
        ],
        out_specs=pl.BlockSpec((tile, width), lambda i: (i, 0)),
        out_shape=jax.ShapeDtypeStruct((rows, width), jnp.bfloat16),
        compiler_params=vmem,
        cost_estimate=cost,
    )(first, second)


def ffn_kernel(hidden_ref, weight_ref, grad_ref, activated_ref, pair_ref):
    width = activated_ref.shape[1]
    low = jnp.bfloat16
    step = 256
    for at in range(0, width, step):
        ff_gate = product_nn(hidden_ref[...], weight_ref[:, at : at + step])
        ff_up = product_nn(hidden_ref[...], weight_ref[:, width + at : width + at + step])
        grad = grad_ref[:, at : at + step]
        sig_gate = jax.nn.sigmoid(ff_gate)
        passed = ff_gate * sig_gate
        activated_ref[:, at : at + step] = (passed * ff_up).astype(low)
        pair_ref[:, width + at : width + at + step] = (grad * passed).astype(low)
        pair_ref[:, at : at + step] = (
            grad * ff_up * sig_gate * (1.0 + ff_gate * (1.0 - sig_gate))
        ).astype(low)


def ffn(hidden, weight, grad):
    count, depth = hidden.shape
    width = weight.shape[1] // 2
    tile = 256
    return pl.pallas_call(
        ffn_kernel,
        grid=(count // tile,),
        in_specs=[
            pl.BlockSpec((tile, depth), lambda i: (i, 0)),
            pl.BlockSpec((depth, 2 * width), lambda i: (0, 0)),
            pl.BlockSpec((tile, width), lambda i: (i, 0)),
        ],
        out_specs=[
            pl.BlockSpec((tile, width), lambda i: (i, 0)),
            pl.BlockSpec((tile, 2 * width), lambda i: (i, 0)),
        ],
        out_shape=[
            jax.ShapeDtypeStruct((count, width), jnp.bfloat16),
            jax.ShapeDtypeStruct((count, 2 * width), jnp.bfloat16),
        ],
        compiler_params=vmem,
        cost_estimate=light,
    )(hidden, weight, grad)


def row_tables(segments, head_dim):
    count = segments.shape[0]
    index = jnp.arange(count, dtype=jnp.int32)
    previous = jnp.concatenate([jnp.full((1,), -1, jnp.int32), segments[:-1]])
    starts = lax.cummax(jnp.where(segments != previous, index, 0), axis=0)
    position = (index - starts).astype(jnp.float32)
    half = head_dim // 2
    freqs = jnp.power(rope_base, -(jnp.arange(half, dtype=jnp.float32) * 2.0 / head_dim))
    angle = position[:, None] * freqs[None, :]
    cosine, sine = jnp.cos(angle), jnp.sin(angle)
    return (
        jnp.concatenate([cosine, cosine], axis=1),
        jnp.concatenate([-sine, sine], axis=1),
        jnp.where(segments > 0, starts, index)[None, :],
    )


def product_nt(first, second):
    return lax.dot_general(
        first, second, (((1,), (1,)), ((), ())), preferred_element_type=jnp.float32
    )


def product_tn(first, second):
    return lax.dot_general(
        first, second, (((0,), (0,)), ((), ())), preferred_element_type=jnp.float32
    )


def product_nn(first, second):
    return lax.dot_general(
        first, second, (((1,), (0,)), ((), ())), preferred_element_type=jnp.float32
    )


def prepare_tile(raw, gain, cosine, sine):
    inverse = lax.rsqrt(jnp.mean(raw * raw, axis=1, keepdims=True) + eps_norm)
    normed = raw * inverse * gain
    turned = pltpu.roll(normed, raw.shape[1] // 2, 1)
    return (normed * cosine + turned * sine).astype(jnp.bfloat16)


def prepare_back(raw, gain, cosine, sine, grad):
    inverse = lax.rsqrt(jnp.mean(raw * raw, axis=1, keepdims=True) + eps_norm)
    unit = raw * inverse
    grad_normed = grad * cosine + pltpu.roll(grad * sine, raw.shape[1] // 2, 1)
    scaled = grad_normed * gain
    grad_raw = inverse * (scaled - unit * jnp.mean(scaled * unit, axis=1, keepdims=True))
    return (grad_raw.astype(jnp.bfloat16), jnp.sum(grad_normed * unit, axis=0, keepdims=True))


def allowed_tile(first_ref, start, tile, reach):
    rows = lax.broadcasted_iota(jnp.int32, (reach, tile), 0)
    columns = lax.broadcasted_iota(jnp.int32, (reach, tile), 1) + start
    return (rows >= first_ref[0, :, pl.ds(start, tile)]) & (rows <= columns)


def attend_kernel(
    heads, tile, joint_ref, cos_ref, sin_ref, first_ref, gain_query_ref, gain_key_ref,
    mixed_ref, attended_ref, query_ref, key_ref, logsum_ref,
):
    count, head_dim = cos_ref.shape
    scale = head_dim ** (-0.5)
    low = jnp.bfloat16
    key_at = 2 * heads * head_dim
    tiles = count // tile
    for part in range(tiles):
        rows = pl.ds(part * tile, tile)
        key_ref[rows, :] = prepare_tile(
            joint_ref[rows, key_at : key_at + head_dim],
            gain_key_ref[...],
            cos_ref[rows, :],
            sin_ref[rows, :],
        )
    for head in range(heads):
        columns = slice(head * head_dim, (head + 1) * head_dim)
        gates = slice((heads + head) * head_dim, (heads + head + 1) * head_dim)
        for part in range(tiles):
            rows = pl.ds(part * tile, tile)
            reach = (part + 1) * tile
            query = prepare_tile(
                joint_ref[rows, columns], gain_query_ref[...], cos_ref[rows, :], sin_ref[rows, :]
            )
            query_ref[rows, columns] = query
            scores = product_nt(key_ref[:reach, :], query) * scale
            scores = jnp.where(allowed_tile(first_ref, part * tile, tile, reach), scores, -1e30)
            peak = jnp.max(scores, axis=0, keepdims=True)
            weights = jnp.exp(scores - peak)
            total = jnp.sum(weights, axis=0, keepdims=True)
            probs = (weights * (1.0 / total)).astype(low)
            logsum_ref[0, head : head + 1, rows] = peak + jnp.log(total)
            values = joint_ref[:reach, key_at + head_dim : key_at + 2 * head_dim].astype(low)
            attended = product_tn(values, probs).T
            attended_ref[rows, columns] = attended
            gate = joint_ref[rows, gates]
            mixed_ref[rows, columns] = (attended * jax.nn.sigmoid(gate)).astype(low)


def attend_back_kernel(
    heads, tile, joint_ref, cos_ref, sin_ref, first_ref, gain_query_ref, gain_key_ref,
    attended_ref, query_ref, key_ref, logsum_ref, grad_mixed_ref,
    grad_joint_ref, grad_gain_ref, grad_key_acc, grad_value_acc,
):
    count, head_dim = cos_ref.shape
    scale = head_dim ** (-0.5)
    low = jnp.bfloat16
    key_at = 2 * heads * head_dim
    value_at = key_at + head_dim
    tiles = count // tile
    gain_query = jnp.zeros((1, head_dim), jnp.float32)
    gain_key = jnp.zeros((1, head_dim), jnp.float32)
    for head in range(heads):
        columns = slice(head * head_dim, (head + 1) * head_dim)
        gates = slice((heads + head) * head_dim, (heads + head + 1) * head_dim)
        for part in reversed(range(tiles)):
            rows = pl.ds(part * tile, tile)
            reach = (part + 1) * tile
            fresh = head == 0 and part == tiles - 1
            gate = jax.nn.sigmoid(joint_ref[rows, gates])
            grad_mixed = grad_mixed_ref[rows, columns]
            gated = grad_mixed * gate
            grad_attended = gated.astype(low)
            grad_joint_ref[rows, gates] = (gated * attended_ref[rows, columns] * (1.0 - gate)).astype(
                low
            )
            query = query_ref[rows, columns]
            keys = key_ref[:reach, :]
            values = joint_ref[:reach, value_at : value_at + head_dim].astype(low)
            scores = product_nt(keys, query) * scale
            logsum = logsum_ref[0, head : head + 1, rows]
            probs = jnp.where(
                allowed_tile(first_ref, part * tile, tile, reach), jnp.exp(scores - logsum), 0.0
            )
            grad_value = product_nn(probs.astype(low), grad_attended)
            grad_probs = product_nt(values, grad_attended)
            delta = jnp.sum(probs * grad_probs, axis=0, keepdims=True)
            grad_scores = (probs * (grad_probs - delta)).astype(low)
            grad_key = product_nn(grad_scores, query)
            if fresh:
                grad_value_acc[...] = grad_value
                grad_key_acc[...] = grad_key
            else:
                grad_value_acc[:reach, :] += grad_value
                grad_key_acc[:reach, :] += grad_key
            grad_query = product_tn(keys, grad_scores).T * scale
            grad_raw, gain_part = prepare_back(
                joint_ref[rows, columns],
                gain_query_ref[...],
                cos_ref[rows, :],
                sin_ref[rows, :],
                grad_query,
            )
            grad_joint_ref[rows, columns] = grad_raw
            gain_query = gain_query + gain_part
    for part in range(tiles):
        rows = pl.ds(part * tile, tile)
        grad_raw, gain_part = prepare_back(
            joint_ref[rows, key_at:value_at],
            gain_key_ref[...],
            cos_ref[rows, :],
            sin_ref[rows, :],
            grad_key_acc[rows, :] * scale,
        )
        grad_joint_ref[rows, key_at:value_at] = grad_raw
        gain_key = gain_key + gain_part
        grad_joint_ref[rows, value_at : value_at + head_dim] = grad_value_acc[rows, :].astype(low)
    both = jnp.concatenate([gain_query, gain_key], axis=0)

    @pl.when(pl.program_id(0) == 0)
    def begin():
        grad_gain_ref[...] = both

    @pl.when(pl.program_id(0) > 0)
    def add():
        grad_gain_ref[...] += both


def attend_specs(count, head_dim, heads, joint_width):
    wide = lambda width: pl.BlockSpec((count, width), lambda s: (s, 0))
    row = pl.BlockSpec((1, head_dim), lambda s: (0, 0))
    lead = [
        wide(joint_width),
        wide(head_dim),
        wide(head_dim),
        pl.BlockSpec((1, 1, count), lambda s: (s, 0, 0)),
        row,
        row,
    ]
    kept = [
        wide(heads * head_dim),
        wide(heads * head_dim),
        wide(head_dim),
        pl.BlockSpec((1, heads, count), lambda s: (s, 0, 0)),
    ]
    return (lead, kept, wide)


def attend_fwd(joint, cosine, sine, first, gain_query, gain_key, heads, count):
    head_dim = cosine.shape[1]
    lead, kept, wide = attend_specs(count, head_dim, heads, joint.shape[1])
    total = joint.shape[0]
    shape = jax.ShapeDtypeStruct
    return pl.pallas_call(
        partial(attend_kernel, heads, 256),
        grid=(total // count,),
        in_specs=lead,
        out_specs=[wide(heads * head_dim)] + kept,
        out_shape=[
            shape((total, heads * head_dim), jnp.bfloat16),
            shape((total, heads * head_dim), jnp.float32),
            shape((total, heads * head_dim), jnp.bfloat16),
            shape((total, head_dim), jnp.bfloat16),
            shape((total // count, heads, count), jnp.float32),
        ],
        compiler_params=pltpu.CompilerParams(vmem_limit_bytes=40 * 1024 * 1024),
        cost_estimate=light,
    )(joint, cosine, sine, first, gain_query.reshape(1, -1), gain_key.reshape(1, -1))


def attend_bwd(joint, cosine, sine, first, gain_query, gain_key, kept_values, grad_mixed, count):
    head_dim = cosine.shape[1]
    heads = grad_mixed.shape[1] // head_dim
    lead, kept, wide = attend_specs(count, head_dim, heads, joint.shape[1])
    total = joint.shape[0]
    shape = jax.ShapeDtypeStruct
    return pl.pallas_call(
        partial(attend_back_kernel, heads, 256),
        grid=(total // count,),
        in_specs=lead + kept + [wide(heads * head_dim)],
        out_specs=[wide(joint.shape[1]), pl.BlockSpec((2, head_dim), lambda s: (0, 0))],
        out_shape=[shape(joint.shape, jnp.bfloat16), shape((2, head_dim), jnp.float32)],
        scratch_shapes=[
            pltpu.VMEM((count, head_dim), jnp.float32),
            pltpu.VMEM((count, head_dim), jnp.float32),
        ],
        compiler_params=pltpu.CompilerParams(vmem_limit_bytes=48 * 1024 * 1024),
        cost_estimate=light,
    )(
        joint, cosine, sine, first, gain_query.reshape(1, -1), gain_key.reshape(1, -1),
        *kept_values, grad_mixed,
    )


def fast_body(
    tokens,
    cotangent,
    segment_ids,
    gain_attn,
    gain_ffn,
    gain_query,
    gain_key,
    w_query,
    w_gate,
    w_key,
    w_value,
    w_out,
    w_ffgate,
    w_up,
    w_down,
):
    across = lax.axis_index("x")
    place = lax.axis_index("y") * 2 + lax.axis_index("core")
    count, local = tokens.shape
    width = gain_attn.shape[0]
    head_dim = gain_query.shape[0]
    low = jnp.bfloat16
    query_width = w_query.shape[1] // 2
    key_width = w_key.shape[1] // 2
    heads = query_width // head_dim
    hidden_width = w_ffgate.shape[1] // 2
    live = (segment_ids > 0).astype(jnp.float32)[:, None]
    offset = place * local
    gain_attn_own = lax.dynamic_slice_in_dim(gain_attn, offset, local, 0)
    gain_ffn_own = lax.dynamic_slice_in_dim(gain_ffn, offset, local, 0)

    line = Line()
    half = count // 2
    joint_width = 2 * query_width + 2 * key_width
    rows_of = partial(weight_rows, across=across)

    first_columns = [w_query, w_gate, w_key, w_value, w_out]

    def open_first(tokens, *weights):
        upper_y = flip(tokens[:half], "y")
        keep, give = halves(weights, across)
        got = flip(give, "x")
        return (rows_of(keep, got), upper_y)

    first_rows, upper_y = line.run(open_first, tokens, *first_columns)
    first_weight = weight_gather(first_rows)
    grad_out = live * cotangent.astype(jnp.float32)
    grad_out_low = grad_out.astype(low)

    def open_second(tokens, segment_ids, upper_y, w_ffgate, w_up, w_down):
        lower_y = flip(tokens[half:], "y")
        via_x = flip(tokens, "x")
        own_core = flip(tokens, "core")
        other = flip(segment_ids, "x")
        via_y = jnp.concatenate([upper_y, lower_y], axis=0)
        return (via_y, via_x, own_core, other, *halves([w_ffgate, w_up], across), *halves([w_down], across))

    via_y, via_x, own_core, segment_other, keep_pair, give_pair, keep_down, give_down = line.run(
        open_second, tokens, segment_ids, upper_y, w_ffgate, w_up, w_down
    )

    def open_third(tokens, via_y, via_x, own_core, keep_down, give_down):
        steps = relay(tokens, via_y, via_x, own_core, place, gain_attn, True)
        return (rows_of(keep_down, flip(give_down, "x")), *steps)

    down_rows, *steps, target, inverse1 = line.run(
        open_third, tokens, via_y, via_x, own_core, keep_down, give_down
    )
    down_weight = weight_gather(down_rows)

    def open_fourth(grad_out_low, segment_ids, segment_other, *steps):
        via_out = direct(grad_out_low)
        hidden1 = diagonal(*steps, place, gain_attn, True)
        segments = jnp.stack([segment_ids, segment_other])
        cosine, sine, first = jax.vmap(partial(row_tables, head_dim=head_dim))(segments)
        cosine = cosine.reshape(2 * count, head_dim)
        sine = sine.reshape(2 * count, head_dim)
        return (hidden1, cosine, sine, first, *via_out)

    hidden1, cosine, sine, first, *via_out = line.run(
        open_fourth, grad_out_low, segment_ids, segment_other, *steps, target
    )
    steps = line.run(
        lambda *v: relay(*v, place, gain_ffn, False), grad_out_low, *via_out
    )
    out_column = joint_width // query_width

    def attend(hidden1, first_weight, keep_pair, give_pair):
        got_pair = flip(give_pair, "x")
        joint = dot_in(hidden1, first_weight, joint_width)
        mixed, *kept = attend_fwd(
            joint, cosine, sine, first, gain_query, gain_key, heads, count
        )
        return (rows_of(keep_pair, got_pair), joint, mixed, *kept)

    pair_rows, joint, mixed, *kept = line.run(attend, hidden1, first_weight, keep_pair, give_pair)
    pair_weight = weight_gather(pair_rows)
    near_got, far_got = line.run(
        lambda m, w: fold_swap(m, w, place, out_column), mixed, first_weight
    )
    sums = line.run(
        lambda *v: fold_held(v[0], v[1], place, *v[2:], out_column),
        mixed, first_weight, near_got, far_got,
    )

    def cross_out(*values):
        return (*fold_cross(*values[:4]), diagonal(*values[4:], place, gain_ffn, False))

    *sums, grad_out_full = line.run(cross_out, *sums, *steps)
    ends = line.run(fold_close, *sums)

    def residual(values, *ends):
        total = values.astype(jnp.float32) + fold_end(*ends)
        return (total, total.astype(low))

    resid, resid_low = line.run(residual, tokens, *ends)

    def start_resid(resid_low, grad_out_full, down_weight):
        return (*direct(resid_low), dot_in(grad_out_full, down_weight, hidden_width))

    *via_resid, grad_act = line.run(start_resid, resid_low, grad_out_full, down_weight)
    *steps, target, inverse2 = line.run(
        lambda *v: relay(*v, place, gain_ffn, True), resid_low, *via_resid
    )
    hidden2 = line.run(lambda *v: diagonal(*v, place, gain_ffn, True), *steps, target)
    activated, grad_pair = line.run(ffn, hidden2, pair_weight, grad_act)

    gate_grad = line.run(lambda h, g: dot_grad(h, g, hidden_width), hidden2, grad_pair)
    gate_sum = grad_scatter(gate_grad)

    def sent_pair(hidden2, grad_pair, pair_weight):
        return (
            *fold_swap(grad_pair, pair_weight, place),
            dot_grad(hidden2, grad_pair, hidden_width, 1),
        )

    near_got, far_got, up_grad = line.run(sent_pair, hidden2, grad_pair, pair_weight)
    up_sum = grad_scatter(up_grad)
    sums = line.run(
        lambda *v: fold_held(v[0], v[1], place, *v[2:]), grad_pair, pair_weight, near_got, far_got
    )

    def cross_pair(grad_out_full, activated, down_weight, *sums):
        return (
            *fold_cross(*sums),
            dot_grad(grad_out_full, activated),
            *fold_sent(activated, down_weight, place),
        )

    *sums, down_grad, near_ffn, far_ffn = line.run(
        cross_pair, grad_out_full, activated, down_weight, *sums
    )
    down_sum = grad_scatter(down_grad)

    def close_pair(near_ffn, far_ffn, *sums):
        return (*fold_close(*sums), flip(near_ffn, "core"), flip(far_ffn, "core"))

    *ends, near_got, far_got = line.run(close_pair, near_ffn, far_ffn, *sums)

    def partial_dots(grad_own, values, inverse, gain_own):
        dots = jnp.sum(grad_own * gain_own * values.astype(jnp.float32) * inverse, axis=1)
        dots = dots.reshape(-1, 128)
        dots = dots + flip(dots, "core")
        return dots + flip(dots, "y")

    def norm_back(grad_own, values, inverse, gain_own, dots, extra):
        unit = values.astype(jnp.float32) * inverse
        dots = dots.reshape(-1, 1) / width
        grad_input = inverse * (grad_own * gain_own - unit * dots) + extra
        return (grad_input, grad_input.astype(low))

    def gain_part(grad_own, values, inverse):
        return jnp.sum(grad_own * (values.astype(jnp.float32) * inverse), axis=0).reshape(-1, 128)

    def back_dots(values, inverse, gain_own, *ends):
        grad_own = fold_end(*ends)
        return (
            grad_own,
            partial_dots(grad_own, values, inverse, gain_own),
            gain_part(grad_own, values, inverse),
        )

    grad_hidden2, dots, gain_ffn_grad = line.run(
        back_dots, resid_low, inverse2, gain_ffn_own, *ends
    )
    grad_resid, grad_branch = line.run(
        norm_back, grad_hidden2, resid_low, inverse2, gain_ffn_own, dots, grad_out
    )

    def start_branch(grad_branch, activated, down_weight, near_got, far_got):
        return (
            *direct(grad_branch),
            *fold_held(activated, down_weight, place, near_got, far_got),
        )

    via_y, via_x, own_core, *sums_ffn = line.run(
        start_branch, grad_branch, activated, down_weight, near_got, far_got
    )
    gate_sum, = line.enter(gate_sum)
    steps = line.run(
        lambda *v: relay(*v, place, gain_ffn, False), grad_branch, via_y, via_x, own_core
    )

    def mix_back(gate_sum, first_weight, *steps):
        got = flip(give_rows(gate_sum, across), "x")
        grad_branch_full = diagonal(*steps, place, gain_ffn, False)
        grad_mixed = dot_in(grad_branch_full, first_weight, query_width, out_column)
        return (got, grad_branch_full, grad_mixed)

    got_gate, grad_branch_full, grad_mixed = line.run(mix_back, gate_sum, first_weight, *steps)
    up_sum, = line.enter(up_sum)

    def attend_back(joint, grad_mixed, grad_branch_full, mixed, *sums):
        grad_joint, head_gains = attend_bwd(
            joint, cosine, sine, first, gain_query, gain_key, kept, grad_mixed, count
        )
        out_grad = dot_grad(grad_branch_full, mixed, None, 0, heavy)
        return (grad_joint, head_gains, out_grad, *fold_cross(*sums))

    grad_joint, head_gains, out_grad, *sums_ffn = line.run(
        attend_back, joint, grad_mixed, grad_branch_full, mixed, *sums_ffn
    )
    out_sum = grad_scatter(out_grad)

    down_sum, = line.enter(down_sum)

    def sent_attn(hidden1, grad_joint, first_weight, up_sum, down_sum):
        return (
            *fold_swap(grad_joint, first_weight, place),
            flip(give_rows(up_sum, across), "x"),
            flip(give_rows(down_sum, across), "x"),
            dot_grad(hidden1, grad_joint, None, 0, heavy),
        )

    near_got, far_got, got_up, got_down, attn_grads = line.run(
        sent_attn, hidden1, grad_joint, first_weight, up_sum, down_sum
    )
    attn_sum = grad_scatter(attn_grads)
    out_sum, = line.enter(out_sum)

    def held_attn(grad_joint, first_weight, near_got, far_got, gain_ffn_grad, head_gains, *sums):
        early = jnp.concatenate([gain_ffn_grad, head_gains], axis=0)
        early = early + flip(early, "x")
        return (
            early,
            *fold_held(grad_joint, first_weight, place, near_got, far_got),
            *fold_close(*sums),
        )

    early, *sums = line.run(
        held_attn, grad_joint, first_weight, near_got, far_got, gain_ffn_grad, head_gains, *sums_ffn
    )
    sums, ends_ffn = sums[:4], sums[4:]

    def join(rows, got, low_cut, high_cut):
        keep = keep_rows(rows, across)[:, low_cut:high_cut]
        got = got[:, low_cut:high_cut]
        first, second = jnp.where(across == 0, keep, got), jnp.where(across == 0, got, keep)
        return jnp.concatenate([first, second], axis=1).astype(jnp.float32)

    def join_all(rows, got):
        return join(rows, got, 0, rows.shape[1])

    def cross_attn(early, resid, gate_sum, got_gate, *values):
        sums = fold_cross(*values[:4])
        output = (live * (resid + fold_end(*values[4:]))).astype(low)
        return (early + z_flip(early, 1), output, join_all(gate_sum, got_gate), *sums)

    early, output, ffgate_grad, *sums = line.run(
        cross_attn, early, resid, gate_sum, got_gate, *sums, *ends_ffn
    )

    def close_attn(early, up_sum, got_up, *sums):
        return (early + z_flip(early, 2), join_all(up_sum, got_up), *fold_close(*sums))

    early, up_grad, *ends = line.run(close_attn, early, up_sum, got_up, *sums)

    def last_dots(tokens, inverse1, out_sum, *ends):
        grad_own = fold_end(*ends)
        late = gain_part(grad_own, tokens, inverse1)
        return (
            flip(give_rows(out_sum, across), "x"),
            grad_own,
            partial_dots(grad_own, tokens, inverse1, gain_attn_own),
            late,
        )

    got_out, grad_hidden1, dots, late = line.run(last_dots, tokens, inverse1, out_sum, *ends)

    def last_norm(grad_hidden1, tokens, inverse1, dots, grad_resid, late):
        grad_tokens, unused = norm_back(
            grad_hidden1, tokens, inverse1, gain_attn_own, dots, grad_resid
        )
        return (grad_tokens, late + flip(late, "x"))

    grad_tokens, late = line.run(
        last_norm, grad_hidden1, tokens, inverse1, dots, grad_resid, late
    )
    attn_sum, = line.enter(attn_sum)

    def last_out(late, attn_sum, out_sum, got_out, down_sum, got_down):
        got_attn = flip(give_rows(attn_sum, across), "x")
        late = late + z_flip(late, 1)
        return (
            got_attn,
            late + z_flip(late, 2),
            join_all(out_sum, got_out),
            join_all(down_sum, got_down),
        )

    got_attn, late, out_part, down_part = line.run(
        last_out, late, attn_sum, out_sum, got_out, down_sum, got_down
    )
    blocks = local // 128

    def last_spot(late, early):
        own = jnp.stack([late, early[:blocks]])
        spot = lax.dynamic_update_slice_in_dim(
            jnp.zeros((2, width // 128, 128), jnp.float32), own, offset // 128, 1
        ).reshape(-1, 128)
        spot = jnp.concatenate([spot, early[blocks:]], axis=0)
        spot = spot + flip(spot, "core")
        return spot + flip(spot, "y")

    cuts = (
        0,
        query_width,
        2 * query_width,
        2 * query_width + key_width,
        2 * query_width + 2 * key_width,
    )

    def last_parts(attn_sum, got_attn, late, early):
        return (
            last_spot(late, early),
            *[join(attn_sum, got_attn, cuts[i], cuts[i + 1]) for i in range(4)],
        )

    spot, *attn_parts = line.run(last_parts, attn_sum, got_attn, late, early)
    lines = width // 128
    return (
        output,
        grad_tokens,
        spot[:lines].reshape(width),
        spot[lines : 2 * lines].reshape(width),
        spot[2 * lines] + line.token[0],
        spot[2 * lines + 1],
        *attn_parts,
        out_part,
        ffgate_grad,
        up_grad,
        down_part,
    )


def solution(mesh):
    rows, columns = mesh.devices.shape

    def run(*args):
        head_dim = args[5].shape[0]
        query_width, key_width = args[7].shape[1], args[9].shape[1]
        one_key_head = key_width == 2 * columns * head_dim and query_width % key_width == 0
        if not (rows == 8 and columns == 4 and one_key_head):
            return plain(mesh)(*args)
        names = ("z", "x", "y", "core")
        inner = Mesh(mesh.devices.reshape(4, 2, 2, 2), names)
        block = P(("z", "x"), ("y", "core"))
        whole = P()
        in_specs = (block, block, P(("z", "x"))) + (whole,) * 4 + (block,) * 8
        out_specs = (block, block) + (whole,) * 4 + (block,) * 8
        return jax.shard_map(
            fast_body, mesh=inner, in_specs=in_specs, out_specs=out_specs, check_vma=False
        )(*args)

    return run
```

```python
from functools import partial

import jax
import jax.numpy as jnp
from jax import lax
from jax.experimental import pallas as pl
from jax.experimental.pallas import tpu as pltpu
from jax.sharding import Mesh
from jax.sharding import PartitionSpec as P

eps_norm = 1e-06
rope_base = 1000000.0


def norm_rows(values, gain):
    inverse = lax.rsqrt(jnp.mean(values * values, axis=-1, keepdims=True) + eps_norm)
    return (values * inverse * gain, inverse)


def rope_tables(segments, head_dim):
    count = segments.shape[0]
    index = jnp.arange(count, dtype=jnp.int32)
    previous = jnp.concatenate([jnp.full((1,), -1, jnp.int32), segments[:-1]])
    starts = lax.cummax(jnp.where(segments != previous, index, 0), axis=0)
    position = (index - starts).astype(jnp.float32)
    half = head_dim // 2
    freqs = jnp.power(rope_base, -(jnp.arange(half, dtype=jnp.float32) * 2.0 / head_dim))
    angle = position[:, None] * freqs[None, :]
    angle = jnp.concatenate([angle, angle], axis=1)
    return (jnp.cos(angle), jnp.sin(angle))


def attend_mask(segments):
    count = segments.shape[0]
    index = jnp.arange(count, dtype=jnp.int32)
    earlier = index[None, :] < index[:, None]
    same = (segments[None, :] == segments[:, None]) & (segments[None, :] > 0)
    return (index[None, :] == index[:, None]) | earlier & same


def head_prepare(raw, gain, cosine, sine):
    count = raw.shape[0]
    head_dim = gain.shape[0]
    heads = raw.reshape(count, -1, head_dim)
    inverse = lax.rsqrt(jnp.mean(heads * heads, axis=-1, keepdims=True) + eps_norm)
    normed = heads * inverse * gain
    half = head_dim // 2
    turned = jnp.concatenate([-normed[..., half:], normed[..., :half]], axis=-1)
    return (normed * cosine[:, None, :] + turned * sine[:, None, :]).reshape(count, -1)


def feature_gather(values):
    return lax.all_gather(values, "col", axis=1, tiled=True)


def feature_sum(values):
    return lax.psum_scatter(
        values.astype(jnp.bfloat16), "col", scatter_dimension=1, tiled=True
    ).astype(jnp.float32)


def rows_in(operand, weight):
    return jnp.dot(
        operand,
        lax.all_gather(weight, "row", axis=0, tiled=True),
        preferred_element_type=jnp.float32,
    )


def rows_out(operand, weight):
    return lax.dot_general(
        operand,
        lax.all_gather(weight, "row", axis=0, tiled=True),
        (((1,), (1,)), ((), ())),
        preferred_element_type=jnp.float32,
    )


def weight_grads(firsts, seconds):
    blocks = []
    for first, second in zip(firsts, seconds):
        blocks.append(
            lax.dot_general(
                first, second, (((0,), (0,)), ((), ())), preferred_element_type=jnp.float32
            )
        )
    return lax.psum_scatter(
        jnp.concatenate(blocks, axis=1).astype(jnp.bfloat16), "row", scatter_dimension=0, tiled=True
    ).astype(jnp.float32)


def norm_back(partial_grad, unit, inverse, gain, local):
    offset = lax.axis_index("col") * local
    width = unit.shape[1]
    unit_own = lax.dynamic_slice_in_dim(unit, offset, local, 1)
    grad_own = feature_sum(partial_grad)
    gain_own = lax.dynamic_slice_in_dim(gain, offset, local, 0)
    scaled = grad_own * gain_own
    dots = lax.psum(jnp.sum(scaled * unit_own, axis=1), "col")[:, None] / width
    grad_input = inverse * (scaled - unit_own * dots)
    gain_grad = lax.dynamic_update_slice_in_dim(
        jnp.zeros((width,), jnp.float32), jnp.sum(grad_own * unit_own, axis=0), offset, 0
    )
    return (grad_input, gain_grad)


def attend_scores(query, keys, allowed, kv_heads, head_dim):
    count = query.shape[0]
    grouped = query.reshape(count, kv_heads, -1, head_dim)
    keyed = keys.reshape(count, kv_heads, head_dim)
    scores = jnp.einsum(
        "qgrd,kgd->grqk", grouped, keyed, preferred_element_type=jnp.float32
    ) * head_dim ** (-0.5)
    return (jnp.where(allowed, scores, -1e30), grouped, keyed)


def attend_forward(query, keys, values, allowed, kv_heads, head_dim):
    count = query.shape[0]
    scores, grouped, keyed = attend_scores(query, keys, allowed, kv_heads, head_dim)
    peak = jnp.max(scores, axis=-1, keepdims=True)
    weights = jnp.exp(scores - peak)
    total = jnp.sum(weights, axis=-1, keepdims=True)
    probs = (weights / total).astype(jnp.bfloat16)
    valued = values.reshape(count, kv_heads, head_dim)
    attended = jnp.einsum("grqk,kgd->qgrd", probs, valued, preferred_element_type=jnp.float32)
    return (attended.reshape(count, -1), peak + jnp.log(total))


def attend_backward(query, keys, values, allowed, logsum, grad_attended, kv_heads, head_dim):
    count = query.shape[0]
    scores, grouped, keyed = attend_scores(query, keys, allowed, kv_heads, head_dim)
    probs_exact = jnp.exp(scores - logsum)
    probs = probs_exact.astype(jnp.bfloat16)
    valued = values.reshape(count, kv_heads, head_dim)
    grad_grouped = grad_attended.reshape(count, kv_heads, -1, head_dim)
    grad_values = jnp.einsum(
        "grqk,qgrd->kgd", probs, grad_grouped, preferred_element_type=jnp.float32
    )
    grad_probs = jnp.einsum(
        "qgrd,kgd->grqk", grad_grouped, valued, preferred_element_type=jnp.float32
    )
    delta = jnp.sum(probs_exact * grad_probs, axis=-1, keepdims=True)
    grad_scores = (probs_exact * (grad_probs - delta)).astype(jnp.bfloat16)
    grad_query = jnp.einsum(
        "grqk,kgd->qgrd", grad_scores, keyed, preferred_element_type=jnp.float32
    ) * head_dim ** (-0.5)
    grad_keys = jnp.einsum(
        "grqk,qgrd->kgd", grad_scores, grouped, preferred_element_type=jnp.float32
    ) * head_dim ** (-0.5)
    return (
        grad_query.reshape(count, -1),
        grad_keys.reshape(count, -1),
        grad_values.reshape(count, -1).astype(jnp.bfloat16),
    )


def body(
    tokens,
    cotangent,
    segment_ids,
    gain_attn,
    gain_ffn,
    gain_query,
    gain_key,
    w_query,
    w_gate,
    w_key,
    w_value,
    w_out,
    w_ffgate,
    w_up,
    w_down,
):
    local = tokens.shape[1]
    head_dim = gain_query.shape[0]
    query_width = w_query.shape[1]
    key_width = w_key.shape[1]
    kv_heads = key_width // head_dim
    hidden_width = w_ffgate.shape[1]
    live = (segment_ids > 0).astype(jnp.float32)[:, None]
    cosine, sine = rope_tables(segment_ids, head_dim)
    allowed = attend_mask(segment_ids)
    attn_weight = jnp.concatenate([w_query, w_gate, w_key, w_value], axis=1)
    ffn_weight = jnp.concatenate([w_ffgate, w_up], axis=1)
    blocks = (attn_weight, ffn_weight, w_out, w_down)

    def apply_in(operand, which_block):
        return rows_in(operand, blocks[which_block])

    def apply_out(operand, which_block):
        return rows_out(operand, blocks[which_block])

    inputs = feature_gather(tokens).astype(jnp.float32)
    normed1, inverse1 = norm_rows(inputs, gain_attn)
    hidden1 = normed1.astype(jnp.bfloat16)
    joint = apply_in(hidden1, 0)
    query_raw = joint[:, :query_width]
    gate_raw = joint[:, query_width : 2 * query_width]
    key_raw = joint[:, 2 * query_width : 2 * query_width + key_width]
    values = joint[:, 2 * query_width + key_width :].astype(jnp.bfloat16)
    prepare = partial(head_prepare, cosine=cosine, sine=sine)
    query = prepare(query_raw, gain_query).astype(jnp.bfloat16)
    keys = prepare(key_raw, gain_key).astype(jnp.bfloat16)
    attended, logsum = attend_forward(query, keys, values, allowed, kv_heads, head_dim)
    gate_sig = jax.nn.sigmoid(gate_raw)
    mixed = (attended * gate_sig).astype(jnp.bfloat16)
    resid = tokens.astype(jnp.float32) + feature_sum(apply_out(mixed, 2))
    resid_full = feature_gather(resid.astype(jnp.bfloat16)).astype(jnp.float32)
    normed2, inverse2 = norm_rows(resid_full, gain_ffn)
    hidden2 = normed2.astype(jnp.bfloat16)
    ffn_joint = apply_in(hidden2, 1)
    ff_gate = ffn_joint[:, :hidden_width]
    ff_up = ffn_joint[:, hidden_width:]
    sig_gate = jax.nn.sigmoid(ff_gate)
    activated = (jax.nn.silu(ff_gate) * ff_up).astype(jnp.bfloat16)
    ffn_out = feature_sum(apply_out(activated, 3))
    output = (live * (resid + ffn_out)).astype(jnp.bfloat16)
    grad_out = live * cotangent.astype(jnp.float32)
    grad_ffn_full = feature_gather(grad_out.astype(jnp.bfloat16))
    grad_act = apply_in(grad_ffn_full, 3)
    grad_ffup = (grad_act * (ff_gate * sig_gate)).astype(jnp.bfloat16)
    grad_ffgate = (grad_act * ff_up * sig_gate * (1.0 + ff_gate * (1.0 - sig_gate))).astype(
        jnp.bfloat16
    )
    grad_pair = jnp.concatenate([grad_ffgate, grad_ffup], axis=1)
    ffn_grads = weight_grads((hidden2, grad_ffn_full), (grad_pair, activated))
    grad_input2, gain_ffn_grad = norm_back(
        apply_out(grad_pair, 1), resid_full * inverse2, inverse2, gain_ffn, local
    )
    grad_resid = grad_out + grad_input2
    grad_branch_full = feature_gather(grad_resid.astype(jnp.bfloat16))
    grad_mixed = apply_in(grad_branch_full, 2)
    grad_attended = (grad_mixed * gate_sig).astype(jnp.bfloat16)
    grad_gate_raw = (grad_mixed * attended * gate_sig * (1.0 - gate_sig)).astype(jnp.bfloat16)
    grad_query, grad_keys, grad_values = attend_backward(
        query, keys, values, allowed, logsum, grad_attended, kv_heads, head_dim
    )
    unused_query, query_back = jax.vjp(prepare, query_raw, gain_query)
    grad_query_raw, grad_gain_query = query_back(grad_query)
    unused_key, key_back = jax.vjp(prepare, key_raw, gain_key)
    grad_key_raw, grad_gain_key = key_back(grad_keys)
    grad_joint = jnp.concatenate(
        [
            grad_query_raw.astype(jnp.bfloat16),
            grad_gate_raw,
            grad_key_raw.astype(jnp.bfloat16),
            grad_values,
        ],
        axis=1,
    )
    attn_grads = weight_grads((hidden1, grad_branch_full), (grad_joint, mixed))
    grad_input1, gain_attn_grad = norm_back(
        apply_out(grad_joint, 0), inputs * inverse1, inverse1, gain_attn, local
    )
    grad_tokens = grad_resid + grad_input1
    gains = lax.psum(
        (gain_attn_grad, gain_ffn_grad, grad_gain_query, grad_gain_key), ("row", "col")
    )
    second_cut = 2 * query_width
    third_cut = 2 * query_width + key_width
    fourth_cut = 2 * query_width + 2 * key_width
    return (
        output,
        grad_tokens,
        gains[0],
        gains[1],
        gains[2],
        gains[3],
        attn_grads[:, :query_width],
        attn_grads[:, query_width:second_cut],
        attn_grads[:, second_cut:third_cut],
        attn_grads[:, third_cut:fourth_cut],
        attn_grads[:, fourth_cut:],
        ffn_grads[:, :hidden_width],
        ffn_grads[:, hidden_width : 2 * hidden_width],
        ffn_grads[:, 2 * hidden_width :],
    )


def plain(mesh):
    in_specs = (
        P("row", "col"),
        P("row", "col"),
        P("row"),
        P(),
        P(),
        P(),
        P(),
        P("row", "col"),
        P("row", "col"),
        P("row", "col"),
        P("row", "col"),
        P("row", "col"),
        P("row", "col"),
        P("row", "col"),
        P("row", "col"),
    )
    out_specs = (
        P("row", "col"),
        P("row", "col"),
        P(),
        P(),
        P(),
        P(),
        P("row", "col"),
        P("row", "col"),
        P("row", "col"),
        P("row", "col"),
        P("row", "col"),
        P("row", "col"),
        P("row", "col"),
        P("row", "col"),
    )
    return jax.shard_map(body, mesh=mesh, in_specs=in_specs, out_specs=out_specs, check_vma=False)


def tie(*values):
    return lax.optimization_barrier(values)


def flip(values, axis):
    return lax.ppermute(values, axis, [(0, 1), (1, 0)])


light = pl.CostEstimate(flops=0, bytes_accessed=0, transcendentals=0)


heavy = light


class Line:
    def __init__(self):
        self.token = jnp.zeros((8, 128), jnp.float32)

    def enter(self, *values):
        *values, self.token = lax.optimization_barrier((*values, self.token))
        return values

    def run(self, work, *values):
        result = work(*self.enter(*values))
        if isinstance(result, (tuple, list)):
            return self.enter(*result)
        return self.enter(result)[0]


def pack_kernel(normed, place_ref, gain_ref, *refs):
    blocks, out_ref = refs[:4], refs[5]
    width = blocks[0].shape[1]
    place = place_ref[0]
    if normed:
        values = [block[...].astype(jnp.float32) for block in blocks]
        squares = sum(jnp.sum(v * v, axis=1, keepdims=True) for v in values)
        inverse = lax.rsqrt(squares / (4 * width) + eps_norm)
        refs[6][...] = inverse
    for index in range(4):
        columns = pl.ds(pl.multiple_of((place ^ index) * width, width), width)
        if normed:
            result = values[index] * inverse * gain_ref[:, columns]
            out_ref[:, columns] = result.astype(out_ref.dtype)
        else:
            out_ref[:, columns] = blocks[index][...]


def pack(blocks, place, gain, normed, step, target):
    count, width = blocks[0].shape
    tile = 256
    tiles = count // tile
    out_shape = [jax.ShapeDtypeStruct((2 * count, 4 * width), jnp.bfloat16)]
    out_specs = [pl.BlockSpec((tile, 4 * width), lambda i: (i + step * tiles, 0))]
    if normed:
        out_shape.append(jax.ShapeDtypeStruct((count, 1), jnp.float32))
        out_specs.append(pl.BlockSpec((tile, 1), lambda i: (i, 0)))
    aliases = {}
    if target is None:
        target = place.reshape(1)
    else:
        aliases = {6: 0}
    return pl.pallas_call(
        partial(pack_kernel, normed),
        grid=(tiles,),
        in_specs=[
            pl.BlockSpec(memory_space=pltpu.SMEM),
            pl.BlockSpec((1, 4 * width), lambda i: (0, 0)),
        ]
        + [pl.BlockSpec((tile, width), lambda i: (i, 0))] * 4
        + [pl.BlockSpec(memory_space=pl.ANY if aliases else pltpu.SMEM)],
        out_specs=out_specs,
        out_shape=out_shape,
        input_output_aliases=aliases,
        cost_estimate=light,
    )(place.reshape(1), gain.reshape(1, -1), *blocks, target)


def direct(own):
    return (flip(own, "y"), flip(own, "x"), flip(own, "core"))


def relay_flips(via_y, via_x):
    half = via_y.shape[0] // 2
    upper = flip(via_y[:half], "x")
    lower = flip(via_x[half:], "y")
    return (flip(via_y, "core"), via_x, flip(via_x, "core"), upper, lower)


def relay(own, via_y, via_x, own_core, place, gain, normed):
    y_core, *steps = relay_flips(via_y, via_x)
    return (*steps, *pack((own, own_core, via_y, y_core), place, gain, normed, 0, None))


def diagonal(via_x, x_core, upper, lower, target, place, gain, normed):
    crossed = jnp.concatenate([upper, lower], axis=0)
    far = (via_x, x_core, crossed, flip(crossed, "core"))
    return pack(far, place, gain, normed, 1, target)[0]


def halves_kernel(count, across_ref, *refs):
    across = across_ref[0]
    keep_ref, give_ref = refs[count:]
    at = 0
    for weight_ref in refs[:count]:
        width = weight_ref.shape[1] // 2
        for target, side in ((keep_ref, across), (give_ref, 1 - across)):
            target[:, at : at + width] = weight_ref[:, pl.ds(pl.multiple_of(side * width, width), width)]
        at += width


def halves(weights, across):
    rows = weights[0].shape[0]
    width = sum(weight.shape[1] for weight in weights) // 2
    shape = jax.ShapeDtypeStruct((rows, width), jnp.bfloat16)
    whole = pl.BlockSpec(memory_space=pltpu.VMEM)
    return pl.pallas_call(
        partial(halves_kernel, len(weights)),
        in_specs=[pl.BlockSpec(memory_space=pltpu.SMEM)] + [whole] * len(weights),
        out_specs=[whole, whole],
        out_shape=[shape, shape],
        cost_estimate=light,
    )(across.reshape(1), *weights)


def weight_rows(keep, got, across):
    top = jnp.where(across == 0, keep, got)
    bottom = jnp.where(across == 0, got, keep)
    return jnp.concatenate([top, bottom], axis=0)


def weight_gather(rows):
    return lax.all_gather(rows, "z", axis=0, tiled=True)


def grad_scatter(grads):
    return lax.psum_scatter(grads, "z", scatter_dimension=0, tiled=True)


def keep_rows(summed, across):
    rows = summed.shape[0] // 2
    return lax.dynamic_slice_in_dim(summed, across * rows, rows, 0)


def give_rows(summed, across):
    return keep_rows(summed, 1 - across)


def z_flip(values, step):
    return lax.ppermute(values, "z", [(i, i ^ step) for i in range(4)])


vmem = pltpu.CompilerParams(vmem_limit_bytes=56 * 1024 * 1024)


def fold_turn(near_ref, far_ref, turned):
    rows = near_ref.shape[0]

    @pl.when(pl.program_id(0) == 0)
    def turn():
        turned[:, :rows] = near_ref[...].T
        turned[:, rows:] = far_ref[...].T


def fold_sent_kernel(place_ref, operand_ref, near_ref, far_ref, near_out, far_out, turned):
    fold_turn(near_ref, far_ref, turned)
    rows = near_out.shape[1]
    both = product_nn(operand_ref[...], turned[...]).astype(near_out.dtype)
    near_out[...] = both[:, :rows]
    far_out[...] = both[:, rows:]


def fold_held_kernel(
    place_ref, operand_ref, near_ref, far_ref, near_got, far_got,
    upper_send, upper_keep, lower_send, lower_keep, turned,
):
    fold_turn(near_ref, far_ref, turned)
    low = upper_send.dtype
    rows = near_got.shape[1]
    both = product_nn(operand_ref[...], turned[...])
    near = (both[:, :rows] + near_got[...].astype(jnp.float32)).astype(low)
    far = (both[:, rows:] + far_got[...].astype(jnp.float32)).astype(low)
    step = pl.program_id(0)

    @pl.when(step == 0)
    def first():
        upper_send[0] = near
        upper_send[1] = far

    @pl.when(step == 1)
    def second():
        upper_keep[0] = near
        upper_keep[1] = far

    @pl.when(step >= 2)
    def third():
        lower_send[...] = far
        lower_keep[...] = near


def fold_rows(i):
    return (1 - i % 2) * 2 + i // 2


def fold_specs(tile, width, rows, column, near, far):
    return [
        pl.BlockSpec((tile, width), lambda i, p: (fold_rows(i), 0)),
        pl.BlockSpec((rows, width), lambda i, p: (p[0] ^ near, column)),
        pl.BlockSpec((rows, width), lambda i, p: (p[0] ^ far, column)),
    ]


def fold_sent(operand, weight, place, column=0):
    count, width = operand.shape
    rows, tile = weight.shape[0] // 4, count // 4
    out = pl.BlockSpec((tile, rows), lambda i, p: (fold_rows(i), 0))
    near, far = pl.pallas_call(
        fold_sent_kernel,
        grid_spec=pltpu.PrefetchScalarGridSpec(
            num_scalar_prefetch=1,
            grid=(4,),
            in_specs=fold_specs(tile, width, rows, column, 1, 3),
            out_specs=[out, out],
            scratch_shapes=[pltpu.VMEM((width, 2 * rows), jnp.bfloat16)],
        ),
        out_shape=[jax.ShapeDtypeStruct((count, rows), jnp.bfloat16)] * 2,
        compiler_params=vmem,
        cost_estimate=light,
    )(place.reshape(1), operand, weight, weight)
    return (near, far)


def fold_swap(operand, weight, place, column=0):
    return tuple(flip(v, "core") for v in fold_sent(operand, weight, place, column))


def fold_held(operand, weight, place, near_got, far_got, column=0):
    count, width = operand.shape
    rows, tile = weight.shape[0] // 4, count // 4
    got = pl.BlockSpec((tile, rows), lambda i, p: (fold_rows(i), 0))
    whole = pl.BlockSpec((2, tile, rows), lambda i, p: (0, 0, 0))
    late = pl.BlockSpec((tile, rows), lambda i, p: (jnp.where(i < 3, 1, 0), 0))
    shape = jax.ShapeDtypeStruct
    return pl.pallas_call(
        fold_held_kernel,
        grid_spec=pltpu.PrefetchScalarGridSpec(
            num_scalar_prefetch=1,
            grid=(4,),
            in_specs=fold_specs(tile, width, rows, column, 0, 2) + [got, got],
            out_specs=[whole, whole, late, late],
            scratch_shapes=[pltpu.VMEM((width, 2 * rows), jnp.bfloat16)],
        ),
        out_shape=[shape((2, tile, rows), jnp.bfloat16)] * 2
        + [shape((2 * tile, rows), jnp.bfloat16)] * 2,
        compiler_params=vmem,
        cost_estimate=light,
    )(place.reshape(1), operand, weight, weight, near_got, far_got)


def fold_cross(upper_send, upper_keep, lower_send, lower_keep):
    return (flip(upper_send, "x"), upper_keep, flip(lower_send, "y"), lower_keep)


def fold_close_kernel(
    upper_ref, upper_keep, own_ref, own_keep, other_ref, other_keep,
    upper_near, upper_far, lower_own, lower_other,
):
    wide = lambda ref: ref[...].astype(jnp.float32)
    total = wide(upper_ref) + wide(upper_keep)
    upper_near[...] = total[0]
    upper_far[...] = total[1].astype(upper_far.dtype)
    lower_own[...] = wide(own_ref) + wide(own_keep)
    lower_other[...] = (wide(other_ref) + wide(other_keep)).astype(lower_other.dtype)


def fold_close(upper, upper_keep, lower, lower_keep):
    count, rows = upper.shape[1:]
    tile = count // 2
    pair = pl.BlockSpec((2, tile, rows), lambda i: (0, i, 0))
    own = pl.BlockSpec((tile, rows), lambda i: (i, 0))
    other = pl.BlockSpec((tile, rows), lambda i: (i + 2, 0))
    shapes = [jax.ShapeDtypeStruct((count, rows), kind) for kind in (jnp.float32, jnp.bfloat16)]
    upper_near, upper_far, lower_own, lower_other = pl.pallas_call(
        fold_close_kernel,
        grid=(2,),
        in_specs=[pair, pair, own, own, other, other],
        out_specs=[own] * 4,
        out_shape=shapes * 2,
        cost_estimate=light,
    )(upper, upper_keep, lower, lower_keep, lower, lower_keep)
    return (upper_near, flip(upper_far, "y"), lower_own, flip(lower_other, "x"))


def fold_end(upper_near, upper_got, lower_own, lower_got):
    return jnp.concatenate([upper_near + upper_got, lower_own + lower_got], axis=0)


def matmul_kernel(form, operand_ref, weight_ref, out_ref):
    out_ref[...] = form(operand_ref[...], weight_ref[...]).astype(out_ref.dtype)


def dot_in(operand, weight, width, column=0):
    count, depth = operand.shape
    tile = 512
    return pl.pallas_call(
        partial(matmul_kernel, product_nn),
        grid=(count // tile,),
        in_specs=[
            pl.BlockSpec((tile, depth), lambda i: (i, 0)),
            pl.BlockSpec((depth, width), lambda i: (0, column)),
        ],
        out_specs=pl.BlockSpec((tile, width), lambda i: (i, 0)),
        out_shape=jax.ShapeDtypeStruct((count, width), jnp.float32),
        compiler_params=vmem,
        cost_estimate=light,
    )(operand, weight)


def dot_grad(first, second, width=None, column=0, cost=light):
    count, rows = first.shape
    width = second.shape[1] if width is None else width
    tile = 512
    return pl.pallas_call(
        partial(matmul_kernel, product_tn),
        grid=(rows // tile,),
        in_specs=[
            pl.BlockSpec((count, tile), lambda i: (0, i)),
            pl.BlockSpec((count, width), lambda i: (0, column)),
        ],
        out_specs=pl.BlockSpec((tile, width), lambda i: (i, 0)),
        out_shape=jax.ShapeDtypeStruct((rows, width), jnp.bfloat16),
        compiler_params=vmem,
        cost_estimate=cost,
    )(first, second)


def ffn_kernel(hidden_ref, weight_ref, grad_ref, activated_ref, pair_ref):
    width = activated_ref.shape[1]
    low = jnp.bfloat16
    step = 256
    for at in range(0, width, step):
        ff_gate = product_nn(hidden_ref[...], weight_ref[:, at : at + step])
        ff_up = product_nn(hidden_ref[...], weight_ref[:, width + at : width + at + step])
        grad = grad_ref[:, at : at + step]
        sig_gate = jax.nn.sigmoid(ff_gate)
        passed = ff_gate * sig_gate
        activated_ref[:, at : at + step] = (passed * ff_up).astype(low)
        pair_ref[:, width + at : width + at + step] = (grad * passed).astype(low)
        pair_ref[:, at : at + step] = (
            grad * ff_up * sig_gate * (1.0 + ff_gate * (1.0 - sig_gate))
        ).astype(low)


def ffn(hidden, weight, grad):
    count, depth = hidden.shape
    width = weight.shape[1] // 2
    tile = 256
    return pl.pallas_call(
        ffn_kernel,
        grid=(count // tile,),
        in_specs=[
            pl.BlockSpec((tile, depth), lambda i: (i, 0)),
            pl.BlockSpec((depth, 2 * width), lambda i: (0, 0)),
            pl.BlockSpec((tile, width), lambda i: (i, 0)),
        ],
        out_specs=[
            pl.BlockSpec((tile, width), lambda i: (i, 0)),
            pl.BlockSpec((tile, 2 * width), lambda i: (i, 0)),
        ],
        out_shape=[
            jax.ShapeDtypeStruct((count, width), jnp.bfloat16),
            jax.ShapeDtypeStruct((count, 2 * width), jnp.bfloat16),
        ],
        compiler_params=vmem,
        cost_estimate=light,
    )(hidden, weight, grad)


def row_tables(segments, head_dim):
    count = segments.shape[0]
    index = jnp.arange(count, dtype=jnp.int32)
    previous = jnp.concatenate([jnp.full((1,), -1, jnp.int32), segments[:-1]])
    starts = lax.cummax(jnp.where(segments != previous, index, 0), axis=0)
    position = (index - starts).astype(jnp.float32)
    half = head_dim // 2
    freqs = jnp.power(rope_base, -(jnp.arange(half, dtype=jnp.float32) * 2.0 / head_dim))
    angle = position[:, None] * freqs[None, :]
    cosine, sine = jnp.cos(angle), jnp.sin(angle)
    return (
        jnp.concatenate([cosine, cosine], axis=1),
        jnp.concatenate([-sine, sine], axis=1),
        jnp.where(segments > 0, starts, index)[None, :],
    )


def product_nt(first, second):
    return lax.dot_general(
        first, second, (((1,), (1,)), ((), ())), preferred_element_type=jnp.float32
    )


def product_tn(first, second):
    return lax.dot_general(
        first, second, (((0,), (0,)), ((), ())), preferred_element_type=jnp.float32
    )


def product_nn(first, second):
    return lax.dot_general(
        first, second, (((1,), (0,)), ((), ())), preferred_element_type=jnp.float32
    )


def prepare_tile(raw, gain, cosine, sine):
    inverse = lax.rsqrt(jnp.mean(raw * raw, axis=1, keepdims=True) + eps_norm)
    normed = raw * inverse * gain
    turned = pltpu.roll(normed, raw.shape[1] // 2, 1)
    return (normed * cosine + turned * sine).astype(jnp.bfloat16)


def prepare_back(raw, gain, cosine, sine, grad):
    inverse = lax.rsqrt(jnp.mean(raw * raw, axis=1, keepdims=True) + eps_norm)
    unit = raw * inverse
    grad_normed = grad * cosine + pltpu.roll(grad * sine, raw.shape[1] // 2, 1)
    scaled = grad_normed * gain
    grad_raw = inverse * (scaled - unit * jnp.mean(scaled * unit, axis=1, keepdims=True))
    return (grad_raw.astype(jnp.bfloat16), jnp.sum(grad_normed * unit, axis=0, keepdims=True))


def allowed_tile(first_ref, start, tile, reach):
    rows = lax.broadcasted_iota(jnp.int32, (reach, tile), 0)
    columns = lax.broadcasted_iota(jnp.int32, (reach, tile), 1) + start
    return (rows >= first_ref[0, :, pl.ds(start, tile)]) & (rows <= columns)


def attend_kernel(
    heads, tile, joint_ref, cos_ref, sin_ref, first_ref, gain_query_ref, gain_key_ref,
    mixed_ref, attended_ref, query_ref, key_ref, logsum_ref,
):
    count, head_dim = cos_ref.shape
    scale = head_dim ** (-0.5)
    low = jnp.bfloat16
    key_at = 2 * heads * head_dim
    tiles = count // tile
    for part in range(tiles):
        rows = pl.ds(part * tile, tile)
        key_ref[rows, :] = prepare_tile(
            joint_ref[rows, key_at : key_at + head_dim],
            gain_key_ref[...],
            cos_ref[rows, :],
            sin_ref[rows, :],
        )
    for head in range(heads):
        columns = slice(head * head_dim, (head + 1) * head_dim)
        gates = slice((heads + head) * head_dim, (heads + head + 1) * head_dim)
        for part in range(tiles):
            rows = pl.ds(part * tile, tile)
            reach = (part + 1) * tile
            query = prepare_tile(
                joint_ref[rows, columns], gain_query_ref[...], cos_ref[rows, :], sin_ref[rows, :]
            )
            query_ref[rows, columns] = query
            scores = product_nt(key_ref[:reach, :], query) * scale
            scores = jnp.where(allowed_tile(first_ref, part * tile, tile, reach), scores, -1e30)
            peak = jnp.max(scores, axis=0, keepdims=True)
            weights = jnp.exp(scores - peak)
            total = jnp.sum(weights, axis=0, keepdims=True)
            probs = (weights * (1.0 / total)).astype(low)
            logsum_ref[0, head : head + 1, rows] = peak + jnp.log(total)
            values = joint_ref[:reach, key_at + head_dim : key_at + 2 * head_dim].astype(low)
            attended = product_tn(values, probs).T
            attended_ref[rows, columns] = attended
            gate = joint_ref[rows, gates]
            mixed_ref[rows, columns] = (attended * jax.nn.sigmoid(gate)).astype(low)


def attend_back_kernel(
    heads, tile, joint_ref, cos_ref, sin_ref, first_ref, gain_query_ref, gain_key_ref,
    attended_ref, query_ref, key_ref, logsum_ref, grad_mixed_ref,
    grad_joint_ref, grad_gain_ref, grad_key_acc, grad_value_acc,
):
    count, head_dim = cos_ref.shape
    scale = head_dim ** (-0.5)
    low = jnp.bfloat16
    key_at = 2 * heads * head_dim
    value_at = key_at + head_dim
    tiles = count // tile
    gain_query = jnp.zeros((1, head_dim), jnp.float32)
    gain_key = jnp.zeros((1, head_dim), jnp.float32)
    for head in range(heads):
        columns = slice(head * head_dim, (head + 1) * head_dim)
        gates = slice((heads + head) * head_dim, (heads + head + 1) * head_dim)
        for part in reversed(range(tiles)):
            rows = pl.ds(part * tile, tile)
            reach = (part + 1) * tile
            fresh = head == 0 and part == tiles - 1
            gate = jax.nn.sigmoid(joint_ref[rows, gates])
            grad_mixed = grad_mixed_ref[rows, columns]
            gated = grad_mixed * gate
            grad_attended = gated.astype(low)
            grad_joint_ref[rows, gates] = (gated * attended_ref[rows, columns] * (1.0 - gate)).astype(
                low
            )
            query = query_ref[rows, columns]
            keys = key_ref[:reach, :]
            values = joint_ref[:reach, value_at : value_at + head_dim].astype(low)
            scores = product_nt(keys, query) * scale
            logsum = logsum_ref[0, head : head + 1, rows]
            probs = jnp.where(
                allowed_tile(first_ref, part * tile, tile, reach), jnp.exp(scores - logsum), 0.0
            )
            grad_value = product_nn(probs.astype(low), grad_attended)
            grad_probs = product_nt(values, grad_attended)
            delta = jnp.sum(probs * grad_probs, axis=0, keepdims=True)
            grad_scores = (probs * (grad_probs - delta)).astype(low)
            grad_key = product_nn(grad_scores, query)
            if fresh:
                grad_value_acc[...] = grad_value
                grad_key_acc[...] = grad_key
            else:
                grad_value_acc[:reach, :] += grad_value
                grad_key_acc[:reach, :] += grad_key
            grad_query = product_tn(keys, grad_scores).T * scale
            grad_raw, gain_part = prepare_back(
                joint_ref[rows, columns],
                gain_query_ref[...],
                cos_ref[rows, :],
                sin_ref[rows, :],
                grad_query,
            )
            grad_joint_ref[rows, columns] = grad_raw
            gain_query = gain_query + gain_part
    for part in range(tiles):
        rows = pl.ds(part * tile, tile)
        grad_raw, gain_part = prepare_back(
            joint_ref[rows, key_at:value_at],
            gain_key_ref[...],
            cos_ref[rows, :],
            sin_ref[rows, :],
            grad_key_acc[rows, :] * scale,
        )
        grad_joint_ref[rows, key_at:value_at] = grad_raw
        gain_key = gain_key + gain_part
        grad_joint_ref[rows, value_at : value_at + head_dim] = grad_value_acc[rows, :].astype(low)
    both = jnp.concatenate([gain_query, gain_key], axis=0)

    @pl.when(pl.program_id(0) == 0)
    def begin():
        grad_gain_ref[...] = both

    @pl.when(pl.program_id(0) > 0)
    def add():
        grad_gain_ref[...] += both


def attend_specs(count, head_dim, heads, joint_width):
    wide = lambda width: pl.BlockSpec((count, width), lambda s: (s, 0))
    row = pl.BlockSpec((1, head_dim), lambda s: (0, 0))
    lead = [
        wide(joint_width),
        wide(head_dim),
        wide(head_dim),
        pl.BlockSpec((1, 1, count), lambda s: (s, 0, 0)),
        row,
        row,
    ]
    kept = [
        wide(heads * head_dim),
        wide(heads * head_dim),
        wide(head_dim),
        pl.BlockSpec((1, heads, count), lambda s: (s, 0, 0)),
    ]
    return (lead, kept, wide)


def attend_fwd(joint, cosine, sine, first, gain_query, gain_key, heads, count):
    head_dim = cosine.shape[1]
    lead, kept, wide = attend_specs(count, head_dim, heads, joint.shape[1])
    total = joint.shape[0]
    shape = jax.ShapeDtypeStruct
    return pl.pallas_call(
        partial(attend_kernel, heads, 256),
        grid=(total // count,),
        in_specs=lead,
        out_specs=[wide(heads * head_dim)] + kept,
        out_shape=[
            shape((total, heads * head_dim), jnp.bfloat16),
            shape((total, heads * head_dim), jnp.float32),
            shape((total, heads * head_dim), jnp.bfloat16),
            shape((total, head_dim), jnp.bfloat16),
            shape((total // count, heads, count), jnp.float32),
        ],
        compiler_params=pltpu.CompilerParams(vmem_limit_bytes=40 * 1024 * 1024),
        cost_estimate=light,
    )(joint, cosine, sine, first, gain_query.reshape(1, -1), gain_key.reshape(1, -1))


def attend_bwd(joint, cosine, sine, first, gain_query, gain_key, kept_values, grad_mixed, count):
    head_dim = cosine.shape[1]
    heads = grad_mixed.shape[1] // head_dim
    lead, kept, wide = attend_specs(count, head_dim, heads, joint.shape[1])
    total = joint.shape[0]
    shape = jax.ShapeDtypeStruct
    return pl.pallas_call(
        partial(attend_back_kernel, heads, 256),
        grid=(total // count,),
        in_specs=lead + kept + [wide(heads * head_dim)],
        out_specs=[wide(joint.shape[1]), pl.BlockSpec((2, head_dim), lambda s: (0, 0))],
        out_shape=[shape(joint.shape, jnp.bfloat16), shape((2, head_dim), jnp.float32)],
        scratch_shapes=[
            pltpu.VMEM((count, head_dim), jnp.float32),
            pltpu.VMEM((count, head_dim), jnp.float32),
        ],
        compiler_params=pltpu.CompilerParams(vmem_limit_bytes=48 * 1024 * 1024),
        cost_estimate=light,
    )(
        joint, cosine, sine, first, gain_query.reshape(1, -1), gain_key.reshape(1, -1),
        *kept_values, grad_mixed,
    )


def fast_body(
    tokens,
    cotangent,
    segment_ids,
    gain_attn,
    gain_ffn,
    gain_query,
    gain_key,
    w_query,
    w_gate,
    w_key,
    w_value,
    w_out,
    w_ffgate,
    w_up,
    w_down,
):
    across = lax.axis_index("x")
    place = lax.axis_index("y") * 2 + lax.axis_index("core")
    count, local = tokens.shape
    width = gain_attn.shape[0]
    head_dim = gain_query.shape[0]
    low = jnp.bfloat16
    query_width = w_query.shape[1] // 2
    key_width = w_key.shape[1] // 2
    heads = query_width // head_dim
    hidden_width = w_ffgate.shape[1] // 2
    live = (segment_ids > 0).astype(jnp.float32)[:, None]
    offset = place * local
    gain_attn_own = lax.dynamic_slice_in_dim(gain_attn, offset, local, 0)
    gain_ffn_own = lax.dynamic_slice_in_dim(gain_ffn, offset, local, 0)

    line = Line()
    half = count // 2
    joint_width = 2 * query_width + 2 * key_width
    rows_of = partial(weight_rows, across=across)

    first_columns = [w_query, w_gate, w_key, w_value, w_out]

    def open_first(tokens, *weights):
        upper_y = flip(tokens[:half], "y")
        keep, give = halves(weights, across)
        got = flip(give, "x")
        return (rows_of(keep, got), upper_y)

    first_rows, upper_y = line.run(open_first, tokens, *first_columns)
    first_weight = weight_gather(first_rows)
    grad_out = live * cotangent.astype(jnp.float32)
    grad_out_low = grad_out.astype(low)

    def open_second(tokens, segment_ids, upper_y, w_ffgate, w_up, w_down):
        lower_y = flip(tokens[half:], "y")
        via_x = flip(tokens, "x")
        own_core = flip(tokens, "core")
        other = flip(segment_ids, "x")
        via_y = jnp.concatenate([upper_y, lower_y], axis=0)
        return (via_y, via_x, own_core, other, *halves([w_ffgate, w_up], across), *halves([w_down], across))

    via_y, via_x, own_core, segment_other, keep_pair, give_pair, keep_down, give_down = line.run(
        open_second, tokens, segment_ids, upper_y, w_ffgate, w_up, w_down
    )

    def open_third(tokens, via_y, via_x, own_core, keep_down, give_down):
        steps = relay(tokens, via_y, via_x, own_core, place, gain_attn, True)
        return (rows_of(keep_down, flip(give_down, "x")), *steps)

    down_rows, *steps, target, inverse1 = line.run(
        open_third, tokens, via_y, via_x, own_core, keep_down, give_down
    )
    down_weight = weight_gather(down_rows)

    def open_fourth(grad_out_low, segment_ids, segment_other, *steps):
        via_out = direct(grad_out_low)
        hidden1 = diagonal(*steps, place, gain_attn, True)
        segments = jnp.stack([segment_ids, segment_other])
        cosine, sine, first = jax.vmap(partial(row_tables, head_dim=head_dim))(segments)
        cosine = cosine.reshape(2 * count, head_dim)
        sine = sine.reshape(2 * count, head_dim)
        return (hidden1, cosine, sine, first, *via_out)

    hidden1, cosine, sine, first, *via_out = line.run(
        open_fourth, grad_out_low, segment_ids, segment_other, *steps, target
    )
    out_column = joint_width // query_width

    def attend(hidden1, first_weight, keep_pair, give_pair, via_y, via_x):
        steps = relay_flips(via_y, via_x)
        got_pair = flip(give_pair, "x")
        joint = dot_in(hidden1, first_weight, joint_width)
        mixed, *kept = attend_fwd(
            joint, cosine, sine, first, gain_query, gain_key, heads, count
        )
        return (rows_of(keep_pair, got_pair), joint, mixed, *kept, *steps)

    out_y, out_x, out_core = via_out
    pair_rows, joint, mixed, *rest = line.run(
        attend, hidden1, first_weight, keep_pair, give_pair, out_y, out_x
    )
    kept, steps = rest[:4], rest[4:]
    pair_weight = weight_gather(pair_rows)
    near_got, far_got = line.run(
        lambda m, w: fold_swap(m, w, place, out_column), mixed, first_weight
    )
    sums = line.run(
        lambda *v: fold_held(v[0], v[1], place, *v[2:], out_column),
        mixed, first_weight, near_got, far_got,
    )

    def cross_out(grad_out_low, own_core, via_y, y_core, via_x, x_core, upper, lower, *sums):
        crossing = fold_cross(*sums)
        near = (grad_out_low, own_core, via_y, y_core)
        target = pack(near, place, gain_ffn, False, 0, None)[0]
        return (
            *crossing,
            diagonal(via_x, x_core, upper, lower, target, place, gain_ffn, False),
        )

    *sums, grad_out_full = line.run(cross_out, grad_out_low, out_core, out_y, *steps, *sums)
    ends = line.run(fold_close, *sums)

    def residual(values, *ends):
        total = values.astype(jnp.float32) + fold_end(*ends)
        return (total, total.astype(low))

    resid, resid_low = line.run(residual, tokens, *ends)

    def start_resid(resid_low, grad_out_full, down_weight):
        return (*direct(resid_low), dot_in(grad_out_full, down_weight, hidden_width))

    *via_resid, grad_act = line.run(start_resid, resid_low, grad_out_full, down_weight)
    *steps, target, inverse2 = line.run(
        lambda *v: relay(*v, place, gain_ffn, True), resid_low, *via_resid
    )
    hidden2 = line.run(lambda *v: diagonal(*v, place, gain_ffn, True), *steps, target)
    activated, grad_pair = line.run(ffn, hidden2, pair_weight, grad_act)


    def sent_pair(hidden2, grad_pair, pair_weight):
        return (
            *fold_swap(grad_pair, pair_weight, place),
            dot_grad(hidden2, grad_pair, hidden_width),
        )

    near_got, far_got, gate_grad = line.run(sent_pair, hidden2, grad_pair, pair_weight)
    gate_sum = grad_scatter(gate_grad)
    sums = line.run(
        lambda *v: fold_held(v[0], v[1], place, *v[2:]), grad_pair, pair_weight, near_got, far_got
    )

    def cross_pair(hidden2, grad_pair, activated, down_weight, *sums):
        return (
            *fold_cross(*sums),
            dot_grad(hidden2, grad_pair, hidden_width, 1),
            *fold_sent(activated, down_weight, place),
        )

    *sums, up_grad, near_ffn, far_ffn = line.run(
        cross_pair, hidden2, grad_pair, activated, down_weight, *sums
    )
    up_sum = grad_scatter(up_grad)

    def close_pair(near_ffn, far_ffn, *sums):
        return (*fold_close(*sums), flip(near_ffn, "core"), flip(far_ffn, "core"))

    *ends, near_got, far_got = line.run(close_pair, near_ffn, far_ffn, *sums)

    def partial_dots(grad_own, values, inverse, gain_own):
        dots = jnp.sum(grad_own * gain_own * values.astype(jnp.float32) * inverse, axis=1)
        dots = dots.reshape(-1, 128)
        dots = dots + flip(dots, "core")
        return dots + flip(dots, "y")

    def norm_back(grad_own, values, inverse, gain_own, dots, extra):
        unit = values.astype(jnp.float32) * inverse
        dots = dots.reshape(-1, 1) / width
        grad_input = inverse * (grad_own * gain_own - unit * dots) + extra
        return (grad_input, grad_input.astype(low))

    def gain_part(grad_own, values, inverse):
        return jnp.sum(grad_own * (values.astype(jnp.float32) * inverse), axis=0).reshape(-1, 128)

    def back_dots(values, inverse, gain_own, *ends):
        grad_own = fold_end(*ends)
        return (
            grad_own,
            partial_dots(grad_own, values, inverse, gain_own),
            gain_part(grad_own, values, inverse),
        )

    grad_hidden2, dots, gain_ffn_grad = line.run(
        back_dots, resid_low, inverse2, gain_ffn_own, *ends
    )
    grad_resid, grad_branch = line.run(
        norm_back, grad_hidden2, resid_low, inverse2, gain_ffn_own, dots, grad_out
    )

    def start_branch(grad_branch, grad_out_full, activated, down_weight, near_got, far_got):
        return (
            *direct(grad_branch),
            dot_grad(grad_out_full, activated),
            *fold_held(activated, down_weight, place, near_got, far_got),
        )

    via_y, via_x, own_core, down_grad, *sums_ffn = line.run(
        start_branch, grad_branch, grad_out_full, activated, down_weight, near_got, far_got
    )
    down_sum = grad_scatter(down_grad)
    gate_sum, = line.enter(gate_sum)
    steps = line.run(
        lambda *v: relay(*v, place, gain_ffn, False), grad_branch, via_y, via_x, own_core
    )

    def mix_back(gate_sum, first_weight, *steps):
        got_gate = flip(give_rows(gate_sum, across), "x")
        grad_branch_full = diagonal(*steps, place, gain_ffn, False)
        return (
            got_gate,
            grad_branch_full,
            dot_in(grad_branch_full, first_weight, query_width, out_column),
        )

    got_gate, grad_branch_full, grad_mixed = line.run(mix_back, gate_sum, first_weight, *steps)
    up_sum, = line.enter(up_sum)

    def attend_back(joint, grad_mixed, *sums):
        grad_joint, head_gains = attend_bwd(
            joint, cosine, sine, first, gain_query, gain_key, kept, grad_mixed, count
        )
        return (grad_joint, head_gains, *fold_cross(*sums))

    grad_joint, head_gains, *sums_ffn = line.run(attend_back, joint, grad_mixed, *sums_ffn)

    def sent_attn(hidden1, grad_joint, first_weight, up_sum):
        return (
            *fold_swap(grad_joint, first_weight, place),
            dot_grad(hidden1, grad_joint),
            flip(give_rows(up_sum, across), "x"),
        )

    near_got, far_got, attn_grads, got_up = line.run(
        sent_attn, hidden1, grad_joint, first_weight, up_sum
    )
    attn_sum = grad_scatter(attn_grads)
    down_sum, = line.enter(down_sum)

    def held_attn(grad_joint, first_weight, near_got, far_got, gain_ffn_grad, head_gains, *sums):
        early = jnp.concatenate([gain_ffn_grad, head_gains], axis=0)
        early = early + flip(early, "x")
        return (
            early,
            *fold_held(grad_joint, first_weight, place, near_got, far_got),
            *fold_close(*sums),
        )

    early, *sums = line.run(
        held_attn, grad_joint, first_weight, near_got, far_got, gain_ffn_grad, head_gains, *sums_ffn
    )
    sums, ends_ffn = sums[:4], sums[4:]

    def join(rows, got, low_cut, high_cut):
        keep = keep_rows(rows, across)[:, low_cut:high_cut]
        got = got[:, low_cut:high_cut]
        first, second = jnp.where(across == 0, keep, got), jnp.where(across == 0, got, keep)
        return jnp.concatenate([first, second], axis=1).astype(jnp.float32)

    def join_all(rows, got):
        return join(rows, got, 0, rows.shape[1])

    def cross_attn(
        grad_branch_full, mixed, early, resid, gate_sum, got_gate, *values
    ):
        sums = fold_cross(*values[:4])
        output = (live * (resid + fold_end(*values[4:]))).astype(low)
        return (
            early + z_flip(early, 1),
            output,
            join_all(gate_sum, got_gate),
            dot_grad(grad_branch_full, mixed),
            *sums,
        )

    early, output, ffgate_grad, out_grad, *sums = line.run(
        cross_attn, grad_branch_full, mixed, early, resid, gate_sum, got_gate, *sums, *ends_ffn
    )

    out_sum = grad_scatter(out_grad)

    def close_attn(early, up_sum, got_up, *sums):
        return (early + z_flip(early, 2), join_all(up_sum, got_up), *fold_close(*sums))

    early, up_grad, *ends = line.run(close_attn, early, up_sum, got_up, *sums)

    attn_sum, = line.enter(attn_sum)

    def last_dots(tokens, inverse1, attn_sum, down_sum, *ends):
        got_down = flip(give_rows(down_sum, across), "x")
        got_attn = flip(give_rows(attn_sum, across), "x")
        grad_own = fold_end(*ends)
        late = gain_part(grad_own, tokens, inverse1)
        late = late + z_flip(late, 1)
        return (
            got_attn,
            got_down,
            grad_own,
            partial_dots(grad_own, tokens, inverse1, gain_attn_own),
            late + z_flip(late, 2),
        )

    got_attn, got_down, grad_hidden1, dots, late = line.run(
        last_dots, tokens, inverse1, attn_sum, down_sum, *ends
    )
    cuts = (
        0,
        query_width,
        2 * query_width,
        2 * query_width + key_width,
        2 * query_width + 2 * key_width,
    )

    blocks = local // 128

    def last_spot(late, early):
        own = jnp.stack([late, early[:blocks]])
        spot = lax.dynamic_update_slice_in_dim(
            jnp.zeros((2, width // 128, 128), jnp.float32), own, offset // 128, 1
        ).reshape(-1, 128)
        spot = jnp.concatenate([spot, early[blocks:]], axis=0)
        spot = spot + flip(spot, "core")
        return spot + flip(spot, "y")

    def last_norm(
        grad_hidden1, tokens, inverse1, dots, grad_resid, late, early, attn_sum, got_attn, out_sum,
        down_sum, got_down
    ):
        got_out = flip(give_rows(out_sum, across), "x")
        spot = last_spot(late + flip(late, "x"), early)
        grad_tokens, unused = norm_back(
            grad_hidden1, tokens, inverse1, gain_attn_own, dots, grad_resid
        )
        return (
            got_out,
            spot,
            grad_tokens,
            join_all(down_sum, got_down),
            *[join(attn_sum, got_attn, cuts[i], cuts[i + 1]) for i in range(4)],
        )

    got_out, spot, grad_tokens, down_part, *attn_parts = line.run(
        last_norm, grad_hidden1, tokens, inverse1, dots, grad_resid, late, early, attn_sum,
        got_attn, out_sum, down_sum, got_down
    )
    out_part = line.run(join_all, out_sum, got_out)
    lines = width // 128
    return (
        output,
        grad_tokens,
        spot[:lines].reshape(width),
        spot[lines : 2 * lines].reshape(width),
        spot[2 * lines] + line.token[0],
        spot[2 * lines + 1],
        *attn_parts,
        out_part,
        ffgate_grad,
        up_grad,
        down_part,
    )


def solution(mesh):
    rows, columns = mesh.devices.shape

    def run(*args):
        head_dim = args[5].shape[0]
        query_width, key_width = args[7].shape[1], args[9].shape[1]
        one_key_head = key_width == 2 * columns * head_dim and query_width % key_width == 0
        if not (rows == 8 and columns == 4 and one_key_head):
            return plain(mesh)(*args)
        names = ("z", "x", "y", "core")
        inner = Mesh(mesh.devices.reshape(4, 2, 2, 2), names)
        block = P(("z", "x"), ("y", "core"))
        whole = P()
        in_specs = (block, block, P(("z", "x"))) + (whole,) * 4 + (block,) * 8
        out_specs = (block, block) + (whole,) * 4 + (block,) * 8
        return jax.shard_map(
            fast_body, mesh=inner, in_specs=in_specs, out_specs=out_specs, check_vma=False
        )(*args)

    return run
```

```python
from functools import partial

import jax
import jax.numpy as jnp
from jax import lax
from jax.experimental import pallas as pl
from jax.experimental.pallas import tpu as pltpu
from jax.sharding import Mesh
from jax.sharding import PartitionSpec as P

eps_norm = 1e-06
rope_base = 1000000.0


def norm_rows(values, gain):
    inverse = lax.rsqrt(jnp.mean(values * values, axis=-1, keepdims=True) + eps_norm)
    return (values * inverse * gain, inverse)


def rope_tables(segments, head_dim):
    count = segments.shape[0]
    index = jnp.arange(count, dtype=jnp.int32)
    previous = jnp.concatenate([jnp.full((1,), -1, jnp.int32), segments[:-1]])
    starts = lax.cummax(jnp.where(segments != previous, index, 0), axis=0)
    position = (index - starts).astype(jnp.float32)
    half = head_dim // 2
    freqs = jnp.power(rope_base, -(jnp.arange(half, dtype=jnp.float32) * 2.0 / head_dim))
    angle = position[:, None] * freqs[None, :]
    angle = jnp.concatenate([angle, angle], axis=1)
    return (jnp.cos(angle), jnp.sin(angle))


def attend_mask(segments):
    count = segments.shape[0]
    index = jnp.arange(count, dtype=jnp.int32)
    earlier = index[None, :] < index[:, None]
    same = (segments[None, :] == segments[:, None]) & (segments[None, :] > 0)
    return (index[None, :] == index[:, None]) | earlier & same


def head_prepare(raw, gain, cosine, sine):
    count = raw.shape[0]
    head_dim = gain.shape[0]
    heads = raw.reshape(count, -1, head_dim)
    inverse = lax.rsqrt(jnp.mean(heads * heads, axis=-1, keepdims=True) + eps_norm)
    normed = heads * inverse * gain
    half = head_dim // 2
    turned = jnp.concatenate([-normed[..., half:], normed[..., :half]], axis=-1)
    return (normed * cosine[:, None, :] + turned * sine[:, None, :]).reshape(count, -1)


def feature_gather(values):
    return lax.all_gather(values, "col", axis=1, tiled=True)


def feature_sum(values):
    return lax.psum_scatter(
        values.astype(jnp.bfloat16), "col", scatter_dimension=1, tiled=True
    ).astype(jnp.float32)


def rows_in(operand, weight):
    return jnp.dot(
        operand,
        lax.all_gather(weight, "row", axis=0, tiled=True),
        preferred_element_type=jnp.float32,
    )


def rows_out(operand, weight):
    return lax.dot_general(
        operand,
        lax.all_gather(weight, "row", axis=0, tiled=True),
        (((1,), (1,)), ((), ())),
        preferred_element_type=jnp.float32,
    )


def weight_grads(firsts, seconds):
    blocks = []
    for first, second in zip(firsts, seconds):
        blocks.append(
            lax.dot_general(
                first, second, (((0,), (0,)), ((), ())), preferred_element_type=jnp.float32
            )
        )
    return lax.psum_scatter(
        jnp.concatenate(blocks, axis=1).astype(jnp.bfloat16), "row", scatter_dimension=0, tiled=True
    ).astype(jnp.float32)


def norm_back(partial_grad, unit, inverse, gain, local):
    offset = lax.axis_index("col") * local
    width = unit.shape[1]
    unit_own = lax.dynamic_slice_in_dim(unit, offset, local, 1)
    grad_own = feature_sum(partial_grad)
    gain_own = lax.dynamic_slice_in_dim(gain, offset, local, 0)
    scaled = grad_own * gain_own
    dots = lax.psum(jnp.sum(scaled * unit_own, axis=1), "col")[:, None] / width
    grad_input = inverse * (scaled - unit_own * dots)
    gain_grad = lax.dynamic_update_slice_in_dim(
        jnp.zeros((width,), jnp.float32), jnp.sum(grad_own * unit_own, axis=0), offset, 0
    )
    return (grad_input, gain_grad)


def attend_scores(query, keys, allowed, kv_heads, head_dim):
    count = query.shape[0]
    grouped = query.reshape(count, kv_heads, -1, head_dim)
    keyed = keys.reshape(count, kv_heads, head_dim)
    scores = jnp.einsum(
        "qgrd,kgd->grqk", grouped, keyed, preferred_element_type=jnp.float32
    ) * head_dim ** (-0.5)
    return (jnp.where(allowed, scores, -1e30), grouped, keyed)


def attend_forward(query, keys, values, allowed, kv_heads, head_dim):
    count = query.shape[0]
    scores, grouped, keyed = attend_scores(query, keys, allowed, kv_heads, head_dim)
    peak = jnp.max(scores, axis=-1, keepdims=True)
    weights = jnp.exp(scores - peak)
    total = jnp.sum(weights, axis=-1, keepdims=True)
    probs = (weights / total).astype(jnp.bfloat16)
    valued = values.reshape(count, kv_heads, head_dim)
    attended = jnp.einsum("grqk,kgd->qgrd", probs, valued, preferred_element_type=jnp.float32)
    return (attended.reshape(count, -1), peak + jnp.log(total))


def attend_backward(query, keys, values, allowed, logsum, grad_attended, kv_heads, head_dim):
    count = query.shape[0]
    scores, grouped, keyed = attend_scores(query, keys, allowed, kv_heads, head_dim)
    probs_exact = jnp.exp(scores - logsum)
    probs = probs_exact.astype(jnp.bfloat16)
    valued = values.reshape(count, kv_heads, head_dim)
    grad_grouped = grad_attended.reshape(count, kv_heads, -1, head_dim)
    grad_values = jnp.einsum(
        "grqk,qgrd->kgd", probs, grad_grouped, preferred_element_type=jnp.float32
    )
    grad_probs = jnp.einsum(
        "qgrd,kgd->grqk", grad_grouped, valued, preferred_element_type=jnp.float32
    )
    delta = jnp.sum(probs_exact * grad_probs, axis=-1, keepdims=True)
    grad_scores = (probs_exact * (grad_probs - delta)).astype(jnp.bfloat16)
    grad_query = jnp.einsum(
        "grqk,kgd->qgrd", grad_scores, keyed, preferred_element_type=jnp.float32
    ) * head_dim ** (-0.5)
    grad_keys = jnp.einsum(
        "grqk,qgrd->kgd", grad_scores, grouped, preferred_element_type=jnp.float32
    ) * head_dim ** (-0.5)
    return (
        grad_query.reshape(count, -1),
        grad_keys.reshape(count, -1),
        grad_values.reshape(count, -1).astype(jnp.bfloat16),
    )


def body(
    tokens,
    cotangent,
    segment_ids,
    gain_attn,
    gain_ffn,
    gain_query,
    gain_key,
    w_query,
    w_gate,
    w_key,
    w_value,
    w_out,
    w_ffgate,
    w_up,
    w_down,
):
    local = tokens.shape[1]
    head_dim = gain_query.shape[0]
    query_width = w_query.shape[1]
    key_width = w_key.shape[1]
    kv_heads = key_width // head_dim
    hidden_width = w_ffgate.shape[1]
    live = (segment_ids > 0).astype(jnp.float32)[:, None]
    cosine, sine = rope_tables(segment_ids, head_dim)
    allowed = attend_mask(segment_ids)
    attn_weight = jnp.concatenate([w_query, w_gate, w_key, w_value], axis=1)
    ffn_weight = jnp.concatenate([w_ffgate, w_up], axis=1)
    blocks = (attn_weight, ffn_weight, w_out, w_down)

    def apply_in(operand, which_block):
        return rows_in(operand, blocks[which_block])

    def apply_out(operand, which_block):
        return rows_out(operand, blocks[which_block])

    inputs = feature_gather(tokens).astype(jnp.float32)
    normed1, inverse1 = norm_rows(inputs, gain_attn)
    hidden1 = normed1.astype(jnp.bfloat16)
    joint = apply_in(hidden1, 0)
    query_raw = joint[:, :query_width]
    gate_raw = joint[:, query_width : 2 * query_width]
    key_raw = joint[:, 2 * query_width : 2 * query_width + key_width]
    values = joint[:, 2 * query_width + key_width :].astype(jnp.bfloat16)
    prepare = partial(head_prepare, cosine=cosine, sine=sine)
    query = prepare(query_raw, gain_query).astype(jnp.bfloat16)
    keys = prepare(key_raw, gain_key).astype(jnp.bfloat16)
    attended, logsum = attend_forward(query, keys, values, allowed, kv_heads, head_dim)
    gate_sig = jax.nn.sigmoid(gate_raw)
    mixed = (attended * gate_sig).astype(jnp.bfloat16)
    resid = tokens.astype(jnp.float32) + feature_sum(apply_out(mixed, 2))
    resid_full = feature_gather(resid.astype(jnp.bfloat16)).astype(jnp.float32)
    normed2, inverse2 = norm_rows(resid_full, gain_ffn)
    hidden2 = normed2.astype(jnp.bfloat16)
    ffn_joint = apply_in(hidden2, 1)
    ff_gate = ffn_joint[:, :hidden_width]
    ff_up = ffn_joint[:, hidden_width:]
    sig_gate = jax.nn.sigmoid(ff_gate)
    activated = (jax.nn.silu(ff_gate) * ff_up).astype(jnp.bfloat16)
    ffn_out = feature_sum(apply_out(activated, 3))
    output = (live * (resid + ffn_out)).astype(jnp.bfloat16)
    grad_out = live * cotangent.astype(jnp.float32)
    grad_ffn_full = feature_gather(grad_out.astype(jnp.bfloat16))
    grad_act = apply_in(grad_ffn_full, 3)
    grad_ffup = (grad_act * (ff_gate * sig_gate)).astype(jnp.bfloat16)
    grad_ffgate = (grad_act * ff_up * sig_gate * (1.0 + ff_gate * (1.0 - sig_gate))).astype(
        jnp.bfloat16
    )
    grad_pair = jnp.concatenate([grad_ffgate, grad_ffup], axis=1)
    ffn_grads = weight_grads((hidden2, grad_ffn_full), (grad_pair, activated))
    grad_input2, gain_ffn_grad = norm_back(
        apply_out(grad_pair, 1), resid_full * inverse2, inverse2, gain_ffn, local
    )
    grad_resid = grad_out + grad_input2
    grad_branch_full = feature_gather(grad_resid.astype(jnp.bfloat16))
    grad_mixed = apply_in(grad_branch_full, 2)
    grad_attended = (grad_mixed * gate_sig).astype(jnp.bfloat16)
    grad_gate_raw = (grad_mixed * attended * gate_sig * (1.0 - gate_sig)).astype(jnp.bfloat16)
    grad_query, grad_keys, grad_values = attend_backward(
        query, keys, values, allowed, logsum, grad_attended, kv_heads, head_dim
    )
    unused_query, query_back = jax.vjp(prepare, query_raw, gain_query)
    grad_query_raw, grad_gain_query = query_back(grad_query)
    unused_key, key_back = jax.vjp(prepare, key_raw, gain_key)
    grad_key_raw, grad_gain_key = key_back(grad_keys)
    grad_joint = jnp.concatenate(
        [
            grad_query_raw.astype(jnp.bfloat16),
            grad_gate_raw,
            grad_key_raw.astype(jnp.bfloat16),
            grad_values,
        ],
        axis=1,
    )
    attn_grads = weight_grads((hidden1, grad_branch_full), (grad_joint, mixed))
    grad_input1, gain_attn_grad = norm_back(
        apply_out(grad_joint, 0), inputs * inverse1, inverse1, gain_attn, local
    )
    grad_tokens = grad_resid + grad_input1
    gains = lax.psum(
        (gain_attn_grad, gain_ffn_grad, grad_gain_query, grad_gain_key), ("row", "col")
    )
    second_cut = 2 * query_width
    third_cut = 2 * query_width + key_width
    fourth_cut = 2 * query_width + 2 * key_width
    return (
        output,
        grad_tokens,
        gains[0],
        gains[1],
        gains[2],
        gains[3],
        attn_grads[:, :query_width],
        attn_grads[:, query_width:second_cut],
        attn_grads[:, second_cut:third_cut],
        attn_grads[:, third_cut:fourth_cut],
        attn_grads[:, fourth_cut:],
        ffn_grads[:, :hidden_width],
        ffn_grads[:, hidden_width : 2 * hidden_width],
        ffn_grads[:, 2 * hidden_width :],
    )


def plain(mesh):
    in_specs = (
        P("row", "col"),
        P("row", "col"),
        P("row"),
        P(),
        P(),
        P(),
        P(),
        P("row", "col"),
        P("row", "col"),
        P("row", "col"),
        P("row", "col"),
        P("row", "col"),
        P("row", "col"),
        P("row", "col"),
        P("row", "col"),
    )
    out_specs = (
        P("row", "col"),
        P("row", "col"),
        P(),
        P(),
        P(),
        P(),
        P("row", "col"),
        P("row", "col"),
        P("row", "col"),
        P("row", "col"),
        P("row", "col"),
        P("row", "col"),
        P("row", "col"),
        P("row", "col"),
    )
    return jax.shard_map(body, mesh=mesh, in_specs=in_specs, out_specs=out_specs, check_vma=False)


def tie(*values):
    return lax.optimization_barrier(values)


def flip(values, axis):
    return lax.ppermute(values, axis, [(0, 1), (1, 0)])


light = pl.CostEstimate(flops=0, bytes_accessed=0, transcendentals=0)


heavy = light


class Line:
    def __init__(self):
        self.token = jnp.zeros((8, 128), jnp.float32)

    def enter(self, *values):
        *values, self.token = lax.optimization_barrier((*values, self.token))
        return values

    def run(self, work, *values):
        result = work(*self.enter(*values))
        if isinstance(result, (tuple, list)):
            return self.enter(*result)
        return self.enter(result)[0]


def pack_kernel(normed, place_ref, gain_ref, *refs):
    blocks, out_ref = refs[:4], refs[5]
    width = blocks[0].shape[1]
    place = place_ref[0]
    if normed:
        values = [block[...].astype(jnp.float32) for block in blocks]
        squares = sum(jnp.sum(v * v, axis=1, keepdims=True) for v in values)
        inverse = lax.rsqrt(squares / (4 * width) + eps_norm)
        refs[6][...] = inverse
    for index in range(4):
        columns = pl.ds(pl.multiple_of((place ^ index) * width, width), width)
        if normed:
            result = values[index] * inverse * gain_ref[:, columns]
            out_ref[:, columns] = result.astype(out_ref.dtype)
        else:
            out_ref[:, columns] = blocks[index][...]


def pack(blocks, place, gain, normed, step, target):
    count, width = blocks[0].shape
    tile = 256
    tiles = count // tile
    out_shape = [jax.ShapeDtypeStruct((2 * count, 4 * width), jnp.bfloat16)]
    out_specs = [pl.BlockSpec((tile, 4 * width), lambda i: (i + step * tiles, 0))]
    if normed:
        out_shape.append(jax.ShapeDtypeStruct((count, 1), jnp.float32))
        out_specs.append(pl.BlockSpec((tile, 1), lambda i: (i, 0)))
    aliases = {}
    if target is None:
        target = place.reshape(1)
    else:
        aliases = {6: 0}
    return pl.pallas_call(
        partial(pack_kernel, normed),
        grid=(tiles,),
        in_specs=[
            pl.BlockSpec(memory_space=pltpu.SMEM),
            pl.BlockSpec((1, 4 * width), lambda i: (0, 0)),
        ]
        + [pl.BlockSpec((tile, width), lambda i: (i, 0))] * 4
        + [pl.BlockSpec(memory_space=pl.ANY if aliases else pltpu.SMEM)],
        out_specs=out_specs,
        out_shape=out_shape,
        input_output_aliases=aliases,
        cost_estimate=light,
    )(place.reshape(1), gain.reshape(1, -1), *blocks, target)


def direct(own):
    return (flip(own, "y"), flip(own, "x"), flip(own, "core"))


def relay_flips(via_y, via_x):
    half = via_y.shape[0] // 2
    upper = flip(via_y[:half], "x")
    lower = flip(via_x[half:], "y")
    return (flip(via_y, "core"), via_x, flip(via_x, "core"), upper, lower)


def relay(own, via_y, via_x, own_core, place, gain, normed):
    y_core, *steps = relay_flips(via_y, via_x)
    return (*steps, *pack((own, own_core, via_y, y_core), place, gain, normed, 0, None))


def diagonal(via_x, x_core, upper, lower, target, place, gain, normed):
    crossed = jnp.concatenate([upper, lower], axis=0)
    far = (via_x, x_core, crossed, flip(crossed, "core"))
    return pack(far, place, gain, normed, 1, target)[0]


def halves_kernel(count, across_ref, *refs):
    across = across_ref[0]
    keep_ref, give_ref = refs[count:]
    at = 0
    for weight_ref in refs[:count]:
        width = weight_ref.shape[1] // 2
        for target, side in ((keep_ref, across), (give_ref, 1 - across)):
            target[:, at : at + width] = weight_ref[:, pl.ds(pl.multiple_of(side * width, width), width)]
        at += width


def halves(weights, across):
    rows = weights[0].shape[0]
    width = sum(weight.shape[1] for weight in weights) // 2
    shape = jax.ShapeDtypeStruct((rows, width), jnp.bfloat16)
    whole = pl.BlockSpec(memory_space=pltpu.VMEM)
    return pl.pallas_call(
        partial(halves_kernel, len(weights)),
        in_specs=[pl.BlockSpec(memory_space=pltpu.SMEM)] + [whole] * len(weights),
        out_specs=[whole, whole],
        out_shape=[shape, shape],
        cost_estimate=light,
    )(across.reshape(1), *weights)


def weight_rows(keep, got, across):
    top = jnp.where(across == 0, keep, got)
    bottom = jnp.where(across == 0, got, keep)
    return jnp.concatenate([top, bottom], axis=0)


def weight_gather(rows):
    return lax.all_gather(rows, "z", axis=0, tiled=True)


def grad_scatter(grads):
    return lax.psum_scatter(grads, "z", scatter_dimension=0, tiled=True)


def keep_rows(summed, across):
    rows = summed.shape[0] // 2
    return lax.dynamic_slice_in_dim(summed, across * rows, rows, 0)


def give_rows(summed, across):
    return keep_rows(summed, 1 - across)


def z_flip(values, step):
    return lax.ppermute(values, "z", [(i, i ^ step) for i in range(4)])


vmem = pltpu.CompilerParams(vmem_limit_bytes=56 * 1024 * 1024)


def join_kernel(widths, across_ref, sums_ref, got_ref, *out_refs):
    across = across_ref[0]
    rows = got_ref.shape[0]
    keep = pl.ds(pl.multiple_of(across * rows, rows), rows)
    at = 0
    for width, out_ref in zip(widths, out_refs):
        own = pl.ds(pl.multiple_of(across * width, width), width)
        other = pl.ds(pl.multiple_of((1 - across) * width, width), width)
        out_ref[:, own] = sums_ref[keep, at : at + width].astype(jnp.float32)
        out_ref[:, other] = got_ref[:, at : at + width].astype(jnp.float32)
        at += width


def join_parts(sums, got, across, widths):
    rows = got.shape[0]
    whole = pl.BlockSpec(memory_space=pltpu.VMEM)
    return pl.pallas_call(
        partial(join_kernel, widths),
        in_specs=[pl.BlockSpec(memory_space=pltpu.SMEM), whole, whole],
        out_specs=[whole] * len(widths),
        out_shape=[jax.ShapeDtypeStruct((rows, 2 * width), jnp.float32) for width in widths],
        compiler_params=vmem,
        cost_estimate=light,
    )(across.reshape(1), sums, got)


def fold_turn(near_ref, far_ref, turned):
    rows = near_ref.shape[0]

    @pl.when(pl.program_id(0) == 0)
    def turn():
        turned[:, :rows] = near_ref[...].T
        turned[:, rows:] = far_ref[...].T


def fold_sent_kernel(place_ref, operand_ref, near_ref, far_ref, near_out, far_out, turned):
    fold_turn(near_ref, far_ref, turned)
    rows = near_out.shape[1]
    both = product_nn(operand_ref[...], turned[...]).astype(near_out.dtype)
    near_out[...] = both[:, :rows]
    far_out[...] = both[:, rows:]


def fold_held_kernel(
    place_ref, operand_ref, near_ref, far_ref, near_got, far_got,
    upper_send, upper_keep, lower_send, lower_keep, turned,
):
    fold_turn(near_ref, far_ref, turned)
    low = upper_send.dtype
    rows = near_got.shape[1]
    both = product_nn(operand_ref[...], turned[...])
    near = (both[:, :rows] + near_got[...].astype(jnp.float32)).astype(low)
    far = (both[:, rows:] + far_got[...].astype(jnp.float32)).astype(low)
    step = pl.program_id(0)

    @pl.when(step == 0)
    def first():
        upper_send[0] = near
        upper_send[1] = far

    @pl.when(step == 1)
    def second():
        upper_keep[0] = near
        upper_keep[1] = far

    @pl.when(step >= 2)
    def third():
        lower_send[...] = far
        lower_keep[...] = near


def fold_rows(i):
    return (1 - i % 2) * 2 + i // 2


def fold_specs(tile, width, rows, column, near, far):
    return [
        pl.BlockSpec((tile, width), lambda i, p: (fold_rows(i), 0)),
        pl.BlockSpec((rows, width), lambda i, p: (p[0] ^ near, column)),
        pl.BlockSpec((rows, width), lambda i, p: (p[0] ^ far, column)),
    ]


def fold_sent(operand, weight, place, column=0):
    count, width = operand.shape
    rows, tile = weight.shape[0] // 4, count // 4
    out = pl.BlockSpec((tile, rows), lambda i, p: (fold_rows(i), 0))
    near, far = pl.pallas_call(
        fold_sent_kernel,
        grid_spec=pltpu.PrefetchScalarGridSpec(
            num_scalar_prefetch=1,
            grid=(4,),
            in_specs=fold_specs(tile, width, rows, column, 1, 3),
            out_specs=[out, out],
            scratch_shapes=[pltpu.VMEM((width, 2 * rows), jnp.bfloat16)],
        ),
        out_shape=[jax.ShapeDtypeStruct((count, rows), jnp.bfloat16)] * 2,
        compiler_params=vmem,
        cost_estimate=light,
    )(place.reshape(1), operand, weight, weight)
    return (near, far)


def fold_swap(operand, weight, place, column=0):
    return tuple(flip(v, "core") for v in fold_sent(operand, weight, place, column))


def fold_held(operand, weight, place, near_got, far_got, column=0):
    count, width = operand.shape
    rows, tile = weight.shape[0] // 4, count // 4
    got = pl.BlockSpec((tile, rows), lambda i, p: (fold_rows(i), 0))
    whole = pl.BlockSpec((2, tile, rows), lambda i, p: (0, 0, 0))
    late = pl.BlockSpec((tile, rows), lambda i, p: (jnp.where(i < 3, 1, 0), 0))
    shape = jax.ShapeDtypeStruct
    return pl.pallas_call(
        fold_held_kernel,
        grid_spec=pltpu.PrefetchScalarGridSpec(
            num_scalar_prefetch=1,
            grid=(4,),
            in_specs=fold_specs(tile, width, rows, column, 0, 2) + [got, got],
            out_specs=[whole, whole, late, late],
            scratch_shapes=[pltpu.VMEM((width, 2 * rows), jnp.bfloat16)],
        ),
        out_shape=[shape((2, tile, rows), jnp.bfloat16)] * 2
        + [shape((2 * tile, rows), jnp.bfloat16)] * 2,
        compiler_params=vmem,
        cost_estimate=light,
    )(place.reshape(1), operand, weight, weight, near_got, far_got)


def fold_cross(upper_send, upper_keep, lower_send, lower_keep):
    return (flip(upper_send, "x"), upper_keep, flip(lower_send, "y"), lower_keep)


def fold_close_kernel(
    upper_ref, upper_keep, own_ref, own_keep, other_ref, other_keep,
    upper_near, upper_far, lower_own, lower_other,
):
    wide = lambda ref: ref[...].astype(jnp.float32)
    total = wide(upper_ref) + wide(upper_keep)
    upper_near[...] = total[0]
    upper_far[...] = total[1].astype(upper_far.dtype)
    lower_own[...] = wide(own_ref) + wide(own_keep)
    lower_other[...] = (wide(other_ref) + wide(other_keep)).astype(lower_other.dtype)


def fold_close(upper, upper_keep, lower, lower_keep):
    count, rows = upper.shape[1:]
    tile = count // 2
    pair = pl.BlockSpec((2, tile, rows), lambda i: (0, i, 0))
    own = pl.BlockSpec((tile, rows), lambda i: (i, 0))
    other = pl.BlockSpec((tile, rows), lambda i: (i + 2, 0))
    shapes = [jax.ShapeDtypeStruct((count, rows), kind) for kind in (jnp.float32, jnp.bfloat16)]
    upper_near, upper_far, lower_own, lower_other = pl.pallas_call(
        fold_close_kernel,
        grid=(2,),
        in_specs=[pair, pair, own, own, other, other],
        out_specs=[own] * 4,
        out_shape=shapes * 2,
        cost_estimate=light,
    )(upper, upper_keep, lower, lower_keep, lower, lower_keep)
    return (upper_near, flip(upper_far, "y"), lower_own, flip(lower_other, "x"))


def fold_end(upper_near, upper_got, lower_own, lower_got):
    return jnp.concatenate([upper_near + upper_got, lower_own + lower_got], axis=0)


def matmul_kernel(form, operand_ref, weight_ref, out_ref):
    out_ref[...] = form(operand_ref[...], weight_ref[...]).astype(out_ref.dtype)


def dot_in(operand, weight, width, column=0):
    count, depth = operand.shape
    tile = 512
    return pl.pallas_call(
        partial(matmul_kernel, product_nn),
        grid=(count // tile,),
        in_specs=[
            pl.BlockSpec((tile, depth), lambda i: (i, 0)),
            pl.BlockSpec((depth, width), lambda i: (0, column)),
        ],
        out_specs=pl.BlockSpec((tile, width), lambda i: (i, 0)),
        out_shape=jax.ShapeDtypeStruct((count, width), jnp.float32),
        compiler_params=vmem,
        cost_estimate=light,
    )(operand, weight)


def dot_grad(first, second, width=None, column=0, cost=light):
    count, rows = first.shape
    width = second.shape[1] if width is None else width
    tile = 512
    return pl.pallas_call(
        partial(matmul_kernel, product_tn),
        grid=(rows // tile,),
        in_specs=[
            pl.BlockSpec((count, tile), lambda i: (0, i)),
            pl.BlockSpec((count, width), lambda i: (0, column)),
        ],
        out_specs=pl.BlockSpec((tile, width), lambda i: (i, 0)),
        out_shape=jax.ShapeDtypeStruct((rows, width), jnp.bfloat16),
        compiler_params=vmem,
        cost_estimate=cost,
    )(first, second)


def dot_grad_part(first, second, whole, column, target=None):
    count, rows = first.shape
    width = second.shape[1]
    tile = 512
    in_specs = [
        pl.BlockSpec((count, tile), lambda i: (0, i)),
        pl.BlockSpec((count, width), lambda i: (0, 0)),
    ]
    kernel, operands, aliases = partial(matmul_kernel, product_tn), (first, second), {}
    if target is not None:
        in_specs.append(pl.BlockSpec(memory_space=pl.ANY))
        operands, aliases = (first, second, target), {2: 0}
        kernel = lambda a, b, unused, out: matmul_kernel(product_tn, a, b, out)
    return pl.pallas_call(
        kernel,
        grid=(rows // tile,),
        in_specs=in_specs,
        out_specs=pl.BlockSpec((tile, width), lambda i: (i, column)),
        out_shape=jax.ShapeDtypeStruct((rows, whole), jnp.bfloat16),
        input_output_aliases=aliases,
        compiler_params=vmem,
        cost_estimate=light,
    )(*operands)


def ffn_kernel(hidden_ref, weight_ref, grad_ref, activated_ref, pair_ref):
    width = activated_ref.shape[1]
    low = jnp.bfloat16
    step = 256
    for at in range(0, width, step):
        ff_gate = product_nn(hidden_ref[...], weight_ref[:, at : at + step])
        ff_up = product_nn(hidden_ref[...], weight_ref[:, width + at : width + at + step])
        grad = grad_ref[:, at : at + step]
        sig_gate = jax.nn.sigmoid(ff_gate)
        passed = ff_gate * sig_gate
        activated_ref[:, at : at + step] = (passed * ff_up).astype(low)
        pair_ref[:, width + at : width + at + step] = (grad * passed).astype(low)
        pair_ref[:, at : at + step] = (
            grad * ff_up * sig_gate * (1.0 + ff_gate * (1.0 - sig_gate))
        ).astype(low)


def ffn(hidden, weight, grad):
    count, depth = hidden.shape
    width = weight.shape[1] // 2
    tile = 256
    return pl.pallas_call(
        ffn_kernel,
        grid=(count // tile,),
        in_specs=[
            pl.BlockSpec((tile, depth), lambda i: (i, 0)),
            pl.BlockSpec((depth, 2 * width), lambda i: (0, 0)),
            pl.BlockSpec((tile, width), lambda i: (i, 0)),
        ],
        out_specs=[
            pl.BlockSpec((tile, width), lambda i: (i, 0)),
            pl.BlockSpec((tile, 2 * width), lambda i: (i, 0)),
        ],
        out_shape=[
            jax.ShapeDtypeStruct((count, width), jnp.bfloat16),
            jax.ShapeDtypeStruct((count, 2 * width), jnp.bfloat16),
        ],
        compiler_params=vmem,
        cost_estimate=light,
    )(hidden, weight, grad)


def row_tables(segments, head_dim):
    count = segments.shape[0]
    index = jnp.arange(count, dtype=jnp.int32)
    previous = jnp.concatenate([jnp.full((1,), -1, jnp.int32), segments[:-1]])
    starts = lax.cummax(jnp.where(segments != previous, index, 0), axis=0)
    position = (index - starts).astype(jnp.float32)
    half = head_dim // 2
    freqs = jnp.power(rope_base, -(jnp.arange(half, dtype=jnp.float32) * 2.0 / head_dim))
    angle = position[:, None] * freqs[None, :]
    cosine, sine = jnp.cos(angle), jnp.sin(angle)
    return (
        jnp.concatenate([cosine, cosine], axis=1),
        jnp.concatenate([-sine, sine], axis=1),
        jnp.where(segments > 0, starts, index)[None, :],
    )


def product_nt(first, second):
    return lax.dot_general(
        first, second, (((1,), (1,)), ((), ())), preferred_element_type=jnp.float32
    )


def product_tn(first, second):
    return lax.dot_general(
        first, second, (((0,), (0,)), ((), ())), preferred_element_type=jnp.float32
    )


def product_nn(first, second):
    return lax.dot_general(
        first, second, (((1,), (0,)), ((), ())), preferred_element_type=jnp.float32
    )


def prepare_tile(raw, gain, cosine, sine):
    inverse = lax.rsqrt(jnp.mean(raw * raw, axis=1, keepdims=True) + eps_norm)
    normed = raw * inverse * gain
    turned = pltpu.roll(normed, raw.shape[1] // 2, 1)
    return (normed * cosine + turned * sine).astype(jnp.bfloat16)


def prepare_back(raw, gain, cosine, sine, grad):
    inverse = lax.rsqrt(jnp.mean(raw * raw, axis=1, keepdims=True) + eps_norm)
    unit = raw * inverse
    grad_normed = grad * cosine + pltpu.roll(grad * sine, raw.shape[1] // 2, 1)
    scaled = grad_normed * gain
    grad_raw = inverse * (scaled - unit * jnp.mean(scaled * unit, axis=1, keepdims=True))
    return (grad_raw.astype(jnp.bfloat16), jnp.sum(grad_normed * unit, axis=0, keepdims=True))


def allowed_tile(first_ref, start, tile, reach):
    rows = lax.broadcasted_iota(jnp.int32, (reach, tile), 0)
    columns = lax.broadcasted_iota(jnp.int32, (reach, tile), 1) + start
    return (rows >= first_ref[0, :, pl.ds(start, tile)]) & (rows <= columns)


def attend_kernel(
    heads, tile, joint_ref, cos_ref, sin_ref, first_ref, gain_query_ref, gain_key_ref,
    mixed_ref, attended_ref, query_ref, key_ref, logsum_ref,
):
    count, head_dim = cos_ref.shape
    scale = head_dim ** (-0.5)
    low = jnp.bfloat16
    key_at = 2 * heads * head_dim
    tiles = count // tile
    for part in range(tiles):
        rows = pl.ds(part * tile, tile)
        key_ref[rows, :] = prepare_tile(
            joint_ref[rows, key_at : key_at + head_dim],
            gain_key_ref[...],
            cos_ref[rows, :],
            sin_ref[rows, :],
        )
    for head in range(heads):
        columns = slice(head * head_dim, (head + 1) * head_dim)
        gates = slice((heads + head) * head_dim, (heads + head + 1) * head_dim)
        for part in range(tiles):
            rows = pl.ds(part * tile, tile)
            reach = (part + 1) * tile
            query = prepare_tile(
                joint_ref[rows, columns], gain_query_ref[...], cos_ref[rows, :], sin_ref[rows, :]
            )
            query_ref[rows, columns] = query
            scores = product_nt(key_ref[:reach, :], query) * scale
            scores = jnp.where(allowed_tile(first_ref, part * tile, tile, reach), scores, -1e30)
            peak = jnp.max(scores, axis=0, keepdims=True)
            weights = jnp.exp(scores - peak)
            total = jnp.sum(weights, axis=0, keepdims=True)
            probs = (weights * (1.0 / total)).astype(low)
            logsum_ref[0, head : head + 1, rows] = peak + jnp.log(total)
            values = joint_ref[:reach, key_at + head_dim : key_at + 2 * head_dim].astype(low)
            attended = product_tn(values, probs).T
            attended_ref[rows, columns] = attended
            gate = joint_ref[rows, gates]
            mixed_ref[rows, columns] = (attended * jax.nn.sigmoid(gate)).astype(low)


def attend_back_kernel(
    heads, tile, joint_ref, cos_ref, sin_ref, first_ref, gain_query_ref, gain_key_ref,
    attended_ref, query_ref, key_ref, logsum_ref, grad_mixed_ref,
    grad_joint_ref, grad_gain_ref, grad_key_acc, grad_value_acc,
):
    count, head_dim = cos_ref.shape
    scale = head_dim ** (-0.5)
    low = jnp.bfloat16
    key_at = 2 * heads * head_dim
    value_at = key_at + head_dim
    tiles = count // tile
    gain_query = jnp.zeros((1, head_dim), jnp.float32)
    gain_key = jnp.zeros((1, head_dim), jnp.float32)
    for head in range(heads):
        columns = slice(head * head_dim, (head + 1) * head_dim)
        gates = slice((heads + head) * head_dim, (heads + head + 1) * head_dim)
        for part in reversed(range(tiles)):
            rows = pl.ds(part * tile, tile)
            reach = (part + 1) * tile
            fresh = head == 0 and part == tiles - 1
            gate = jax.nn.sigmoid(joint_ref[rows, gates])
            grad_mixed = grad_mixed_ref[rows, columns]
            gated = grad_mixed * gate
            grad_attended = gated.astype(low)
            grad_joint_ref[rows, gates] = (gated * attended_ref[rows, columns] * (1.0 - gate)).astype(
                low
            )
            query = query_ref[rows, columns]
            keys = key_ref[:reach, :]
            values = joint_ref[:reach, value_at : value_at + head_dim].astype(low)
            scores = product_nt(keys, query) * scale
            logsum = logsum_ref[0, head : head + 1, rows]
            probs = jnp.where(
                allowed_tile(first_ref, part * tile, tile, reach), jnp.exp(scores - logsum), 0.0
            )
            grad_value = product_nn(probs.astype(low), grad_attended)
            grad_probs = product_nt(values, grad_attended)
            delta = jnp.sum(probs * grad_probs, axis=0, keepdims=True)
            grad_scores = (probs * (grad_probs - delta)).astype(low)
            grad_key = product_nn(grad_scores, query)
            if fresh:
                grad_value_acc[...] = grad_value
                grad_key_acc[...] = grad_key
            else:
                grad_value_acc[:reach, :] += grad_value
                grad_key_acc[:reach, :] += grad_key
            grad_query = product_tn(keys, grad_scores).T * scale
            grad_raw, gain_part = prepare_back(
                joint_ref[rows, columns],
                gain_query_ref[...],
                cos_ref[rows, :],
                sin_ref[rows, :],
                grad_query,
            )
            grad_joint_ref[rows, columns] = grad_raw
            gain_query = gain_query + gain_part
    for part in range(tiles):
        rows = pl.ds(part * tile, tile)
        grad_raw, gain_part = prepare_back(
            joint_ref[rows, key_at:value_at],
            gain_key_ref[...],
            cos_ref[rows, :],
            sin_ref[rows, :],
            grad_key_acc[rows, :] * scale,
        )
        grad_joint_ref[rows, key_at:value_at] = grad_raw
        gain_key = gain_key + gain_part
        grad_joint_ref[rows, value_at : value_at + head_dim] = grad_value_acc[rows, :].astype(low)
    both = jnp.concatenate([gain_query, gain_key], axis=0)

    @pl.when(pl.program_id(0) == 0)
    def begin():
        grad_gain_ref[...] = both

    @pl.when(pl.program_id(0) > 0)
    def add():
        grad_gain_ref[...] += both


def attend_specs(count, head_dim, heads, joint_width):
    wide = lambda width: pl.BlockSpec((count, width), lambda s: (s, 0))
    row = pl.BlockSpec((1, head_dim), lambda s: (0, 0))
    lead = [
        wide(joint_width),
        wide(head_dim),
        wide(head_dim),
        pl.BlockSpec((1, 1, count), lambda s: (s, 0, 0)),
        row,
        row,
    ]
    kept = [
        wide(heads * head_dim),
        wide(heads * head_dim),
        wide(head_dim),
        pl.BlockSpec((1, heads, count), lambda s: (s, 0, 0)),
    ]
    return (lead, kept, wide)


def attend_fwd(joint, cosine, sine, first, gain_query, gain_key, heads, count):
    head_dim = cosine.shape[1]
    lead, kept, wide = attend_specs(count, head_dim, heads, joint.shape[1])
    total = joint.shape[0]
    shape = jax.ShapeDtypeStruct
    return pl.pallas_call(
        partial(attend_kernel, heads, 256),
        grid=(total // count,),
        in_specs=lead,
        out_specs=[wide(heads * head_dim)] + kept,
        out_shape=[
            shape((total, heads * head_dim), jnp.bfloat16),
            shape((total, heads * head_dim), jnp.float32),
            shape((total, heads * head_dim), jnp.bfloat16),
            shape((total, head_dim), jnp.bfloat16),
            shape((total // count, heads, count), jnp.float32),
        ],
        compiler_params=pltpu.CompilerParams(vmem_limit_bytes=40 * 1024 * 1024),
        cost_estimate=light,
    )(joint, cosine, sine, first, gain_query.reshape(1, -1), gain_key.reshape(1, -1))


def attend_bwd(joint, cosine, sine, first, gain_query, gain_key, kept_values, grad_mixed, count):
    head_dim = cosine.shape[1]
    heads = grad_mixed.shape[1] // head_dim
    lead, kept, wide = attend_specs(count, head_dim, heads, joint.shape[1])
    total = joint.shape[0]
    shape = jax.ShapeDtypeStruct
    return pl.pallas_call(
        partial(attend_back_kernel, heads, 256),
        grid=(total // count,),
        in_specs=lead + kept + [wide(heads * head_dim)],
        out_specs=[wide(joint.shape[1]), pl.BlockSpec((2, head_dim), lambda s: (0, 0))],
        out_shape=[shape(joint.shape, jnp.bfloat16), shape((2, head_dim), jnp.float32)],
        scratch_shapes=[
            pltpu.VMEM((count, head_dim), jnp.float32),
            pltpu.VMEM((count, head_dim), jnp.float32),
        ],
        compiler_params=pltpu.CompilerParams(vmem_limit_bytes=48 * 1024 * 1024),
        cost_estimate=light,
    )(
        joint, cosine, sine, first, gain_query.reshape(1, -1), gain_key.reshape(1, -1),
        *kept_values, grad_mixed,
    )


def fast_body(
    tokens,
    cotangent,
    segment_ids,
    gain_attn,
    gain_ffn,
    gain_query,
    gain_key,
    w_query,
    w_gate,
    w_key,
    w_value,
    w_out,
    w_ffgate,
    w_up,
    w_down,
):
    across = lax.axis_index("x")
    place = lax.axis_index("y") * 2 + lax.axis_index("core")
    count, local = tokens.shape
    width = gain_attn.shape[0]
    head_dim = gain_query.shape[0]
    low = jnp.bfloat16
    query_width = w_query.shape[1] // 2
    key_width = w_key.shape[1] // 2
    heads = query_width // head_dim
    hidden_width = w_ffgate.shape[1] // 2
    live = (segment_ids > 0).astype(jnp.float32)[:, None]
    offset = place * local
    gain_attn_own = lax.dynamic_slice_in_dim(gain_attn, offset, local, 0)
    gain_ffn_own = lax.dynamic_slice_in_dim(gain_ffn, offset, local, 0)

    line = Line()
    half = count // 2
    joint_width = 2 * query_width + 2 * key_width
    rows_of = partial(weight_rows, across=across)

    first_columns = [w_query, w_gate, w_key, w_value, w_out]

    def open_first(tokens, *weights):
        upper_y = flip(tokens[:half], "y")
        keep, give = halves(weights, across)
        got = flip(give, "x")
        return (rows_of(keep, got), upper_y)

    first_rows, upper_y = line.run(open_first, tokens, *first_columns)
    first_weight = weight_gather(first_rows)
    grad_out = live * cotangent.astype(jnp.float32)
    grad_out_low = grad_out.astype(low)

    def open_second(tokens, segment_ids, upper_y, w_ffgate, w_up, w_down):
        lower_y = flip(tokens[half:], "y")
        via_x = flip(tokens, "x")
        own_core = flip(tokens, "core")
        other = flip(segment_ids, "x")
        via_y = jnp.concatenate([upper_y, lower_y], axis=0)
        return (via_y, via_x, own_core, other, *halves([w_ffgate, w_up], across), *halves([w_down], across))

    via_y, via_x, own_core, segment_other, keep_pair, give_pair, keep_down, give_down = line.run(
        open_second, tokens, segment_ids, upper_y, w_ffgate, w_up, w_down
    )

    def open_third(tokens, via_y, via_x, own_core, keep_down, give_down):
        steps = relay(tokens, via_y, via_x, own_core, place, gain_attn, True)
        return (rows_of(keep_down, flip(give_down, "x")), *steps)

    down_rows, *steps, target, inverse1 = line.run(
        open_third, tokens, via_y, via_x, own_core, keep_down, give_down
    )
    down_weight = weight_gather(down_rows)

    def open_fourth(grad_out_low, segment_ids, segment_other, *steps):
        via_out = direct(grad_out_low)
        hidden1 = diagonal(*steps, place, gain_attn, True)
        segments = jnp.stack([segment_ids, segment_other])
        cosine, sine, first = jax.vmap(partial(row_tables, head_dim=head_dim))(segments)
        cosine = cosine.reshape(2 * count, head_dim)
        sine = sine.reshape(2 * count, head_dim)
        return (hidden1, cosine, sine, first, *via_out)

    hidden1, cosine, sine, first, *via_out = line.run(
        open_fourth, grad_out_low, segment_ids, segment_other, *steps, target
    )
    out_column = joint_width // query_width

    def attend(hidden1, first_weight, keep_pair, give_pair, via_y, via_x):
        steps = relay_flips(via_y, via_x)
        got_pair = flip(give_pair, "x")
        joint = dot_in(hidden1, first_weight, joint_width)
        mixed, *kept = attend_fwd(
            joint, cosine, sine, first, gain_query, gain_key, heads, count
        )
        return (rows_of(keep_pair, got_pair), joint, mixed, *kept, *steps)

    out_y, out_x, out_core = via_out
    pair_rows, joint, mixed, *rest = line.run(
        attend, hidden1, first_weight, keep_pair, give_pair, out_y, out_x
    )
    kept, steps = rest[:4], rest[4:]
    pair_weight = weight_gather(pair_rows)
    near_got, far_got = line.run(
        lambda m, w: fold_swap(m, w, place, out_column), mixed, first_weight
    )
    sums = line.run(
        lambda *v: fold_held(v[0], v[1], place, *v[2:], out_column),
        mixed, first_weight, near_got, far_got,
    )

    def cross_out(grad_out_low, own_core, via_y, y_core, via_x, x_core, upper, lower, *sums):
        crossing = fold_cross(*sums)
        near = (grad_out_low, own_core, via_y, y_core)
        target = pack(near, place, gain_ffn, False, 0, None)[0]
        return (
            *crossing,
            diagonal(via_x, x_core, upper, lower, target, place, gain_ffn, False),
        )

    *sums, grad_out_full = line.run(cross_out, grad_out_low, out_core, out_y, *steps, *sums)
    ends = line.run(fold_close, *sums)

    def residual(values, *ends):
        total = values.astype(jnp.float32) + fold_end(*ends)
        return (total, total.astype(low))

    resid, resid_low = line.run(residual, tokens, *ends)

    def start_resid(resid_low, grad_out_full, down_weight):
        return (*direct(resid_low), dot_in(grad_out_full, down_weight, hidden_width))

    *via_resid, grad_act = line.run(start_resid, resid_low, grad_out_full, down_weight)
    *steps, target, inverse2 = line.run(
        lambda *v: relay(*v, place, gain_ffn, True), resid_low, *via_resid
    )
    hidden2 = line.run(lambda *v: diagonal(*v, place, gain_ffn, True), *steps, target)
    activated, grad_pair = line.run(ffn, hidden2, pair_weight, grad_act)


    def sent_pair(hidden2, grad_pair, pair_weight):
        return (
            *fold_swap(grad_pair, pair_weight, place),
            dot_grad(hidden2, grad_pair, hidden_width),
        )

    near_got, far_got, gate_grad = line.run(sent_pair, hidden2, grad_pair, pair_weight)
    gate_sum = grad_scatter(gate_grad)
    sums = line.run(
        lambda *v: fold_held(v[0], v[1], place, *v[2:]), grad_pair, pair_weight, near_got, far_got
    )

    def cross_pair(hidden2, grad_pair, activated, down_weight, *sums):
        return (
            *fold_cross(*sums),
            dot_grad(hidden2, grad_pair, hidden_width, 1),
            *fold_sent(activated, down_weight, place),
        )

    *sums, up_grad, near_ffn, far_ffn = line.run(
        cross_pair, hidden2, grad_pair, activated, down_weight, *sums
    )
    up_sum = grad_scatter(up_grad)

    def close_pair(near_ffn, far_ffn, *sums):
        return (*fold_close(*sums), flip(near_ffn, "core"), flip(far_ffn, "core"))

    *ends, near_got, far_got = line.run(close_pair, near_ffn, far_ffn, *sums)

    def partial_dots(grad_own, values, inverse, gain_own):
        dots = jnp.sum(grad_own * gain_own * values.astype(jnp.float32) * inverse, axis=1)
        dots = dots.reshape(-1, 128)
        dots = dots + flip(dots, "core")
        return dots + flip(dots, "y")

    def norm_back(grad_own, values, inverse, gain_own, dots, extra):
        unit = values.astype(jnp.float32) * inverse
        dots = dots.reshape(-1, 1) / width
        grad_input = inverse * (grad_own * gain_own - unit * dots) + extra
        return (grad_input, grad_input.astype(low))

    def gain_part(grad_own, values, inverse):
        return jnp.sum(grad_own * (values.astype(jnp.float32) * inverse), axis=0).reshape(-1, 128)

    def back_dots(values, inverse, gain_own, *ends):
        grad_own = fold_end(*ends)
        return (
            grad_own,
            partial_dots(grad_own, values, inverse, gain_own),
            gain_part(grad_own, values, inverse),
        )

    grad_hidden2, dots, gain_ffn_grad = line.run(
        back_dots, resid_low, inverse2, gain_ffn_own, *ends
    )
    grad_resid, grad_branch = line.run(
        norm_back, grad_hidden2, resid_low, inverse2, gain_ffn_own, dots, grad_out
    )

    def start_branch(grad_branch, grad_out_full, activated, down_weight, near_got, far_got):
        return (
            *direct(grad_branch),
            dot_grad(grad_out_full, activated),
            *fold_held(activated, down_weight, place, near_got, far_got),
        )

    via_y, via_x, own_core, down_grad, *sums_ffn = line.run(
        start_branch, grad_branch, grad_out_full, activated, down_weight, near_got, far_got
    )
    down_sum = grad_scatter(down_grad)
    gate_sum, = line.enter(gate_sum)
    steps = line.run(
        lambda *v: relay(*v, place, gain_ffn, False), grad_branch, via_y, via_x, own_core
    )

    def mix_back(gate_sum, first_weight, *steps):
        got_gate = flip(give_rows(gate_sum, across), "x")
        grad_branch_full = diagonal(*steps, place, gain_ffn, False)
        return (
            got_gate,
            grad_branch_full,
            dot_in(grad_branch_full, first_weight, query_width, out_column),
        )

    got_gate, grad_branch_full, grad_mixed = line.run(mix_back, gate_sum, first_weight, *steps)
    up_sum, = line.enter(up_sum)

    def attend_back(joint, grad_mixed, grad_branch_full, mixed, *sums):
        grad_joint, head_gains = attend_bwd(
            joint, cosine, sine, first, gain_query, gain_key, kept, grad_mixed, count
        )
        last_grads = dot_grad_part(
            grad_branch_full, mixed, joint_width + query_width, out_column
        )
        return (grad_joint, head_gains, last_grads, *fold_cross(*sums))

    grad_joint, head_gains, last_grads, *sums_ffn = line.run(
        attend_back, joint, grad_mixed, grad_branch_full, mixed, *sums_ffn
    )

    def sent_attn(hidden1, grad_joint, first_weight, last_grads, up_sum):
        return (
            *fold_swap(grad_joint, first_weight, place),
            dot_grad_part(hidden1, grad_joint, last_grads.shape[1], 0, last_grads),
            flip(give_rows(up_sum, across), "x"),
        )

    near_got, far_got, last_grads, got_up = line.run(
        sent_attn, hidden1, grad_joint, first_weight, last_grads, up_sum
    )
    attn_sum = grad_scatter(last_grads)
    down_sum, = line.enter(down_sum)

    def held_attn(grad_joint, first_weight, near_got, far_got, gain_ffn_grad, head_gains, *sums):
        early = jnp.concatenate([gain_ffn_grad, head_gains], axis=0)
        early = early + flip(early, "x")
        return (
            early,
            *fold_held(grad_joint, first_weight, place, near_got, far_got),
            *fold_close(*sums),
        )

    early, *sums = line.run(
        held_attn, grad_joint, first_weight, near_got, far_got, gain_ffn_grad, head_gains, *sums_ffn
    )
    sums, ends_ffn = sums[:4], sums[4:]

    def join(rows, got, low_cut, high_cut):
        keep = keep_rows(rows, across)[:, low_cut:high_cut]
        got = got[:, low_cut:high_cut]
        first, second = jnp.where(across == 0, keep, got), jnp.where(across == 0, got, keep)
        return jnp.concatenate([first, second], axis=1).astype(jnp.float32)

    def join_all(rows, got):
        return join(rows, got, 0, rows.shape[1])

    def cross_attn(early, resid, gate_sum, got_gate, *values):
        sums = fold_cross(*values[:4])
        output = (live * (resid + fold_end(*values[4:]))).astype(low)
        return (
            early + z_flip(early, 1),
            output,
            join_all(gate_sum, got_gate),
            *sums,
        )

    early, output, ffgate_grad, *sums = line.run(
        cross_attn, early, resid, gate_sum, got_gate, *sums, *ends_ffn
    )

    def close_attn(early, up_sum, got_up, *sums):
        return (early + z_flip(early, 2), join_all(up_sum, got_up), *fold_close(*sums))

    early, up_grad, *ends = line.run(close_attn, early, up_sum, got_up, *sums)

    def last_dots(tokens, inverse1, down_sum, *ends):
        got_down = flip(give_rows(down_sum, across), "x")
        grad_own = fold_end(*ends)
        late = gain_part(grad_own, tokens, inverse1)
        late = late + z_flip(late, 1)
        return (
            got_down,
            grad_own,
            partial_dots(grad_own, tokens, inverse1, gain_attn_own),
            late + z_flip(late, 2),
        )

    got_down, grad_hidden1, dots, late = line.run(last_dots, tokens, inverse1, down_sum, *ends)
    cuts = (
        0,
        query_width,
        2 * query_width,
        2 * query_width + key_width,
        2 * query_width + 2 * key_width,
    )

    blocks = local // 128

    def last_spot(late, early):
        own = jnp.stack([late, early[:blocks]])
        spot = lax.dynamic_update_slice_in_dim(
            jnp.zeros((2, width // 128, 128), jnp.float32), own, offset // 128, 1
        ).reshape(-1, 128)
        spot = jnp.concatenate([spot, early[blocks:]], axis=0)
        spot = spot + flip(spot, "core")
        return spot + flip(spot, "y")

    def last_norm(
        grad_hidden1, tokens, inverse1, dots, grad_resid, late, early, attn_sum, down_sum, got_down
    ):
        got_attn = flip(give_rows(attn_sum, across), "x")
        spot = last_spot(late + flip(late, "x"), early)
        grad_tokens, unused = norm_back(
            grad_hidden1, tokens, inverse1, gain_attn_own, dots, grad_resid
        )
        return (got_attn, spot, grad_tokens, join_all(down_sum, got_down))

    got_attn, spot, grad_tokens, down_part = line.run(
        last_norm, grad_hidden1, tokens, inverse1, dots, grad_resid, late, early, attn_sum,
        down_sum, got_down
    )
    widths = (query_width, query_width, key_width, key_width, query_width)
    *attn_parts, out_part = line.run(
        lambda sums, got: join_parts(sums, got, across, widths), attn_sum, got_attn
    )
    lines = width // 128
    return (
        output,
        grad_tokens,
        spot[:lines].reshape(width),
        spot[lines : 2 * lines].reshape(width),
        spot[2 * lines] + line.token[0],
        spot[2 * lines + 1],
        *attn_parts,
        out_part,
        ffgate_grad,
        up_grad,
        down_part,
    )


def solution(mesh):
    rows, columns = mesh.devices.shape

    def run(*args):
        head_dim = args[5].shape[0]
        query_width, key_width = args[7].shape[1], args[9].shape[1]
        one_key_head = key_width == 2 * columns * head_dim and query_width % key_width == 0
        if not (rows == 8 and columns == 4 and one_key_head):
            return plain(mesh)(*args)
        names = ("z", "x", "y", "core")
        inner = Mesh(mesh.devices.reshape(4, 2, 2, 2), names)
        block = P(("z", "x"), ("y", "core"))
        whole = P()
        in_specs = (block, block, P(("z", "x"))) + (whole,) * 4 + (block,) * 8
        out_specs = (block, block) + (whole,) * 4 + (block,) * 8
        return jax.shard_map(
            fast_body, mesh=inner, in_specs=in_specs, out_specs=out_specs, check_vma=False
        )(*args)

    return run
```

```python
from functools import partial

import jax
import jax.numpy as jnp
from jax import lax
from jax.experimental import pallas as pl
from jax.experimental.pallas import tpu as pltpu
from jax.sharding import Mesh
from jax.sharding import PartitionSpec as P

eps_norm = 1e-06
rope_base = 1000000.0


def norm_rows(values, gain):
    inverse = lax.rsqrt(jnp.mean(values * values, axis=-1, keepdims=True) + eps_norm)
    return (values * inverse * gain, inverse)


def rope_tables(segments, head_dim):
    count = segments.shape[0]
    index = jnp.arange(count, dtype=jnp.int32)
    previous = jnp.concatenate([jnp.full((1,), -1, jnp.int32), segments[:-1]])
    starts = lax.cummax(jnp.where(segments != previous, index, 0), axis=0)
    position = (index - starts).astype(jnp.float32)
    half = head_dim // 2
    freqs = jnp.power(rope_base, -(jnp.arange(half, dtype=jnp.float32) * 2.0 / head_dim))
    angle = position[:, None] * freqs[None, :]
    angle = jnp.concatenate([angle, angle], axis=1)
    return (jnp.cos(angle), jnp.sin(angle))


def attend_mask(segments):
    count = segments.shape[0]
    index = jnp.arange(count, dtype=jnp.int32)
    earlier = index[None, :] < index[:, None]
    same = (segments[None, :] == segments[:, None]) & (segments[None, :] > 0)
    return (index[None, :] == index[:, None]) | earlier & same


def head_prepare(raw, gain, cosine, sine):
    count = raw.shape[0]
    head_dim = gain.shape[0]
    heads = raw.reshape(count, -1, head_dim)
    inverse = lax.rsqrt(jnp.mean(heads * heads, axis=-1, keepdims=True) + eps_norm)
    normed = heads * inverse * gain
    half = head_dim // 2
    turned = jnp.concatenate([-normed[..., half:], normed[..., :half]], axis=-1)
    return (normed * cosine[:, None, :] + turned * sine[:, None, :]).reshape(count, -1)


def feature_gather(values):
    return lax.all_gather(values, "col", axis=1, tiled=True)


def feature_sum(values):
    return lax.psum_scatter(
        values.astype(jnp.bfloat16), "col", scatter_dimension=1, tiled=True
    ).astype(jnp.float32)


def rows_in(operand, weight):
    return jnp.dot(
        operand,
        lax.all_gather(weight, "row", axis=0, tiled=True),
        preferred_element_type=jnp.float32,
    )


def rows_out(operand, weight):
    return lax.dot_general(
        operand,
        lax.all_gather(weight, "row", axis=0, tiled=True),
        (((1,), (1,)), ((), ())),
        preferred_element_type=jnp.float32,
    )


def weight_grads(firsts, seconds):
    blocks = []
    for first, second in zip(firsts, seconds):
        blocks.append(
            lax.dot_general(
                first, second, (((0,), (0,)), ((), ())), preferred_element_type=jnp.float32
            )
        )
    return lax.psum_scatter(
        jnp.concatenate(blocks, axis=1).astype(jnp.bfloat16), "row", scatter_dimension=0, tiled=True
    ).astype(jnp.float32)


def norm_back(partial_grad, unit, inverse, gain, local):
    offset = lax.axis_index("col") * local
    width = unit.shape[1]
    unit_own = lax.dynamic_slice_in_dim(unit, offset, local, 1)
    grad_own = feature_sum(partial_grad)
    gain_own = lax.dynamic_slice_in_dim(gain, offset, local, 0)
    scaled = grad_own * gain_own
    dots = lax.psum(jnp.sum(scaled * unit_own, axis=1), "col")[:, None] / width
    grad_input = inverse * (scaled - unit_own * dots)
    gain_grad = lax.dynamic_update_slice_in_dim(
        jnp.zeros((width,), jnp.float32), jnp.sum(grad_own * unit_own, axis=0), offset, 0
    )
    return (grad_input, gain_grad)


def attend_scores(query, keys, allowed, kv_heads, head_dim):
    count = query.shape[0]
    grouped = query.reshape(count, kv_heads, -1, head_dim)
    keyed = keys.reshape(count, kv_heads, head_dim)
    scores = jnp.einsum(
        "qgrd,kgd->grqk", grouped, keyed, preferred_element_type=jnp.float32
    ) * head_dim ** (-0.5)
    return (jnp.where(allowed, scores, -1e30), grouped, keyed)


def attend_forward(query, keys, values, allowed, kv_heads, head_dim):
    count = query.shape[0]
    scores, grouped, keyed = attend_scores(query, keys, allowed, kv_heads, head_dim)
    peak = jnp.max(scores, axis=-1, keepdims=True)
    weights = jnp.exp(scores - peak)
    total = jnp.sum(weights, axis=-1, keepdims=True)
    probs = (weights / total).astype(jnp.bfloat16)
    valued = values.reshape(count, kv_heads, head_dim)
    attended = jnp.einsum("grqk,kgd->qgrd", probs, valued, preferred_element_type=jnp.float32)
    return (attended.reshape(count, -1), peak + jnp.log(total))


def attend_backward(query, keys, values, allowed, logsum, grad_attended, kv_heads, head_dim):
    count = query.shape[0]
    scores, grouped, keyed = attend_scores(query, keys, allowed, kv_heads, head_dim)
    probs_exact = jnp.exp(scores - logsum)
    probs = probs_exact.astype(jnp.bfloat16)
    valued = values.reshape(count, kv_heads, head_dim)
    grad_grouped = grad_attended.reshape(count, kv_heads, -1, head_dim)
    grad_values = jnp.einsum(
        "grqk,qgrd->kgd", probs, grad_grouped, preferred_element_type=jnp.float32
    )
    grad_probs = jnp.einsum(
        "qgrd,kgd->grqk", grad_grouped, valued, preferred_element_type=jnp.float32
    )
    delta = jnp.sum(probs_exact * grad_probs, axis=-1, keepdims=True)
    grad_scores = (probs_exact * (grad_probs - delta)).astype(jnp.bfloat16)
    grad_query = jnp.einsum(
        "grqk,kgd->qgrd", grad_scores, keyed, preferred_element_type=jnp.float32
    ) * head_dim ** (-0.5)
    grad_keys = jnp.einsum(
        "grqk,qgrd->kgd", grad_scores, grouped, preferred_element_type=jnp.float32
    ) * head_dim ** (-0.5)
    return (
        grad_query.reshape(count, -1),
        grad_keys.reshape(count, -1),
        grad_values.reshape(count, -1).astype(jnp.bfloat16),
    )


def body(
    tokens,
    cotangent,
    segment_ids,
    gain_attn,
    gain_ffn,
    gain_query,
    gain_key,
    w_query,
    w_gate,
    w_key,
    w_value,
    w_out,
    w_ffgate,
    w_up,
    w_down,
):
    local = tokens.shape[1]
    head_dim = gain_query.shape[0]
    query_width = w_query.shape[1]
    key_width = w_key.shape[1]
    kv_heads = key_width // head_dim
    hidden_width = w_ffgate.shape[1]
    live = (segment_ids > 0).astype(jnp.float32)[:, None]
    cosine, sine = rope_tables(segment_ids, head_dim)
    allowed = attend_mask(segment_ids)
    attn_weight = jnp.concatenate([w_query, w_gate, w_key, w_value], axis=1)
    ffn_weight = jnp.concatenate([w_ffgate, w_up], axis=1)
    blocks = (attn_weight, ffn_weight, w_out, w_down)

    def apply_in(operand, which_block):
        return rows_in(operand, blocks[which_block])

    def apply_out(operand, which_block):
        return rows_out(operand, blocks[which_block])

    inputs = feature_gather(tokens).astype(jnp.float32)
    normed1, inverse1 = norm_rows(inputs, gain_attn)
    hidden1 = normed1.astype(jnp.bfloat16)
    joint = apply_in(hidden1, 0)
    query_raw = joint[:, :query_width]
    gate_raw = joint[:, query_width : 2 * query_width]
    key_raw = joint[:, 2 * query_width : 2 * query_width + key_width]
    values = joint[:, 2 * query_width + key_width :].astype(jnp.bfloat16)
    prepare = partial(head_prepare, cosine=cosine, sine=sine)
    query = prepare(query_raw, gain_query).astype(jnp.bfloat16)
    keys = prepare(key_raw, gain_key).astype(jnp.bfloat16)
    attended, logsum = attend_forward(query, keys, values, allowed, kv_heads, head_dim)
    gate_sig = jax.nn.sigmoid(gate_raw)
    mixed = (attended * gate_sig).astype(jnp.bfloat16)
    resid = tokens.astype(jnp.float32) + feature_sum(apply_out(mixed, 2))
    resid_full = feature_gather(resid.astype(jnp.bfloat16)).astype(jnp.float32)
    normed2, inverse2 = norm_rows(resid_full, gain_ffn)
    hidden2 = normed2.astype(jnp.bfloat16)
    ffn_joint = apply_in(hidden2, 1)
    ff_gate = ffn_joint[:, :hidden_width]
    ff_up = ffn_joint[:, hidden_width:]
    sig_gate = jax.nn.sigmoid(ff_gate)
    activated = (jax.nn.silu(ff_gate) * ff_up).astype(jnp.bfloat16)
    ffn_out = feature_sum(apply_out(activated, 3))
    output = (live * (resid + ffn_out)).astype(jnp.bfloat16)
    grad_out = live * cotangent.astype(jnp.float32)
    grad_ffn_full = feature_gather(grad_out.astype(jnp.bfloat16))
    grad_act = apply_in(grad_ffn_full, 3)
    grad_ffup = (grad_act * (ff_gate * sig_gate)).astype(jnp.bfloat16)
    grad_ffgate = (grad_act * ff_up * sig_gate * (1.0 + ff_gate * (1.0 - sig_gate))).astype(
        jnp.bfloat16
    )
    grad_pair = jnp.concatenate([grad_ffgate, grad_ffup], axis=1)
    ffn_grads = weight_grads((hidden2, grad_ffn_full), (grad_pair, activated))
    grad_input2, gain_ffn_grad = norm_back(
        apply_out(grad_pair, 1), resid_full * inverse2, inverse2, gain_ffn, local
    )
    grad_resid = grad_out + grad_input2
    grad_branch_full = feature_gather(grad_resid.astype(jnp.bfloat16))
    grad_mixed = apply_in(grad_branch_full, 2)
    grad_attended = (grad_mixed * gate_sig).astype(jnp.bfloat16)
    grad_gate_raw = (grad_mixed * attended * gate_sig * (1.0 - gate_sig)).astype(jnp.bfloat16)
    grad_query, grad_keys, grad_values = attend_backward(
        query, keys, values, allowed, logsum, grad_attended, kv_heads, head_dim
    )
    unused_query, query_back = jax.vjp(prepare, query_raw, gain_query)
    grad_query_raw, grad_gain_query = query_back(grad_query)
    unused_key, key_back = jax.vjp(prepare, key_raw, gain_key)
    grad_key_raw, grad_gain_key = key_back(grad_keys)
    grad_joint = jnp.concatenate(
        [
            grad_query_raw.astype(jnp.bfloat16),
            grad_gate_raw,
            grad_key_raw.astype(jnp.bfloat16),
            grad_values,
        ],
        axis=1,
    )
    attn_grads = weight_grads((hidden1, grad_branch_full), (grad_joint, mixed))
    grad_input1, gain_attn_grad = norm_back(
        apply_out(grad_joint, 0), inputs * inverse1, inverse1, gain_attn, local
    )
    grad_tokens = grad_resid + grad_input1
    gains = lax.psum(
        (gain_attn_grad, gain_ffn_grad, grad_gain_query, grad_gain_key), ("row", "col")
    )
    second_cut = 2 * query_width
    third_cut = 2 * query_width + key_width
    fourth_cut = 2 * query_width + 2 * key_width
    return (
        output,
        grad_tokens,
        gains[0],
        gains[1],
        gains[2],
        gains[3],
        attn_grads[:, :query_width],
        attn_grads[:, query_width:second_cut],
        attn_grads[:, second_cut:third_cut],
        attn_grads[:, third_cut:fourth_cut],
        attn_grads[:, fourth_cut:],
        ffn_grads[:, :hidden_width],
        ffn_grads[:, hidden_width : 2 * hidden_width],
        ffn_grads[:, 2 * hidden_width :],
    )


def plain(mesh):
    in_specs = (
        P("row", "col"),
        P("row", "col"),
        P("row"),
        P(),
        P(),
        P(),
        P(),
        P("row", "col"),
        P("row", "col"),
        P("row", "col"),
        P("row", "col"),
        P("row", "col"),
        P("row", "col"),
        P("row", "col"),
        P("row", "col"),
    )
    out_specs = (
        P("row", "col"),
        P("row", "col"),
        P(),
        P(),
        P(),
        P(),
        P("row", "col"),
        P("row", "col"),
        P("row", "col"),
        P("row", "col"),
        P("row", "col"),
        P("row", "col"),
        P("row", "col"),
        P("row", "col"),
    )
    return jax.shard_map(body, mesh=mesh, in_specs=in_specs, out_specs=out_specs, check_vma=False)


def tie(*values):
    return lax.optimization_barrier(values)


def flip(values, axis):
    return lax.ppermute(values, axis, [(0, 1), (1, 0)])


light = pl.CostEstimate(flops=0, bytes_accessed=0, transcendentals=0)


heavy = light


class Line:
    def __init__(self):
        self.token = jnp.zeros((8, 128), jnp.float32)

    def enter(self, *values):
        *values, self.token = lax.optimization_barrier((*values, self.token))
        return values

    def run(self, work, *values):
        result = work(*self.enter(*values))
        if isinstance(result, (tuple, list)):
            return self.enter(*result)
        return self.enter(result)[0]


def pack_kernel(normed, place_ref, gain_ref, *refs):
    blocks, out_ref = refs[:4], refs[5]
    width = blocks[0].shape[1]
    place = place_ref[0]
    if normed:
        values = [block[...].astype(jnp.float32) for block in blocks]
        squares = sum(jnp.sum(v * v, axis=1, keepdims=True) for v in values)
        inverse = lax.rsqrt(squares / (4 * width) + eps_norm)
        refs[6][...] = inverse
    for index in range(4):
        columns = pl.ds(pl.multiple_of((place ^ index) * width, width), width)
        if normed:
            result = values[index] * inverse * gain_ref[:, columns]
            out_ref[:, columns] = result.astype(out_ref.dtype)
        else:
            out_ref[:, columns] = blocks[index][...]


def pack(blocks, place, gain, normed, step, target):
    count, width = blocks[0].shape
    tile = 256
    tiles = count // tile
    out_shape = [jax.ShapeDtypeStruct((2 * count, 4 * width), jnp.bfloat16)]
    out_specs = [pl.BlockSpec((tile, 4 * width), lambda i: (i + step * tiles, 0))]
    if normed:
        out_shape.append(jax.ShapeDtypeStruct((count, 1), jnp.float32))
        out_specs.append(pl.BlockSpec((tile, 1), lambda i: (i, 0)))
    aliases = {}
    if target is None:
        target = place.reshape(1)
    else:
        aliases = {6: 0}
    return pl.pallas_call(
        partial(pack_kernel, normed),
        grid=(tiles,),
        in_specs=[
            pl.BlockSpec(memory_space=pltpu.SMEM),
            pl.BlockSpec((1, 4 * width), lambda i: (0, 0)),
        ]
        + [pl.BlockSpec((tile, width), lambda i: (i, 0))] * 4
        + [pl.BlockSpec(memory_space=pl.ANY if aliases else pltpu.SMEM)],
        out_specs=out_specs,
        out_shape=out_shape,
        input_output_aliases=aliases,
        cost_estimate=light,
    )(place.reshape(1), gain.reshape(1, -1), *blocks, target)


def direct(own):
    return (flip(own, "y"), flip(own, "x"), flip(own, "core"))


def cut_kernel(first_ref, second_ref, upper_ref, lower_ref):
    upper_ref[...] = first_ref[...]
    lower_ref[...] = second_ref[...]


def cut_halves(first, second):
    half, width = first.shape[0] // 2, first.shape[1]
    tile = half // 2
    shape = jax.ShapeDtypeStruct((half, width), first.dtype)
    out = pl.BlockSpec((tile, width), lambda i: (i, 0))
    return pl.pallas_call(
        cut_kernel,
        grid=(2,),
        in_specs=[out, pl.BlockSpec((tile, width), lambda i: (i + 2, 0))],
        out_specs=[out, out],
        out_shape=[shape, shape],
        cost_estimate=light,
    )(first, second)


def relay_flips(via_y, via_x):
    upper, lower = cut_halves(via_y, via_x)
    upper, lower = flip(upper, "x"), flip(lower, "y")
    return (flip(via_y, "core"), via_x, flip(via_x, "core"), upper, lower)


def relay(own, via_y, via_x, own_core, place, gain, normed):
    y_core, *steps = relay_flips(via_y, via_x)
    return (*steps, *pack((own, own_core, via_y, y_core), place, gain, normed, 0, None))


def diagonal(via_x, x_core, upper, lower, target, place, gain, normed):
    crossed = jnp.concatenate([upper, lower], axis=0)
    far = (via_x, x_core, crossed, flip(crossed, "core"))
    return pack(far, place, gain, normed, 1, target)[0]


def halves_kernel(count, across_ref, *refs):
    across = across_ref[0]
    keep_ref, give_ref = refs[count:]
    at = 0
    for weight_ref in refs[:count]:
        width = weight_ref.shape[1] // 2
        for target, side in ((keep_ref, across), (give_ref, 1 - across)):
            target[:, at : at + width] = weight_ref[:, pl.ds(pl.multiple_of(side * width, width), width)]
        at += width


def halves(weights, across):
    rows = weights[0].shape[0]
    width = sum(weight.shape[1] for weight in weights) // 2
    shape = jax.ShapeDtypeStruct((rows, width), jnp.bfloat16)
    whole = pl.BlockSpec(memory_space=pltpu.VMEM)
    return pl.pallas_call(
        partial(halves_kernel, len(weights)),
        in_specs=[pl.BlockSpec(memory_space=pltpu.SMEM)] + [whole] * len(weights),
        out_specs=[whole, whole],
        out_shape=[shape, shape],
        cost_estimate=light,
    )(across.reshape(1), *weights)


def weight_rows(keep, got, across):
    top = jnp.where(across == 0, keep, got)
    bottom = jnp.where(across == 0, got, keep)
    return jnp.concatenate([top, bottom], axis=0)


def weight_gather(rows):
    return lax.all_gather(rows, "z", axis=0, tiled=True)


def grad_scatter(grads):
    return lax.psum_scatter(grads, "z", scatter_dimension=0, tiled=True)


def keep_rows(summed, across):
    rows = summed.shape[0] // 2
    return lax.dynamic_slice_in_dim(summed, across * rows, rows, 0)


def give_rows(summed, across):
    return keep_rows(summed, 1 - across)


def z_flip(values, step):
    return lax.ppermute(values, "z", [(i, i ^ step) for i in range(4)])


vmem = pltpu.CompilerParams(vmem_limit_bytes=56 * 1024 * 1024)


def join_kernel(widths, across_ref, sums_ref, got_ref, *out_refs):
    across = across_ref[0]
    rows = got_ref.shape[0]
    keep = pl.ds(pl.multiple_of(across * rows, rows), rows)
    at = 0
    for width, out_ref in zip(widths, out_refs):
        own = pl.ds(pl.multiple_of(across * width, width), width)
        other = pl.ds(pl.multiple_of((1 - across) * width, width), width)
        out_ref[:, own] = sums_ref[keep, at : at + width].astype(jnp.float32)
        out_ref[:, other] = got_ref[:, at : at + width].astype(jnp.float32)
        at += width


def join_parts(sums, got, across, widths):
    rows = got.shape[0]
    whole = pl.BlockSpec(memory_space=pltpu.VMEM)
    return pl.pallas_call(
        partial(join_kernel, widths),
        in_specs=[pl.BlockSpec(memory_space=pltpu.SMEM), whole, whole],
        out_specs=[whole] * len(widths),
        out_shape=[jax.ShapeDtypeStruct((rows, 2 * width), jnp.float32) for width in widths],
        compiler_params=vmem,
        cost_estimate=light,
    )(across.reshape(1), sums, got)


def fold_turn(near_ref, far_ref, turned):
    rows = near_ref.shape[0]

    @pl.when(pl.program_id(0) == 0)
    def turn():
        turned[:, :rows] = near_ref[...].T
        turned[:, rows:] = far_ref[...].T


def fold_sent_kernel(place_ref, operand_ref, near_ref, far_ref, near_out, far_out, turned):
    fold_turn(near_ref, far_ref, turned)
    rows = near_out.shape[1]
    both = product_nn(operand_ref[...], turned[...]).astype(near_out.dtype)
    near_out[...] = both[:, :rows]
    far_out[...] = both[:, rows:]


def fold_held_kernel(
    place_ref, operand_ref, near_ref, far_ref, near_got, far_got,
    upper_send, upper_keep, lower_send, lower_keep, turned,
):
    fold_turn(near_ref, far_ref, turned)
    low = upper_send.dtype
    rows = near_got.shape[1]
    both = product_nn(operand_ref[...], turned[...])
    near = (both[:, :rows] + near_got[...].astype(jnp.float32)).astype(low)
    far = (both[:, rows:] + far_got[...].astype(jnp.float32)).astype(low)
    step = pl.program_id(0)

    @pl.when(step == 0)
    def first():
        upper_send[0] = near
        upper_send[1] = far

    @pl.when(step == 1)
    def second():
        upper_keep[0] = near
        upper_keep[1] = far

    @pl.when(step >= 2)
    def third():
        lower_send[...] = far
        lower_keep[...] = near


def fold_rows(i):
    return (1 - i % 2) * 2 + i // 2


def fold_specs(tile, width, rows, column, near, far):
    return [
        pl.BlockSpec((tile, width), lambda i, p: (fold_rows(i), 0)),
        pl.BlockSpec((rows, width), lambda i, p: (p[0] ^ near, column)),
        pl.BlockSpec((rows, width), lambda i, p: (p[0] ^ far, column)),
    ]


def fold_sent(operand, weight, place, column=0):
    count, width = operand.shape
    rows, tile = weight.shape[0] // 4, count // 4
    out = pl.BlockSpec((tile, rows), lambda i, p: (fold_rows(i), 0))
    near, far = pl.pallas_call(
        fold_sent_kernel,
        grid_spec=pltpu.PrefetchScalarGridSpec(
            num_scalar_prefetch=1,
            grid=(4,),
            in_specs=fold_specs(tile, width, rows, column, 1, 3),
            out_specs=[out, out],
            scratch_shapes=[pltpu.VMEM((width, 2 * rows), jnp.bfloat16)],
        ),
        out_shape=[jax.ShapeDtypeStruct((count, rows), jnp.bfloat16)] * 2,
        compiler_params=vmem,
        cost_estimate=light,
    )(place.reshape(1), operand, weight, weight)
    return (near, far)


def fold_swap(operand, weight, place, column=0):
    return tuple(flip(v, "core") for v in fold_sent(operand, weight, place, column))


def fold_held(operand, weight, place, near_got, far_got, column=0):
    count, width = operand.shape
    rows, tile = weight.shape[0] // 4, count // 4
    got = pl.BlockSpec((tile, rows), lambda i, p: (fold_rows(i), 0))
    whole = pl.BlockSpec((2, tile, rows), lambda i, p: (0, 0, 0))
    late = pl.BlockSpec((tile, rows), lambda i, p: (jnp.where(i < 3, 1, 0), 0))
    shape = jax.ShapeDtypeStruct
    return pl.pallas_call(
        fold_held_kernel,
        grid_spec=pltpu.PrefetchScalarGridSpec(
            num_scalar_prefetch=1,
            grid=(4,),
            in_specs=fold_specs(tile, width, rows, column, 0, 2) + [got, got],
            out_specs=[whole, whole, late, late],
            scratch_shapes=[pltpu.VMEM((width, 2 * rows), jnp.bfloat16)],
        ),
        out_shape=[shape((2, tile, rows), jnp.bfloat16)] * 2
        + [shape((2 * tile, rows), jnp.bfloat16)] * 2,
        compiler_params=vmem,
        cost_estimate=light,
    )(place.reshape(1), operand, weight, weight, near_got, far_got)


def fold_cross(upper_send, upper_keep, lower_send, lower_keep):
    return (flip(upper_send, "x"), upper_keep, flip(lower_send, "y"), lower_keep)


def fold_close_kernel(
    upper_ref, upper_keep, own_ref, own_keep, other_ref, other_keep,
    upper_near, upper_far, lower_own, lower_other,
):
    wide = lambda ref: ref[...].astype(jnp.float32)
    total = wide(upper_ref) + wide(upper_keep)
    upper_near[...] = total[0]
    upper_far[...] = total[1].astype(upper_far.dtype)
    lower_own[...] = wide(own_ref) + wide(own_keep)
    lower_other[...] = (wide(other_ref) + wide(other_keep)).astype(lower_other.dtype)


def fold_close(upper, upper_keep, lower, lower_keep):
    count, rows = upper.shape[1:]
    tile = count // 2
    pair = pl.BlockSpec((2, tile, rows), lambda i: (0, i, 0))
    own = pl.BlockSpec((tile, rows), lambda i: (i, 0))
    other = pl.BlockSpec((tile, rows), lambda i: (i + 2, 0))
    shapes = [jax.ShapeDtypeStruct((count, rows), kind) for kind in (jnp.float32, jnp.bfloat16)]
    upper_near, upper_far, lower_own, lower_other = pl.pallas_call(
        fold_close_kernel,
        grid=(2,),
        in_specs=[pair, pair, own, own, other, other],
        out_specs=[own] * 4,
        out_shape=shapes * 2,
        cost_estimate=light,
    )(upper, upper_keep, lower, lower_keep, lower, lower_keep)
    return (upper_near, flip(upper_far, "y"), lower_own, flip(lower_other, "x"))


def fold_end(upper_near, upper_got, lower_own, lower_got):
    return jnp.concatenate([upper_near + upper_got, lower_own + lower_got], axis=0)


def matmul_kernel(form, operand_ref, weight_ref, out_ref):
    out_ref[...] = form(operand_ref[...], weight_ref[...]).astype(out_ref.dtype)


def dot_in(operand, weight, width, column=0):
    count, depth = operand.shape
    tile = 512
    return pl.pallas_call(
        partial(matmul_kernel, product_nn),
        grid=(count // tile,),
        in_specs=[
            pl.BlockSpec((tile, depth), lambda i: (i, 0)),
            pl.BlockSpec((depth, width), lambda i: (0, column)),
        ],
        out_specs=pl.BlockSpec((tile, width), lambda i: (i, 0)),
        out_shape=jax.ShapeDtypeStruct((count, width), jnp.float32),
        compiler_params=vmem,
        cost_estimate=light,
    )(operand, weight)


def dot_grad(first, second, width=None, column=0, cost=light):
    count, rows = first.shape
    width = second.shape[1] if width is None else width
    tile = 512
    return pl.pallas_call(
        partial(matmul_kernel, product_tn),
        grid=(rows // tile,),
        in_specs=[
            pl.BlockSpec((count, tile), lambda i: (0, i)),
            pl.BlockSpec((count, width), lambda i: (0, column)),
        ],
        out_specs=pl.BlockSpec((tile, width), lambda i: (i, 0)),
        out_shape=jax.ShapeDtypeStruct((rows, width), jnp.bfloat16),
        compiler_params=vmem,
        cost_estimate=cost,
    )(first, second)


def dot_grad_part(first, second, whole, column, target=None):
    count, rows = first.shape
    width = second.shape[1]
    tile = 512
    in_specs = [
        pl.BlockSpec((count, tile), lambda i: (0, i)),
        pl.BlockSpec((count, width), lambda i: (0, 0)),
    ]
    kernel, operands, aliases = partial(matmul_kernel, product_tn), (first, second), {}
    if target is not None:
        in_specs.append(pl.BlockSpec(memory_space=pl.ANY))
        operands, aliases = (first, second, target), {2: 0}
        kernel = lambda a, b, unused, out: matmul_kernel(product_tn, a, b, out)
    return pl.pallas_call(
        kernel,
        grid=(rows // tile,),
        in_specs=in_specs,
        out_specs=pl.BlockSpec((tile, width), lambda i: (i, column)),
        out_shape=jax.ShapeDtypeStruct((rows, whole), jnp.bfloat16),
        input_output_aliases=aliases,
        compiler_params=vmem,
        cost_estimate=light,
    )(*operands)


def ffn_kernel(hidden_ref, weight_ref, grad_ref, activated_ref, pair_ref):
    width = activated_ref.shape[1]
    low = jnp.bfloat16
    step = 256
    for at in range(0, width, step):
        ff_gate = product_nn(hidden_ref[...], weight_ref[:, at : at + step])
        ff_up = product_nn(hidden_ref[...], weight_ref[:, width + at : width + at + step])
        grad = grad_ref[:, at : at + step]
        sig_gate = jax.nn.sigmoid(ff_gate)
        passed = ff_gate * sig_gate
        activated_ref[:, at : at + step] = (passed * ff_up).astype(low)
        pair_ref[:, width + at : width + at + step] = (grad * passed).astype(low)
        pair_ref[:, at : at + step] = (
            grad * ff_up * sig_gate * (1.0 + ff_gate * (1.0 - sig_gate))
        ).astype(low)


def ffn(hidden, weight, grad):
    count, depth = hidden.shape
    width = weight.shape[1] // 2
    tile = 256
    return pl.pallas_call(
        ffn_kernel,
        grid=(count // tile,),
        in_specs=[
            pl.BlockSpec((tile, depth), lambda i: (i, 0)),
            pl.BlockSpec((depth, 2 * width), lambda i: (0, 0)),
            pl.BlockSpec((tile, width), lambda i: (i, 0)),
        ],
        out_specs=[
            pl.BlockSpec((tile, width), lambda i: (i, 0)),
            pl.BlockSpec((tile, 2 * width), lambda i: (i, 0)),
        ],
        out_shape=[
            jax.ShapeDtypeStruct((count, width), jnp.bfloat16),
            jax.ShapeDtypeStruct((count, 2 * width), jnp.bfloat16),
        ],
        compiler_params=vmem,
        cost_estimate=light,
    )(hidden, weight, grad)


def row_tables(segments, head_dim):
    count = segments.shape[0]
    index = jnp.arange(count, dtype=jnp.int32)
    previous = jnp.concatenate([jnp.full((1,), -1, jnp.int32), segments[:-1]])
    starts = lax.cummax(jnp.where(segments != previous, index, 0), axis=0)
    position = (index - starts).astype(jnp.float32)
    half = head_dim // 2
    freqs = jnp.power(rope_base, -(jnp.arange(half, dtype=jnp.float32) * 2.0 / head_dim))
    angle = position[:, None] * freqs[None, :]
    cosine, sine = jnp.cos(angle), jnp.sin(angle)
    return (
        jnp.concatenate([cosine, cosine], axis=1),
        jnp.concatenate([-sine, sine], axis=1),
        jnp.where(segments > 0, starts, index)[None, :],
    )


def product_nt(first, second):
    return lax.dot_general(
        first, second, (((1,), (1,)), ((), ())), preferred_element_type=jnp.float32
    )


def product_tn(first, second):
    return lax.dot_general(
        first, second, (((0,), (0,)), ((), ())), preferred_element_type=jnp.float32
    )


def product_nn(first, second):
    return lax.dot_general(
        first, second, (((1,), (0,)), ((), ())), preferred_element_type=jnp.float32
    )


def prepare_tile(raw, gain, cosine, sine):
    inverse = lax.rsqrt(jnp.mean(raw * raw, axis=1, keepdims=True) + eps_norm)
    normed = raw * inverse * gain
    turned = pltpu.roll(normed, raw.shape[1] // 2, 1)
    return (normed * cosine + turned * sine).astype(jnp.bfloat16)


def prepare_back(raw, gain, cosine, sine, grad):
    inverse = lax.rsqrt(jnp.mean(raw * raw, axis=1, keepdims=True) + eps_norm)
    unit = raw * inverse
    grad_normed = grad * cosine + pltpu.roll(grad * sine, raw.shape[1] // 2, 1)
    scaled = grad_normed * gain
    grad_raw = inverse * (scaled - unit * jnp.mean(scaled * unit, axis=1, keepdims=True))
    return (grad_raw.astype(jnp.bfloat16), jnp.sum(grad_normed * unit, axis=0, keepdims=True))


def allowed_tile(first_ref, start, tile, reach):
    rows = lax.broadcasted_iota(jnp.int32, (reach, tile), 0)
    columns = lax.broadcasted_iota(jnp.int32, (reach, tile), 1) + start
    return (rows >= first_ref[0, :, pl.ds(start, tile)]) & (rows <= columns)


def attend_kernel(
    heads, tile, joint_ref, cos_ref, sin_ref, first_ref, gain_query_ref, gain_key_ref,
    mixed_ref, attended_ref, query_ref, key_ref, logsum_ref,
):
    count, head_dim = cos_ref.shape
    scale = head_dim ** (-0.5)
    low = jnp.bfloat16
    key_at = 2 * heads * head_dim
    tiles = count // tile
    for part in range(tiles):
        rows = pl.ds(part * tile, tile)
        key_ref[rows, :] = prepare_tile(
            joint_ref[rows, key_at : key_at + head_dim],
            gain_key_ref[...],
            cos_ref[rows, :],
            sin_ref[rows, :],
        )
    for head in range(heads):
        columns = slice(head * head_dim, (head + 1) * head_dim)
        gates = slice((heads + head) * head_dim, (heads + head + 1) * head_dim)
        for part in range(tiles):
            rows = pl.ds(part * tile, tile)
            reach = (part + 1) * tile
            query = prepare_tile(
                joint_ref[rows, columns], gain_query_ref[...], cos_ref[rows, :], sin_ref[rows, :]
            )
            query_ref[rows, columns] = query
            scores = product_nt(key_ref[:reach, :], query) * scale
            scores = jnp.where(allowed_tile(first_ref, part * tile, tile, reach), scores, -1e30)
            peak = jnp.max(scores, axis=0, keepdims=True)
            weights = jnp.exp(scores - peak)
            total = jnp.sum(weights, axis=0, keepdims=True)
            probs = (weights * (1.0 / total)).astype(low)
            logsum_ref[0, head : head + 1, rows] = peak + jnp.log(total)
            values = joint_ref[:reach, key_at + head_dim : key_at + 2 * head_dim].astype(low)
            attended = product_tn(values, probs).T
            attended_ref[rows, columns] = attended
            gate = joint_ref[rows, gates]
            mixed_ref[rows, columns] = (attended * jax.nn.sigmoid(gate)).astype(low)


def attend_back_kernel(
    heads, tile, joint_ref, cos_ref, sin_ref, first_ref, gain_query_ref, gain_key_ref,
    attended_ref, query_ref, key_ref, logsum_ref, grad_mixed_ref,
    grad_joint_ref, grad_gain_ref, grad_key_acc, grad_value_acc,
):
    count, head_dim = cos_ref.shape
    scale = head_dim ** (-0.5)
    low = jnp.bfloat16
    key_at = 2 * heads * head_dim
    value_at = key_at + head_dim
    tiles = count // tile
    gain_query = jnp.zeros((1, head_dim), jnp.float32)
    gain_key = jnp.zeros((1, head_dim), jnp.float32)
    for head in range(heads):
        columns = slice(head * head_dim, (head + 1) * head_dim)
        gates = slice((heads + head) * head_dim, (heads + head + 1) * head_dim)
        for part in reversed(range(tiles)):
            rows = pl.ds(part * tile, tile)
            reach = (part + 1) * tile
            fresh = head == 0 and part == tiles - 1
            gate = jax.nn.sigmoid(joint_ref[rows, gates])
            grad_mixed = grad_mixed_ref[rows, columns]
            gated = grad_mixed * gate
            grad_attended = gated.astype(low)
            grad_joint_ref[rows, gates] = (gated * attended_ref[rows, columns] * (1.0 - gate)).astype(
                low
            )
            query = query_ref[rows, columns]
            keys = key_ref[:reach, :]
            values = joint_ref[:reach, value_at : value_at + head_dim].astype(low)
            scores = product_nt(keys, query) * scale
            logsum = logsum_ref[0, head : head + 1, rows]
            probs = jnp.where(
                allowed_tile(first_ref, part * tile, tile, reach), jnp.exp(scores - logsum), 0.0
            )
            grad_value = product_nn(probs.astype(low), grad_attended)
            grad_probs = product_nt(values, grad_attended)
            delta = jnp.sum(probs * grad_probs, axis=0, keepdims=True)
            grad_scores = (probs * (grad_probs - delta)).astype(low)
            grad_key = product_nn(grad_scores, query)
            if fresh:
                grad_value_acc[...] = grad_value
                grad_key_acc[...] = grad_key
            else:
                grad_value_acc[:reach, :] += grad_value
                grad_key_acc[:reach, :] += grad_key
            grad_query = product_tn(keys, grad_scores).T * scale
            grad_raw, gain_part = prepare_back(
                joint_ref[rows, columns],
                gain_query_ref[...],
                cos_ref[rows, :],
                sin_ref[rows, :],
                grad_query,
            )
            grad_joint_ref[rows, columns] = grad_raw
            gain_query = gain_query + gain_part
    for part in range(tiles):
        rows = pl.ds(part * tile, tile)
        grad_raw, gain_part = prepare_back(
            joint_ref[rows, key_at:value_at],
            gain_key_ref[...],
            cos_ref[rows, :],
            sin_ref[rows, :],
            grad_key_acc[rows, :] * scale,
        )
        grad_joint_ref[rows, key_at:value_at] = grad_raw
        gain_key = gain_key + gain_part
        grad_joint_ref[rows, value_at : value_at + head_dim] = grad_value_acc[rows, :].astype(low)
    both = jnp.concatenate([gain_query, gain_key], axis=0)

    @pl.when(pl.program_id(0) == 0)
    def begin():
        grad_gain_ref[...] = both

    @pl.when(pl.program_id(0) > 0)
    def add():
        grad_gain_ref[...] += both


def attend_specs(count, head_dim, heads, joint_width):
    wide = lambda width: pl.BlockSpec((count, width), lambda s: (s, 0))
    row = pl.BlockSpec((1, head_dim), lambda s: (0, 0))
    lead = [
        wide(joint_width),
        wide(head_dim),
        wide(head_dim),
        pl.BlockSpec((1, 1, count), lambda s: (s, 0, 0)),
        row,
        row,
    ]
    kept = [
        wide(heads * head_dim),
        wide(heads * head_dim),
        wide(head_dim),
        pl.BlockSpec((1, heads, count), lambda s: (s, 0, 0)),
    ]
    return (lead, kept, wide)


def attend_fwd(joint, cosine, sine, first, gain_query, gain_key, heads, count):
    head_dim = cosine.shape[1]
    lead, kept, wide = attend_specs(count, head_dim, heads, joint.shape[1])
    total = joint.shape[0]
    shape = jax.ShapeDtypeStruct
    return pl.pallas_call(
        partial(attend_kernel, heads, 256),
        grid=(total // count,),
        in_specs=lead,
        out_specs=[wide(heads * head_dim)] + kept,
        out_shape=[
            shape((total, heads * head_dim), jnp.bfloat16),
            shape((total, heads * head_dim), jnp.float32),
            shape((total, heads * head_dim), jnp.bfloat16),
            shape((total, head_dim), jnp.bfloat16),
            shape((total // count, heads, count), jnp.float32),
        ],
        compiler_params=pltpu.CompilerParams(vmem_limit_bytes=40 * 1024 * 1024),
        cost_estimate=light,
    )(joint, cosine, sine, first, gain_query.reshape(1, -1), gain_key.reshape(1, -1))


def attend_bwd(joint, cosine, sine, first, gain_query, gain_key, kept_values, grad_mixed, count):
    head_dim = cosine.shape[1]
    heads = grad_mixed.shape[1] // head_dim
    lead, kept, wide = attend_specs(count, head_dim, heads, joint.shape[1])
    total = joint.shape[0]
    shape = jax.ShapeDtypeStruct
    return pl.pallas_call(
        partial(attend_back_kernel, heads, 256),
        grid=(total // count,),
        in_specs=lead + kept + [wide(heads * head_dim)],
        out_specs=[wide(joint.shape[1]), pl.BlockSpec((2, head_dim), lambda s: (0, 0))],
        out_shape=[shape(joint.shape, jnp.bfloat16), shape((2, head_dim), jnp.float32)],
        scratch_shapes=[
            pltpu.VMEM((count, head_dim), jnp.float32),
            pltpu.VMEM((count, head_dim), jnp.float32),
        ],
        compiler_params=pltpu.CompilerParams(vmem_limit_bytes=48 * 1024 * 1024),
        cost_estimate=light,
    )(
        joint, cosine, sine, first, gain_query.reshape(1, -1), gain_key.reshape(1, -1),
        *kept_values, grad_mixed,
    )


def fast_body(
    tokens,
    cotangent,
    segment_ids,
    gain_attn,
    gain_ffn,
    gain_query,
    gain_key,
    w_query,
    w_gate,
    w_key,
    w_value,
    w_out,
    w_ffgate,
    w_up,
    w_down,
):
    across = lax.axis_index("x")
    place = lax.axis_index("y") * 2 + lax.axis_index("core")
    count, local = tokens.shape
    width = gain_attn.shape[0]
    head_dim = gain_query.shape[0]
    low = jnp.bfloat16
    query_width = w_query.shape[1] // 2
    key_width = w_key.shape[1] // 2
    heads = query_width // head_dim
    hidden_width = w_ffgate.shape[1] // 2
    live = (segment_ids > 0).astype(jnp.float32)[:, None]
    offset = place * local
    gain_attn_own = lax.dynamic_slice_in_dim(gain_attn, offset, local, 0)
    gain_ffn_own = lax.dynamic_slice_in_dim(gain_ffn, offset, local, 0)

    line = Line()
    half = count // 2
    joint_width = 2 * query_width + 2 * key_width
    rows_of = partial(weight_rows, across=across)

    first_columns = [w_query, w_gate, w_key, w_value, w_out]

    def open_first(tokens, *weights):
        upper_y = flip(tokens[:half], "y")
        keep, give = halves(weights, across)
        got = flip(give, "x")
        return (rows_of(keep, got), upper_y)

    first_rows, upper_y = line.run(open_first, tokens, *first_columns)
    first_weight = weight_gather(first_rows)
    grad_out = live * cotangent.astype(jnp.float32)
    grad_out_low = grad_out.astype(low)

    def open_second(tokens, segment_ids, upper_y, w_ffgate, w_up, w_down):
        lower_y = flip(tokens[half:], "y")
        via_x = flip(tokens, "x")
        own_core = flip(tokens, "core")
        other = flip(segment_ids, "x")
        via_y = jnp.concatenate([upper_y, lower_y], axis=0)
        return (via_y, via_x, own_core, other, *halves([w_ffgate, w_up], across), *halves([w_down], across))

    via_y, via_x, own_core, segment_other, keep_pair, give_pair, keep_down, give_down = line.run(
        open_second, tokens, segment_ids, upper_y, w_ffgate, w_up, w_down
    )

    def open_third(tokens, via_y, via_x, own_core, keep_down, give_down):
        steps = relay(tokens, via_y, via_x, own_core, place, gain_attn, True)
        return (rows_of(keep_down, flip(give_down, "x")), *steps)

    down_rows, *steps, target, inverse1 = line.run(
        open_third, tokens, via_y, via_x, own_core, keep_down, give_down
    )
    down_weight = weight_gather(down_rows)

    def open_fourth(grad_out_low, segment_ids, segment_other, *steps):
        via_out = direct(grad_out_low)
        hidden1 = diagonal(*steps, place, gain_attn, True)
        segments = jnp.stack([segment_ids, segment_other])
        cosine, sine, first = jax.vmap(partial(row_tables, head_dim=head_dim))(segments)
        cosine = cosine.reshape(2 * count, head_dim)
        sine = sine.reshape(2 * count, head_dim)
        return (hidden1, cosine, sine, first, *via_out)

    hidden1, cosine, sine, first, *via_out = line.run(
        open_fourth, grad_out_low, segment_ids, segment_other, *steps, target
    )
    out_column = joint_width // query_width

    def attend(hidden1, first_weight, keep_pair, give_pair, via_y, via_x):
        steps = relay_flips(via_y, via_x)
        got_pair = flip(give_pair, "x")
        joint = dot_in(hidden1, first_weight, joint_width)
        mixed, *kept = attend_fwd(
            joint, cosine, sine, first, gain_query, gain_key, heads, count
        )
        return (rows_of(keep_pair, got_pair), joint, mixed, *kept, *steps)

    out_y, out_x, out_core = via_out
    pair_rows, joint, mixed, *rest = line.run(
        attend, hidden1, first_weight, keep_pair, give_pair, out_y, out_x
    )
    kept, steps = rest[:4], rest[4:]
    pair_weight = weight_gather(pair_rows)
    near_got, far_got = line.run(
        lambda m, w: fold_swap(m, w, place, out_column), mixed, first_weight
    )
    sums = line.run(
        lambda *v: fold_held(v[0], v[1], place, *v[2:], out_column),
        mixed, first_weight, near_got, far_got,
    )

    def cross_out(grad_out_low, own_core, via_y, y_core, via_x, x_core, upper, lower, *sums):
        crossing = fold_cross(*sums)
        near = (grad_out_low, own_core, via_y, y_core)
        target = pack(near, place, gain_ffn, False, 0, None)[0]
        return (
            *crossing,
            diagonal(via_x, x_core, upper, lower, target, place, gain_ffn, False),
        )

    *sums, grad_out_full = line.run(cross_out, grad_out_low, out_core, out_y, *steps, *sums)
    ends = line.run(fold_close, *sums)

    def residual(values, *ends):
        total = values.astype(jnp.float32) + fold_end(*ends)
        return (total, total.astype(low))

    resid, resid_low = line.run(residual, tokens, *ends)

    def start_resid(resid_low, grad_out_full, down_weight):
        return (*direct(resid_low), dot_in(grad_out_full, down_weight, hidden_width))

    *via_resid, grad_act = line.run(start_resid, resid_low, grad_out_full, down_weight)
    *steps, target, inverse2 = line.run(
        lambda *v: relay(*v, place, gain_ffn, True), resid_low, *via_resid
    )
    hidden2 = line.run(lambda *v: diagonal(*v, place, gain_ffn, True), *steps, target)
    activated, grad_pair = line.run(ffn, hidden2, pair_weight, grad_act)


    def sent_pair(hidden2, grad_pair, pair_weight):
        return (
            *fold_swap(grad_pair, pair_weight, place),
            dot_grad(hidden2, grad_pair, hidden_width),
        )

    near_got, far_got, gate_grad = line.run(sent_pair, hidden2, grad_pair, pair_weight)
    gate_sum = grad_scatter(gate_grad)
    sums = line.run(
        lambda *v: fold_held(v[0], v[1], place, *v[2:]), grad_pair, pair_weight, near_got, far_got
    )

    def cross_pair(hidden2, grad_pair, activated, down_weight, *sums):
        return (
            *fold_cross(*sums),
            dot_grad(hidden2, grad_pair, hidden_width, 1),
            *fold_sent(activated, down_weight, place),
        )

    *sums, up_grad, near_ffn, far_ffn = line.run(
        cross_pair, hidden2, grad_pair, activated, down_weight, *sums
    )
    up_sum = grad_scatter(up_grad)

    def close_pair(near_ffn, far_ffn, *sums):
        return (*fold_close(*sums), flip(near_ffn, "core"), flip(far_ffn, "core"))

    *ends, near_got, far_got = line.run(close_pair, near_ffn, far_ffn, *sums)

    def partial_dots(grad_own, values, inverse, gain_own):
        dots = jnp.sum(grad_own * gain_own * values.astype(jnp.float32) * inverse, axis=1)
        dots = dots.reshape(-1, 128)
        dots = dots + flip(dots, "core")
        return dots + flip(dots, "y")

    def norm_back(grad_own, values, inverse, gain_own, dots, extra):
        unit = values.astype(jnp.float32) * inverse
        dots = dots.reshape(-1, 1) / width
        grad_input = inverse * (grad_own * gain_own - unit * dots) + extra
        return (grad_input, grad_input.astype(low))

    def gain_part(grad_own, values, inverse):
        return jnp.sum(grad_own * (values.astype(jnp.float32) * inverse), axis=0).reshape(-1, 128)

    def back_dots(values, inverse, gain_own, *ends):
        grad_own = fold_end(*ends)
        return (
            grad_own,
            partial_dots(grad_own, values, inverse, gain_own),
            gain_part(grad_own, values, inverse),
        )

    grad_hidden2, dots, gain_ffn_grad = line.run(
        back_dots, resid_low, inverse2, gain_ffn_own, *ends
    )
    grad_resid, grad_branch = line.run(
        norm_back, grad_hidden2, resid_low, inverse2, gain_ffn_own, dots, grad_out
    )

    def start_branch(grad_branch, grad_out_full, activated, down_weight, near_got, far_got):
        return (
            *direct(grad_branch),
            dot_grad(grad_out_full, activated),
            *fold_held(activated, down_weight, place, near_got, far_got),
        )

    via_y, via_x, own_core, down_grad, *sums_ffn = line.run(
        start_branch, grad_branch, grad_out_full, activated, down_weight, near_got, far_got
    )
    down_sum = grad_scatter(down_grad)
    gate_sum, = line.enter(gate_sum)
    steps = line.run(
        lambda *v: relay(*v, place, gain_ffn, False), grad_branch, via_y, via_x, own_core
    )

    def mix_back(gate_sum, first_weight, *steps):
        got_gate = flip(give_rows(gate_sum, across), "x")
        grad_branch_full = diagonal(*steps, place, gain_ffn, False)
        return (
            got_gate,
            grad_branch_full,
            dot_in(grad_branch_full, first_weight, query_width, out_column),
        )

    got_gate, grad_branch_full, grad_mixed = line.run(mix_back, gate_sum, first_weight, *steps)
    up_sum, = line.enter(up_sum)

    def attend_back(joint, grad_mixed, grad_branch_full, mixed, *sums):
        grad_joint, head_gains = attend_bwd(
            joint, cosine, sine, first, gain_query, gain_key, kept, grad_mixed, count
        )
        last_grads = dot_grad_part(
            grad_branch_full, mixed, joint_width + query_width, out_column
        )
        return (grad_joint, head_gains, last_grads, *fold_cross(*sums))

    grad_joint, head_gains, last_grads, *sums_ffn = line.run(
        attend_back, joint, grad_mixed, grad_branch_full, mixed, *sums_ffn
    )

    def sent_attn(hidden1, grad_joint, first_weight, last_grads, up_sum):
        return (
            *fold_swap(grad_joint, first_weight, place),
            dot_grad_part(hidden1, grad_joint, last_grads.shape[1], 0, last_grads),
            flip(give_rows(up_sum, across), "x"),
        )

    near_got, far_got, last_grads, got_up = line.run(
        sent_attn, hidden1, grad_joint, first_weight, last_grads, up_sum
    )
    attn_sum = grad_scatter(last_grads)
    down_sum, = line.enter(down_sum)

    def held_attn(grad_joint, first_weight, near_got, far_got, gain_ffn_grad, head_gains, *sums):
        early = jnp.concatenate([gain_ffn_grad, head_gains], axis=0)
        early = early + flip(early, "x")
        return (
            early,
            *fold_held(grad_joint, first_weight, place, near_got, far_got),
            *fold_close(*sums),
        )

    early, *sums = line.run(
        held_attn, grad_joint, first_weight, near_got, far_got, gain_ffn_grad, head_gains, *sums_ffn
    )
    sums, ends_ffn = sums[:4], sums[4:]

    def join(rows, got, low_cut, high_cut):
        keep = keep_rows(rows, across)[:, low_cut:high_cut]
        got = got[:, low_cut:high_cut]
        first, second = jnp.where(across == 0, keep, got), jnp.where(across == 0, got, keep)
        return jnp.concatenate([first, second], axis=1).astype(jnp.float32)

    def join_all(rows, got):
        return join(rows, got, 0, rows.shape[1])

    def cross_attn(early, resid, gate_sum, got_gate, *values):
        sums = fold_cross(*values[:4])
        output = (live * (resid + fold_end(*values[4:]))).astype(low)
        return (
            early + z_flip(early, 1),
            output,
            join_all(gate_sum, got_gate),
            *sums,
        )

    early, output, ffgate_grad, *sums = line.run(
        cross_attn, early, resid, gate_sum, got_gate, *sums, *ends_ffn
    )

    def close_attn(early, up_sum, got_up, *sums):
        return (early + z_flip(early, 2), join_all(up_sum, got_up), *fold_close(*sums))

    early, up_grad, *ends = line.run(close_attn, early, up_sum, got_up, *sums)

    def last_dots(tokens, inverse1, down_sum, *ends):
        got_down = flip(give_rows(down_sum, across), "x")
        grad_own = fold_end(*ends)
        late = gain_part(grad_own, tokens, inverse1)
        late = late + z_flip(late, 1)
        return (
            got_down,
            grad_own,
            partial_dots(grad_own, tokens, inverse1, gain_attn_own),
            late + z_flip(late, 2),
        )

    got_down, grad_hidden1, dots, late = line.run(last_dots, tokens, inverse1, down_sum, *ends)
    cuts = (
        0,
        query_width,
        2 * query_width,
        2 * query_width + key_width,
        2 * query_width + 2 * key_width,
    )

    blocks = local // 128

    def last_spot(late, early):
        own = jnp.stack([late, early[:blocks]])
        spot = lax.dynamic_update_slice_in_dim(
            jnp.zeros((2, width // 128, 128), jnp.float32), own, offset // 128, 1
        ).reshape(-1, 128)
        spot = jnp.concatenate([spot, early[blocks:]], axis=0)
        spot = spot + flip(spot, "core")
        return spot + flip(spot, "y")

    def last_norm(
        grad_hidden1, tokens, inverse1, dots, grad_resid, late, early, attn_sum, down_sum, got_down
    ):
        got_attn = flip(give_rows(attn_sum, across), "x")
        spot = last_spot(late + flip(late, "x"), early)
        grad_tokens, unused = norm_back(
            grad_hidden1, tokens, inverse1, gain_attn_own, dots, grad_resid
        )
        return (got_attn, spot, grad_tokens, *join_parts(down_sum, got_down, across, (hidden_width,)))

    got_attn, spot, grad_tokens, down_part = line.run(
        last_norm, grad_hidden1, tokens, inverse1, dots, grad_resid, late, early, attn_sum,
        down_sum, got_down
    )
    widths = (query_width, query_width, key_width, key_width, query_width)
    *attn_parts, out_part = line.run(
        lambda sums, got: join_parts(sums, got, across, widths), attn_sum, got_attn
    )
    lines = width // 128
    return (
        output,
        grad_tokens,
        spot[:lines].reshape(width),
        spot[lines : 2 * lines].reshape(width),
        spot[2 * lines] + line.token[0],
        spot[2 * lines + 1],
        *attn_parts,
        out_part,
        ffgate_grad,
        up_grad,
        down_part,
    )


def solution(mesh):
    rows, columns = mesh.devices.shape

    def run(*args):
        head_dim = args[5].shape[0]
        query_width, key_width = args[7].shape[1], args[9].shape[1]
        one_key_head = key_width == 2 * columns * head_dim and query_width % key_width == 0
        if not (rows == 8 and columns == 4 and one_key_head):
            return plain(mesh)(*args)
        names = ("z", "x", "y", "core")
        inner = Mesh(mesh.devices.reshape(4, 2, 2, 2), names)
        block = P(("z", "x"), ("y", "core"))
        whole = P()
        in_specs = (block, block, P(("z", "x"))) + (whole,) * 4 + (block,) * 8
        out_specs = (block, block) + (whole,) * 4 + (block,) * 8
        return jax.shard_map(
            fast_body, mesh=inner, in_specs=in_specs, out_specs=out_specs, check_vma=False
        )(*args)

    return run
```
